32 devices in a mesh: srv: 2 (over y), head: 4 (over x, core), wsh: 4 (over z).
Axes of the slice: x: 2, y: 2, z: 4, core: 2. Of those that a mesh axis runs over, the one named last changes fastest.
Arguments:
- queries: bfloat16 [1536, 8192], P(('srv', 'wsh'), 'head'), may hold values from -4.5 to 4.5
- keys: bfloat16 [1536, 1024], P(('srv', 'wsh'), 'head'), may hold values from -4.5 to 4.5
- values: bfloat16 [1536, 1024], P(('srv', 'wsh'), 'head'), may hold values from -6 to 6
- doc_ids: int32 [1536], replicated, may hold values from 0 to 2, never falling along the last dimension, each value on 1 to 1152 neighbouring positions
- block_mask: int32 [8, 4], replicated, may hold values from 0 to 1, as said below
- out_weight: bfloat16 [8192, 8192], P(('head', 'wsh')), may hold values from -0.0625 to 0.0625
Outputs:
- projected: bfloat16 [1536, 8192], P(('srv', 'head', 'wsh'))
The draws below stay inside these ranges and needn't reach their ends.
Inputs may be any that keep to these rules, and one draw needn't show every extreme that they name: `block_mask`: column 0 is 1 in every row; other entries are 0 or 1.
All inputs are finite; a program needn't handle non-finite values.
Results may differ from the reference program's by a relative error of at most 0.017.
Values may be sent and summed in bfloat16 or wider, within the bound.
No kernel may reach another device: no remote copies, remote signals or barrier semaphores. Data moves between devices by JAX's collectives and lax.ppermute only.
A program may use at most 128 MiB of HBM per device.

```python
import math
import jax
import jax.numpy as jnp
import numpy as np
from jax import lax

QUERY_HEAD_COUNT = 64
KEY_VALUE_HEADS = 8
HEAD_SIZE = 128
D = 8192
SLAB_TOKENS = 192
SLAB_REACH = 4
SLAB_COUNT = 8
PACKED_TOKENS = 1536
ROWS_DEV = 512


def shared_keys(key):
    base = jax.random.fold_in(key, 7211)
    first = jax.random.fold_in(base, 0)
    window_width = KEY_VALUE_HEADS * HEAD_SIZE
    drawn = jnp.clip(jax.random.normal(first, (PACKED_TOKENS, window_width), jnp.float32), -4.5, 4.5)
    return drawn


def draw_keys(key, part):
    drawn = shared_keys(key)
    return drawn.astype(jnp.bfloat16)


def draw_queries(key, part):
    own_key = jax.random.fold_in(key, 5309)
    query_draw = jnp.clip(jax.random.normal(own_key, (PACKED_TOKENS, QUERY_HEAD_COUNT * HEAD_SIZE), jnp.float32), -4.5, 4.5)
    return query_draw.astype(jnp.bfloat16)


def draw_block_mask(key, part):
    levels = jax.random.randint(jax.random.fold_in(key, 31), (SLAB_COUNT, SLAB_REACH), 0, 4)
    opened = jnp.where(levels > 0, 1, 0).astype(jnp.int32)
    return opened.at[:, 0].set(1)


def steps_of(key, dims, pieces, least, top_value):
    gain, own = 1.0, jax.random.fold_in(key, 6)
    for position, parts in pieces:
        draws = jnp.exp(jax.random.uniform(jax.random.fold_in(own, position), (parts,), jnp.float32, least / len(pieces), top_value / len(pieces)))
        gain = gain * jnp.repeat(draws, dims[position] // parts).reshape([-1 if axis == position else 1 for axis in range(len(dims))])
    return gain


def split_up(number_of, total, reach, slope):
    weights = [(1 << 20) // math.isqrt(rank ** slope) + 1 for rank in range(2, number_of + 1)]
    spare, holding = total - reach - (number_of - 1), [1] * (number_of - 1)
    while spare > 0:
        free = [i for i in range(number_of - 1) if holding[i] < reach]
        pool, remaining = sum([weights[i] for i in free]), spare
        for i in free:
            more = min(reach - holding[i], max(1, remaining * weights[i] // pool), spare)
            holding[i] = holding[i] + more
            spare = spare - more
    return np.array([reach] + holding)


def uneven_parts(key, number_of, total, most, slope):
    if number_of == 2:
        one = jax.random.randint(key, (), max(1, total - most), min(most, total - 1) + 1)
        return jnp.stack([one, total - one])
    tallies = jnp.asarray(split_up(number_of, total, most, slope), jnp.int32)
    pairs = (number_of - 1) // 2
    giver, receiver = tallies[1:1 + 2 * pairs:2], tallies[2:2 + 2 * pairs:2]
    margin = jnp.minimum(giver - 1, most - receiver)
    moved = jax.random.randint(jax.random.fold_in(key, 1), (pairs,), 0, 1 << 20) % (margin + 1)
    tallies = tallies.at[1:1 + 2 * pairs:2].set(giver - moved).at[2:2 + 2 * pairs:2].set(receiver + moved)
    return tallies[jax.random.permutation(jax.random.fold_in(key, 2), number_of)]


def noise(key, shape, width, limit, cuts=(), kind=jnp.bfloat16):
    drawn = width * jax.random.normal(key, shape, jnp.float32)
    if cuts:
        drawn = drawn * steps_of(key, shape, cuts, -0.22, 0.18)
    return jnp.clip(drawn, -limit, limit).astype(kind)


def setup_inputs(seed: int = 0) -> dict:
    arg_keys = jax.random.split(jax.random.key(seed), 7)
    queries = draw_queries(jax.random.fold_in(arg_keys[6], 71), 0)
    keys = draw_keys(jax.random.fold_in(arg_keys[6], 71), 0)
    values = noise(arg_keys[2], (PACKED_TOKENS, KEY_VALUE_HEADS * HEAD_SIZE), 1.0, 6.0, ((0, 8), (1, 4)))
    doc_ids = jnp.searchsorted(jnp.cumsum(uneven_parts(arg_keys[3], 3, PACKED_TOKENS, PACKED_TOKENS - 2 * SLAB_TOKENS, 2)), jnp.arange(PACKED_TOKENS), side="right").astype(jnp.int32)
    block_mask = draw_block_mask(jax.random.fold_in(arg_keys[6], 71), 0)
    out_weight = noise(arg_keys[5], (QUERY_HEAD_COUNT * HEAD_SIZE, D), (QUERY_HEAD_COUNT * HEAD_SIZE) ** -0.5, 0.0625, ((0, 16),))
    return {"queries": queries, "keys": keys, "values": values, "doc_ids": doc_ids, "block_mask": block_mask, "out_weight": out_weight}


def reference(queries, keys, values, doc_ids, block_mask, out_weight):
    query_group_width = QUERY_HEAD_COUNT // KEY_VALUE_HEADS
    score_scale = 1.0 / math.sqrt(HEAD_SIZE)
    query_slab_array = queries.reshape(SLAB_COUNT, SLAB_TOKENS, KEY_VALUE_HEADS, query_group_width, HEAD_SIZE)
    key_slab_array = keys.reshape(SLAB_COUNT, SLAB_TOKENS, KEY_VALUE_HEADS, HEAD_SIZE)
    value_slab_array = values.reshape(SLAB_COUNT, SLAB_TOKENS, KEY_VALUE_HEADS, HEAD_SIZE)
    doc_slabs = doc_ids.reshape(SLAB_COUNT, SLAB_TOKENS)
    padded_keys = jnp.concatenate([jnp.zeros((SLAB_REACH - 1, SLAB_TOKENS, KEY_VALUE_HEADS, HEAD_SIZE), jnp.bfloat16), key_slab_array], axis=0)
    padded_values = jnp.concatenate([jnp.zeros((SLAB_REACH - 1, SLAB_TOKENS, KEY_VALUE_HEADS, HEAD_SIZE), jnp.bfloat16), value_slab_array], axis=0)
    doc_padded = jnp.concatenate([jnp.full((SLAB_REACH - 1, SLAB_TOKENS), -1, jnp.int32), doc_slabs.astype(jnp.int32)], axis=0)

    def one_slab(current_slab):
        query_heads = lax.dynamic_index_in_dim(query_slab_array, current_slab, 0, keepdims=False)
        docs_query = lax.dynamic_index_in_dim(doc_slabs, current_slab, 0, keepdims=False)
        window_keys = lax.dynamic_slice_in_dim(padded_keys, current_slab, SLAB_REACH, 0).reshape(SLAB_REACH * SLAB_TOKENS, KEY_VALUE_HEADS, HEAD_SIZE)
        window_values = lax.dynamic_slice_in_dim(padded_values, current_slab, SLAB_REACH, 0).reshape(SLAB_REACH * SLAB_TOKENS, KEY_VALUE_HEADS, HEAD_SIZE)
        docs_key = lax.dynamic_slice_in_dim(doc_padded, current_slab, SLAB_REACH, 0).reshape(SLAB_REACH * SLAB_TOKENS)
        mask_row = lax.dynamic_index_in_dim(block_mask, current_slab, 0, keepdims=False)
        allowed = jnp.repeat(jnp.flip(mask_row) > 0, SLAB_TOKENS)
        query_pos = current_slab * SLAB_TOKENS + jnp.arange(SLAB_TOKENS, dtype=jnp.int32)
        key_pos = (current_slab - (SLAB_REACH - 1)) * SLAB_TOKENS + jnp.arange(SLAB_REACH * SLAB_TOKENS, dtype=jnp.int32)
        visible = (docs_query[:, None] == docs_key[None, :]) & (key_pos[None, :] <= query_pos[:, None])
        visible = visible & (key_pos >= 0)[None, :] & allowed[None, :]
        scores = jnp.einsum('qhgd,khd->hgqk', query_heads.astype(jnp.float32), window_keys.astype(jnp.float32)) * score_scale
        masked = jnp.where(visible, scores, -1e+30)
        largest = lax.optimization_barrier(jnp.max(masked, axis=-1, keepdims=True))
        softmax_terms = jnp.where(visible, jnp.exp(masked - largest), 0.0)
        normalizer = lax.optimization_barrier(jnp.sum(softmax_terms, axis=-1))
        rounded_terms = softmax_terms.astype(jnp.bfloat16)
        weighted = jnp.einsum('hgqk,khd->qhgd', rounded_terms.astype(jnp.float32), window_values.astype(jnp.float32))
        result = weighted / jnp.transpose(normalizer, (2, 0, 1))[..., None]
        return result.reshape(SLAB_TOKENS, QUERY_HEAD_COUNT * HEAD_SIZE).astype(jnp.bfloat16)
    attention = lax.map(one_slab, jnp.arange(SLAB_COUNT, dtype=jnp.int32)).reshape(PACKED_TOKENS, QUERY_HEAD_COUNT * HEAD_SIZE)
    block_count = QUERY_HEAD_COUNT * HEAD_SIZE // ROWS_DEV

    def add_block(block_index, running):
        lower = (block_index * ROWS_DEV).astype(jnp.int32)
        rows_attention = lax.dynamic_slice_in_dim(attention, lower, ROWS_DEV, 1)
        rows_weight = lax.dynamic_slice_in_dim(out_weight, lower, ROWS_DEV, 0)
        block_term = jnp.dot(rows_attention, rows_weight, preferred_element_type=jnp.float32).astype(jnp.bfloat16)
        block_term = lax.optimization_barrier(block_term)
        return running + block_term.astype(jnp.float32)
    summed = lax.fori_loop(0, block_count, add_block, jnp.zeros((PACKED_TOKENS, D), jnp.float32))
    return summed.astype(jnp.bfloat16)
```

```python
from functools import partial
import math

import jax
import jax.numpy as jnp
import numpy as np
from jax import lax
from jax.experimental import pallas as pl
from jax.experimental.pallas import tpu as pltpu
from jax.sharding import PartitionSpec as P

QUERY_HEAD_COUNT = 64
KEY_VALUE_HEADS = 8
HEAD_SIZE = 128
SLAB_REACH = 4

MASKED = -1e30
NEVER = 1 << 30
F32 = jnp.float32
BF16 = jnp.bfloat16


def destination_order(count):
    table = []
    for z in range(count):
        due = {d: (count - 1 - d + z if d > z else count - 1 - z + d) for d in range(count)}
        due[z] = count
        table.append(sorted(range(count), key=lambda d: (due[d], -d if z < count // 2 else d)))
    return np.array(table, np.int32)


def attend_kernel(place, kv_now, kv_before, key_doc, key_pos, query_doc, query_pos, *refs, slabs, heads, spread):
    queries, (keep, send, key_rows, value_rows) = refs[:slabs], refs[slabs:]
    scale = math.log2(math.e) / math.sqrt(HEAD_SIZE)
    block = kv_now.shape[1]
    for k in range(slabs):
        slab = place[k, 0]
        for o in range(SLAB_REACH):
            rows = slice((SLAB_REACH - 1 - o) * block, (SLAB_REACH - o) * block)
            held = (k + o) % slabs

            def fill(source):
                key_rows[rows, :] = source[held, :, :HEAD_SIZE]
                value_rows[rows, :] = source[held, :, HEAD_SIZE:]

            if o == 0:
                fill(kv_now)
            else:
                pl.when(slab >= o)(partial(fill, kv_now))
                pl.when(slab < o)(partial(fill, kv_before))
        visible = (query_doc[k] == key_doc[k]) & (key_pos[k] <= query_pos[k])
        columns = []
        for h in range(heads):
            scores = lax.dot_general(
                queries[k][:, h * HEAD_SIZE : (h + 1) * HEAD_SIZE],
                key_rows[...],
                (((1,), (1,)), ((), ())),
                preferred_element_type=F32,
            )
            scores = jnp.where(visible, scores, MASKED)
            largest = jnp.max(scores, axis=-1, keepdims=True)
            terms = jnp.exp2((scores - largest) * scale)
            normalizer = jnp.sum(terms, axis=-1, keepdims=True)
            weighted = jnp.dot(terms.astype(BF16), value_rows[...], preferred_element_type=F32)
            columns.append((weighted / normalizer).astype(BF16))
        result = jnp.concatenate(columns, axis=1)
        slot = place[k, 2]

        @pl.when(place[k, 1] == 1)
        def _():
            keep[slot] = result

        @pl.when(place[k, 1] == 0)
        def _():
            send[slot] = result


def attend(place, kv_now, kv_before, key_info, query_info, queries):
    slabs, block, _ = kv_now.shape
    rows, width = queries[0].shape
    out = jax.ShapeDtypeStruct((slabs // 2, rows, width), BF16)
    vmem = pl.BlockSpec(memory_space=pltpu.VMEM)
    terms = slabs * rows * SLAB_REACH * block * (width // HEAD_SIZE)
    return pl.pallas_call(
        partial(attend_kernel, slabs=slabs, heads=width // HEAD_SIZE, spread=None),
        out_shape=(out, out),
        in_specs=[pl.BlockSpec(memory_space=pltpu.SMEM)] + [vmem] * (6 + slabs),
        out_specs=(vmem, vmem),
        scratch_shapes=[pltpu.VMEM((SLAB_REACH * block, HEAD_SIZE), BF16)] * 2,
        compiler_params=pltpu.CompilerParams(vmem_limit_bytes=40 << 20),
        cost_estimate=pl.CostEstimate(
            flops=4 * terms * HEAD_SIZE, bytes_accessed=4 * slabs * rows * width * 2, transcendentals=terms
        ),
    )(place, kv_now, kv_before, *key_info, *query_info, *queries)


def project_kernel(mine, theirs, weight_mine, weight_theirs, *outs, rows):
    total = jnp.dot(mine[...], weight_mine[...], preferred_element_type=F32)
    total = total + jnp.dot(theirs[...], weight_theirs[...], preferred_element_type=F32)
    for n, out in enumerate(outs):
        out[...] = total[n * rows : (n + 1) * rows].astype(BF16)


def project(mine, theirs, weight_mine, weight_theirs, rows):
    count, depth = mine.shape
    width = weight_mine.shape[1]
    tile = 1024 if width % 1024 == 0 else width
    whole = pl.BlockSpec((count, depth), lambda n: (0, 0))
    strip = pl.BlockSpec((depth, tile), lambda n: (0, n))
    pieces = count // rows
    return pl.pallas_call(
        partial(project_kernel, rows=rows),
        grid=(width // tile,),
        out_shape=[jax.ShapeDtypeStruct((rows, width), BF16)] * pieces,
        in_specs=[whole, whole, strip, strip],
        out_specs=[pl.BlockSpec((rows, tile), lambda n: (0, n))] * pieces,
        compiler_params=pltpu.CompilerParams(vmem_limit_bytes=40 << 20),
        cost_estimate=pl.CostEstimate(
            flops=4 * count * depth * width,
            bytes_accessed=4 * depth * width + 2 * count * width,
            transcendentals=0,
        ),
    )(mine, theirs, weight_mine, weight_theirs)


def on_device(queries, keys, values, doc_ids, block_mask, out_weight, *, order):
    groups, head_shards, slabs = (lax.axis_size(a) for a in ("srv", "head", "wsh"))
    srv, head, z = (lax.axis_index(a) for a in ("srv", "head", "wsh"))
    core, x, columns_x = head % 2, head // 2, head_shards // 2
    block = queries.shape[0]
    kv_local = keys.shape[1] // HEAD_SIZE
    width = queries.shape[1] // slabs
    share = block // head_shards
    per_shard = slabs // head_shards
    table = jnp.asarray(order)
    staged = per_shard == 1

    def kv_for(target):
        first = (target * kv_local // slabs) * HEAD_SIZE
        cut = lambda a: lax.dynamic_slice(a, (0, first), (block, HEAD_SIZE))
        return jnp.concatenate([cut(keys), cut(values)], axis=1)

    def around(k):
        return [(i, (i + k) % slabs) for i in range(slabs)]

    def query_rows(target, stage):
        strip = lax.dynamic_slice(queries, (0, target * width), (block, width))
        if not staged:
            return strip
        pieces = [
            lax.dynamic_slice(queries, (table[target, i] * share, target * width), (share, width)) for i in stage
        ]
        return pieces[0] if len(pieces) == 1 else jnp.concatenate(pieces, axis=0)

    stages = [[0], list(range(1, slabs))] if staged else [list(range(slabs))]

    held = [kv_for(z)] + [lax.ppermute(kv_for((z + k) % slabs), "wsh", around(k)) for k in range(1, slabs)]
    kv_now = jnp.stack(held)
    kv_before = lax.ppermute(kv_now, "srv", [(g, g + 1) for g in range(groups - 1)])
    stage_queries = [
        [query_rows(z, stage)]
        + [lax.ppermute(query_rows((z + k) % slabs, stage), "wsh", around(k)) for k in range(1, slabs)]
        for stage in stages
    ]
    siblings = [(h, h ^ 1) for h in range(head_shards)]
    weight_sibling = lax.ppermute(out_weight, "head", siblings)

    slab_of = (z - jnp.arange(slabs, dtype=jnp.int32)) % slabs
    offsets = jnp.arange(SLAB_REACH - 1, -1, -1, dtype=jnp.int32)
    global_slab = srv * slabs + slab_of
    source = global_slab[:, None] - offsets[None, :]
    docs = doc_ids.reshape(-1, block)
    open_pair = jnp.take_along_axis(
        block_mask[global_slab], jnp.broadcast_to(offsets[None, :], source.shape), axis=1
    )
    live = (open_pair > 0) & (source >= 0)
    within = jnp.arange(block, dtype=jnp.int32)
    key_doc = docs[jnp.maximum(source, 0)].reshape(slabs, 1, -1)
    key_pos = jnp.where(live[..., None], source[..., None] * block + within, NEVER).reshape(slabs, 1, -1)
    target = slab_of // per_shard
    place = jnp.stack(
        [slab_of, (target % 2 == core).astype(jnp.int32), ((target // 2 - x) % columns_x) * per_shard + slab_of % per_shard],
        axis=1,
    ).astype(jnp.int32)

    partials = []
    for stage, blocks in zip(stages, stage_queries):
        if staged:
            rows = jnp.concatenate([table[z, i] * share + jnp.arange(share, dtype=jnp.int32) for i in stage])
        else:
            rows = within
        query_doc = docs[global_slab][:, rows][..., None]
        query_pos = (global_slab[:, None] * block + rows[None, :])[..., None]
        keep, send = attend(place, kv_now, kv_before, (key_doc, key_pos), (query_doc, query_pos), blocks)
        if not staged:
            keep, send = (
                jnp.concatenate(
                    [
                        lax.dynamic_slice_in_dim(a.reshape(columns_x, -1, width), table[z, i] * share, share, 1)
                        for i in stage
                    ],
                    axis=1,
                )
                for a in (keep, send)
            )
        theirs = lax.ppermute(send, "head", siblings)
        results = project(
            keep.reshape(-1, width), theirs.reshape(-1, width), out_weight, weight_sibling, share
        )
        count = len(stage)
        for n in range(count):
            partials.append([results[k * count + n] for k in range(columns_x)])

    sums = []
    for own, *others in partials:
        total = own.astype(F32)
        for k, other in enumerate(others, 1):
            route = [(h, (h + 2 * k) % head_shards) for h in range(head_shards)]
            total = total + lax.ppermute(other, "head", route).astype(F32)
        sums.append(total.astype(BF16))

    position = np.argsort(order, axis=1)

    def along(direction):
        arrived = None
        for t in range(slabs - 1):
            which = np.zeros(slabs, np.int32)
            route = []
            for i in range(slabs):
                step = i if direction > 0 else slabs - 1 - i
                if step <= t:
                    d = slabs - 1 - t + step
                    d = d if direction > 0 else slabs - 1 - d
                    which[i] = position[i, d]
                    route.append((i, i + direction))
            message = sums[which[0 if direction > 0 else slabs - 1]]
            for i in range(slabs):
                if any(i == r[0] for r in route) and sums[which[i]] is not message:
                    message = jnp.where(z == i, sums[which[i]], message)
            if arrived is not None:
                message = (message.astype(F32) + arrived.astype(F32)).astype(BF16)
            arrived = lax.ppermute(message, "wsh", route)
        return arrived

    total = sums[-1].astype(F32)
    if slabs > 1:
        total = total + along(1).astype(F32) + along(-1).astype(F32)
    return total.astype(BF16)


def solution(mesh):
    in_specs = (
        P(("srv", "wsh"), "head"),
        P(("srv", "wsh"), "head"),
        P(("srv", "wsh"), "head"),
        P(),
        P(),
        P(("head", "wsh"), None),
    )
    out_specs = P(("srv", "head", "wsh"), None)
    return jax.shard_map(
        partial(on_device, order=destination_order(mesh.shape["wsh"])),
        mesh=mesh,
        in_specs=in_specs,
        out_specs=out_specs,
        check_vma=False,
    )
```

```python
from functools import partial
import math

import jax
import jax.numpy as jnp
import numpy as np
from jax import lax
from jax.experimental import pallas as pl
from jax.experimental.pallas import tpu as pltpu
from jax.sharding import PartitionSpec as P

QUERY_HEAD_COUNT = 64
KEY_VALUE_HEADS = 8
HEAD_SIZE = 128
SLAB_REACH = 4

MASKED = -1e30
F32 = jnp.float32
BF16 = jnp.bfloat16
VMEM = pl.BlockSpec(memory_space=pltpu.VMEM)
SMEM = pl.BlockSpec(memory_space=pltpu.SMEM)
HBM = pl.BlockSpec(memory_space=pl.ANY)
LIMIT = pltpu.CompilerParams(vmem_limit_bytes=28 << 20)
TILE = 1024


def destination_order(count):
    table = []
    for z in range(count):
        due = {d: (count - 1 - d + z if d > z else count - 1 - z + d) for d in range(count)}
        due[z] = count
        table.append(sorted(range(count), key=lambda d: (due[d], -d if z < count // 2 else d)))
    return np.array(table, np.int32)


def in_vmem(array):
    return pltpu.with_memory_space_constraint(array, pltpu.VMEM)


def joined(parts):
    return parts[0] if len(parts) == 1 else jnp.concatenate(parts, axis=0)


def attend_kernel(info, key_doc, doc_col, *refs, slabs, heads, share, pieces, offset, columns_x, per_shard, fetched):
    refs = list(refs)
    take = lambda n: [refs.pop(0) for _ in range(n)]
    now, before, queries, weights = take(slabs), take(slabs), take(slabs), take(fetched)
    (keep, send), copied = take(2), take(fetched)
    key_rows, value_rows = take(2)
    copies = [pltpu.make_async_copy(w, c, refs[0].at[n]) for n, (w, c) in enumerate(zip(weights, copied))]
    for copy in copies:
        copy.start()
    scale = math.log2(math.e) / math.sqrt(HEAD_SIZE)
    block = doc_col.shape[1]
    span = SLAB_REACH * block
    rows = share * pieces
    z, core, x = info[0], info[1], info[2]
    starts = [pl.multiple_of(info[3 + n], 16) for n in range(pieces)]
    column = lax.broadcasted_iota(jnp.int32, (share, span), 1) - (SLAB_REACH - 1) * block
    row = lax.broadcasted_iota(jnp.int32, (share, span), 0)
    causal = joined([column - row <= start for start in starts])
    for k in range(slabs):
        slab = lax.rem(z - k + slabs, slabs)
        for o in range(SLAB_REACH):
            place = slice((SLAB_REACH - 1 - o) * block, (SLAB_REACH - o) * block)
            held = (k + o) % slabs

            def fill(source):
                key_rows[place, :] = source[:block, :]
                value_rows[place, :] = source[block : 2 * block, :]

            if o == 0:
                fill(now[held])
            else:
                pl.when(slab >= o)(partial(fill, now[held]))
                pl.when(slab < o)(partial(fill, before[held]))
        query_doc = joined([doc_col[slab, pl.ds(start, share), :] for start in starts])
        visible = causal & (query_doc == key_doc[slab])
        scores = lax.dot_general(
            queries[k][offset : offset + heads * rows, :],
            key_rows[...],
            (((1,), (1,)), ((), ())),
            preferred_element_type=F32,
        ).reshape(heads, rows, span)
        scores = jnp.where(visible[None], scores, MASKED)
        largest = jnp.max(scores, axis=-1, keepdims=True)
        terms = jnp.exp2((scores - largest) * scale)
        normalizer = jnp.sum(terms, axis=-1, keepdims=True)
        weighted = jnp.dot(
            terms.reshape(heads * rows, span).astype(BF16), value_rows[...], preferred_element_type=F32
        ).reshape(heads, rows, HEAD_SIZE)
        result = (weighted / normalizer).astype(BF16)
        result = jnp.concatenate([result[h] for h in range(heads)], axis=1)
        target = lax.div(slab, per_shard)
        slot = lax.rem(lax.div(target, 2) - x + columns_x, columns_x) * per_shard + lax.rem(slab, per_shard)

        @pl.when(lax.rem(target, 2) == core)
        def _():
            keep[slot] = result

        @pl.when(lax.rem(target, 2) != core)
        def _():
            send[slot] = result

    for copy in copies:
        copy.wait()


def attend(info, docs, now, before, queries, weights, *, heads, share, pieces, offset, columns_x, per_shard):
    slabs, block = docs[1].shape[:2]
    rows = share * pieces
    out = jax.ShapeDtypeStruct((slabs // 2, rows, heads * HEAD_SIZE), BF16)
    terms = slabs * rows * SLAB_REACH * block * heads
    fetched = len(weights)
    return pl.pallas_call(
        partial(
            attend_kernel,
            slabs=slabs,
            heads=heads,
            share=share,
            pieces=pieces,
            offset=offset,
            columns_x=columns_x,
            per_shard=per_shard,
            fetched=fetched,
        ),
        out_shape=[out, out] + [pltpu.VMEM(w.shape, w.dtype) for w in weights],
        in_specs=[SMEM] + [VMEM] * (2 + 3 * slabs) + [HBM] * fetched,
        out_specs=[VMEM] * (2 + fetched),
        scratch_shapes=[pltpu.VMEM((SLAB_REACH * block, HEAD_SIZE), BF16)] * 2
        + [pltpu.SemaphoreType.DMA((fetched,))] * (fetched > 0),
        compiler_params=LIMIT,
        cost_estimate=pl.CostEstimate(
            flops=4 * terms * HEAD_SIZE, bytes_accessed=sum(w.size * 2 for w in weights), transcendentals=terms
        ),
        name="attend",
    )(info, *docs, *now, *before, *queries, *weights)


def first_half_kernel(rows_here, weight, fetch, total, fetched, semaphore):
    copy = pltpu.make_async_copy(fetch, fetched, semaphore)
    copy.start()
    for n in range(0, total.shape[1], TILE):
        total[:, n : n + TILE] = jnp.dot(rows_here[...], weight[:, n : n + TILE], preferred_element_type=F32)
    copy.wait()


def first_half(rows_here, weight, fetch):
    count, depth = rows_here.shape
    width = weight.shape[1]
    return pl.pallas_call(
        first_half_kernel,
        out_shape=[pltpu.VMEM((count, width), F32), pltpu.VMEM(fetch.shape, fetch.dtype)],
        in_specs=[VMEM, VMEM, HBM],
        out_specs=[VMEM, VMEM],
        scratch_shapes=[pltpu.SemaphoreType.DMA],
        compiler_params=LIMIT,
        cost_estimate=pl.CostEstimate(
            flops=2 * count * depth * width, bytes_accessed=2 * depth * width, transcendentals=0
        ),
        name="first_half",
    )(rows_here, in_vmem(weight), fetch)


def project_kernel(*refs, terms, begun, share, halves):
    lhs, rhs, (*start, ) = refs[:terms], refs[terms : 2 * terms], refs[2 * terms : 2 * terms + begun]
    outs = refs[2 * terms + begun :]
    half = outs[0].shape[1]
    for n in range(0, half * halves, TILE):
        total = sum(
            jnp.dot(a[...], w[:, n : n + TILE], preferred_element_type=F32) for a, w in zip(lhs, rhs)
        )
        for s in start:
            total = total + s[:, n : n + TILE]
        for m in range(total.shape[0] // share):
            outs[m * halves + n // half][:, n % half : n % half + TILE] = total[m * share : (m + 1) * share].astype(BF16)


def project(lhs, rhs, start, share, halves):
    count, depth = lhs[0].shape
    width = rhs[0].shape[1]
    return pl.pallas_call(
        partial(project_kernel, terms=len(lhs), begun=len(start), share=share, halves=halves),
        out_shape=[jax.ShapeDtypeStruct((share, width // halves), BF16)] * (count // share * halves),
        in_specs=[VMEM] * (2 * len(lhs) + len(start)),
        out_specs=[VMEM] * (count // share * halves),
        compiler_params=LIMIT,
        cost_estimate=pl.CostEstimate(
            flops=2 * len(lhs) * count * depth * width, bytes_accessed=2 * count * width, transcendentals=0
        ),
        name="project",
    )(*lhs, *[in_vmem(w) for w in rhs], *[in_vmem(s) for s in start])


def on_device(queries, keys, values, doc_ids, block_mask, out_weight, *, order):
    groups, head_shards, slabs = (lax.axis_size(a) for a in ("srv", "head", "wsh"))
    srv, head, z = (lax.axis_index(a) for a in ("srv", "head", "wsh"))
    core, x, columns_x = head % 2, head // 2, head_shards // 2
    block = queries.shape[0]
    kv_local = keys.shape[1] // HEAD_SIZE
    heads = queries.shape[1] // HEAD_SIZE // slabs
    share = block // head_shards
    per_shard = slabs // head_shards
    table = jnp.asarray(order)
    staged = per_shard == 1
    stages = [[0], list(range(1, slabs))] if staged else [list(range(slabs))]
    halves = 2

    def kv_for(target):
        first = (target * kv_local // slabs) * HEAD_SIZE
        return [lax.dynamic_slice(a, (0, first), (block, HEAD_SIZE)) for a in (keys, values)]

    def query_rows(target, stage):
        pieces = [(table[target, i] * share, share) for i in stage] if staged else [(0, block)]
        return [
            lax.dynamic_slice(queries, (start, (target * heads + h) * HEAD_SIZE), (count, HEAD_SIZE))
            for h in range(heads)
            for start, count in pieces
        ]

    def around(array, k):
        return lax.ppermute(array, "wsh", [(i, (i + k) % slabs) for i in range(slabs)])

    siblings = [(h, h ^ 1) for h in range(head_shards)]

    def load(k):
        target = (z + k) % slabs
        return jnp.concatenate(kv_for(target) + query_rows(target, stages[0]), axis=0)

    loads = [load(0)] + [around(load(k), k) for k in range(1, slabs)]
    before = [
        lax.ppermute(a[: 2 * block], "srv", [(g, g + 1) for g in range(groups - 1)]) for a in loads
    ]
    weight_sibling = lax.ppermute(out_weight, "head", siblings)
    stage_queries = [loads]
    for stage in stages[1:]:
        rest = [jnp.concatenate(query_rows((z + k) % slabs, stage), axis=0) for k in range(slabs)]
        rest, loads = lax.optimization_barrier((rest, loads))
        stage_queries.append([rest[0]] + [around(rest[k], k) for k in range(1, slabs)])

    own_docs = lax.dynamic_slice(doc_ids, (srv * slabs * block,), (slabs * block,)).reshape(slabs, block)
    reach = SLAB_REACH - 1
    padded = jnp.concatenate([jnp.full((reach * block,), -1, jnp.int32), doc_ids])
    window = lax.dynamic_slice(padded, (srv * slabs * block,), ((slabs + reach) * block,)).reshape(-1, block)
    opened = lax.dynamic_slice(block_mask, (srv * slabs, 0), (slabs, SLAB_REACH))
    key_doc = jnp.stack(
        [
            jnp.where(opened[:, reach - j, None] > 0, window[j : j + slabs], -1)
            for j in range(SLAB_REACH)
        ],
        axis=1,
    ).reshape(slabs, 1, SLAB_REACH * block)
    docs = (key_doc, own_docs[..., None])

    partials = []
    weight_near = None
    for n, (stage, arrived) in enumerate(zip(stages, stage_queries)):
        if staged:
            starts = [table[z, i] * share for i in stage]
            sizes = dict(share=share, pieces=len(stage))
        else:
            starts = [jnp.int32(0)]
            sizes = dict(share=block, pieces=1)
        info = jnp.stack([z, core, x] + starts).astype(jnp.int32)
        fetch = [] if n else [out_weight] if staged else [out_weight, weight_sibling]
        keep, send, *fetched = attend(
            info,
            docs,
            loads,
            before,
            arrived,
            fetch,
            heads=heads,
            offset=2 * block if n == 0 else 0,
            columns_x=columns_x,
            per_shard=per_shard,
            **sizes,
        )
        if not staged:
            keep, send = (
                jnp.concatenate(
                    [
                        lax.dynamic_slice_in_dim(a.reshape(columns_x, -1, a.shape[-1]), table[z, i] * share, share, 1)
                        for i in stage
                    ],
                    axis=1,
                )
                for a in (keep, send)
            )
        theirs = lax.ppermute(send, "head", siblings)
        keep, theirs = (a.reshape(-1, a.shape[-1]) for a in (keep, theirs))
        if n == 0 and staged:
            weight_near = fetched[0]
            begun, weight_far = first_half(keep, weight_near, weight_sibling)
            results = project([theirs], [weight_far], [begun], share, halves)
        else:
            if fetched:
                weight_near, weight_far = fetched
            results = project([keep, theirs], [weight_near, weight_far], [], share, halves)
        for m in range(len(stage)):
            partials.append(
                [
                    [results[(k * len(stage) + m) * halves + half] for half in range(halves)]
                    for k in range(columns_x)
                ]
            )

    sums = [[] for _ in range(halves)]
    for piece in partials:
        for half in range(halves):
            total = piece[0][half].astype(F32)
            for k in range(1, columns_x):
                route = [(h, (h + 2 * k) % head_shards) for h in range(head_shards)]
                total = total + lax.ppermute(piece[k][half], "head", route).astype(F32)
            sums[half].append(total.astype(BF16))

    position = np.argsort(order, axis=1)

    def senders(direction, t):
        found = {}
        for i in range(slabs):
            step = i if direction > 0 else slabs - 1 - i
            if step <= t:
                d = slabs - 1 - t + step
                found[i] = int(position[i, d if direction > 0 else slabs - 1 - d])
        return found

    def message(which, own, arrived):
        picked = None
        for i, piece in which.items():
            picked = own[piece] if picked is None else jnp.where(z == i, own[piece], picked)
        if arrived is None:
            return picked
        return (picked.astype(F32) + arrived.astype(F32)).astype(BF16)

    arrived = [{1: None, -1: None} for _ in range(halves)]
    for t in range(slabs - 1):
        for half in range(halves):
            last = arrived[half]
            found = {direction: senders(direction, t) for direction in (1, -1)}
            routes = {direction: [(i, i + direction) for i in found[direction]] for direction in found}
            for direction in found:
                last[direction] = lax.ppermute(
                    message(found[direction], sums[half], last[direction]), "wsh", routes[direction]
                )
    outs = []
    for half in range(halves):
        total = sums[half][-1].astype(F32)
        if slabs > 1:
            total = total + arrived[half][1].astype(F32) + arrived[half][-1].astype(F32)
        outs.append(total.astype(BF16))
    return jnp.concatenate(outs, axis=1)


def solution(mesh):
    in_specs = (
        P(("srv", "wsh"), "head"),
        P(("srv", "wsh"), "head"),
        P(("srv", "wsh"), "head"),
        P(),
        P(),
        P(("head", "wsh"), None),
    )
    out_specs = P(("srv", "head", "wsh"), None)
    return jax.shard_map(
        partial(on_device, order=destination_order(mesh.shape["wsh"])),
        mesh=mesh,
        in_specs=in_specs,
        out_specs=out_specs,
        check_vma=False,
    )
```

```python
from functools import partial
import math

import jax
import jax.numpy as jnp
import numpy as np
from jax import lax
from jax.experimental import pallas as pl
from jax.experimental.pallas import tpu as pltpu
from jax.sharding import PartitionSpec as P

QUERY_HEAD_COUNT = 64
KEY_VALUE_HEADS = 8
HEAD_SIZE = 128
SLAB_REACH = 4

MASKED = -1e30
F32 = jnp.float32
BF16 = jnp.bfloat16
VMEM = pl.BlockSpec(memory_space=pltpu.VMEM)
SMEM = pl.BlockSpec(memory_space=pltpu.SMEM)
HBM = pl.BlockSpec(memory_space=pltpu.HBM)
LIMIT = pltpu.CompilerParams(vmem_limit_bytes=20 << 20)
TILE = 1024


def destination_order(count):
    table = []
    for z in range(count):
        due = {d: (count - 1 - d + z if d > z else count - 1 - z + d) for d in range(count)}
        due[z] = count
        table.append(sorted(range(count), key=lambda d: (due[d], -d if z < count // 2 else d)))
    return np.array(table, np.int32)


def in_vmem(array):
    return pltpu.with_memory_space_constraint(array, pltpu.VMEM)


def in_hbm(array):
    return pltpu.with_memory_space_constraint(array, pltpu.HBM)


def after(value, *others):
    return lax.optimization_barrier((value, others))[0]


def chosen(table, z, i):
    picked = jnp.int32(int(table[0, i]))
    for n in range(1, table.shape[0]):
        picked = jnp.where(z == n, jnp.int32(int(table[n, i])), picked)
    return picked


def joined(parts):
    return parts[0] if len(parts) == 1 else jnp.concatenate(parts, axis=0)


def pack_kernel(queries, keys, values, *outs, slabs, heads, kv_local, order, share, stages):
    z = lax.axis_index("wsh")
    block = queries.shape[0]
    for k in range(slabs):
        target = lax.rem(z + k, slabs)
        first = pl.multiple_of(lax.div(target * kv_local, slabs) * HEAD_SIZE, HEAD_SIZE)
        load = outs[k]
        load[:block, :] = keys[:, pl.ds(first, HEAD_SIZE)]
        load[block : 2 * block, :] = values[:, pl.ds(first, HEAD_SIZE)]
        for n, stage in enumerate(stages):
            out, place = outs[n * slabs + k], 2 * block if n == 0 else 0
            for h in range(heads):
                column = pl.multiple_of((target * heads + h) * HEAD_SIZE, HEAD_SIZE)
                for i in stage:
                    if share == block:
                        rows, count = slice(None), block
                    else:
                        rows, count = pl.ds(pl.multiple_of(chosen(order, target, i) * share, 16), share), share
                    out[place : place + count, :] = queries[rows, pl.ds(column, HEAD_SIZE)]
                    place += count


def pack(queries, keys, values, *, slabs, heads, kv_local, order, share, stages):
    block = queries.shape[0]
    counts = [heads * share * len(stage) + (2 * block if n == 0 else 0) for n, stage in enumerate(stages)]
    return pl.pallas_call(
        partial(
            pack_kernel, slabs=slabs, heads=heads, kv_local=kv_local, order=order, share=share, stages=stages
        ),
        out_shape=[jax.ShapeDtypeStruct((count, HEAD_SIZE), BF16) for count in counts for _ in range(slabs)],
        in_specs=[VMEM] * 3,
        out_specs=[VMEM] * (slabs * len(stages)),
        compiler_params=LIMIT,
        cost_estimate=pl.CostEstimate(flops=0, bytes_accessed=4 * queries.size, transcendentals=0),
        name="pack",
    )(queries, keys, values)


def attend_kernel(key_doc, *refs, slabs, heads, share, stage, order, offset, columns_x, per_shard, fetched):
    refs = list(refs)
    take = lambda n: [refs.pop(0) for _ in range(n)]
    now, before, queries, weights = take(slabs), take(slabs), take(slabs), take(fetched)
    (keep, send), copied = take(2), take(fetched)
    key_rows, value_rows = take(2)
    copies = [pltpu.make_async_copy(w, c, refs[0].at[n]) for n, (w, c) in enumerate(zip(weights, copied))]
    for copy in copies:
        copy.start()
    scale = math.log2(math.e) / math.sqrt(HEAD_SIZE)
    span = key_doc.shape[2]
    block = span // SLAB_REACH
    rows = share * len(stage)
    srv, head, z = (lax.axis_index(a) for a in ("srv", "head", "wsh"))
    core, x = lax.rem(head, 2), lax.div(head, 2)
    column = lax.broadcasted_iota(jnp.int32, (share, span), 1) - (SLAB_REACH - 1) * block
    row = lax.broadcasted_iota(jnp.int32, (share, span), 0)
    behind = [column - row - (0 if share == block else chosen(order, z, i) * share) for i in stage]
    causal = joined([b <= 0 for b in behind])
    for k in range(slabs):
        slab = lax.rem(z - k + slabs, slabs)
        for o in range(SLAB_REACH):
            place = slice((SLAB_REACH - 1 - o) * block, (SLAB_REACH - o) * block)
            held = (k + o) % slabs

            def fill(source):
                key_rows[place, :] = source[:block, :]
                value_rows[place, :] = source[block : 2 * block, :]

            if o == 0:
                fill(now[held])
            else:
                pl.when(slab >= o)(partial(fill, now[held]))
                pl.when(slab < o)(partial(fill, before[held]))
        docs = key_doc[srv * slabs + slab]
        query_doc = joined([jnp.max(jnp.where(b == 0, docs, -2.0), axis=1, keepdims=True) for b in behind])
        visible = causal & (query_doc == docs)
        scores = lax.dot_general(
            queries[k][offset : offset + heads * rows, :],
            key_rows[...],
            (((1,), (1,)), ((), ())),
            preferred_element_type=F32,
        ).reshape(heads, rows, span)
        scores = jnp.where(visible[None], scores, MASKED)
        largest = jnp.max(scores, axis=-1, keepdims=True)
        terms = jnp.exp2((scores - largest) * scale)
        normalizer = jnp.sum(terms, axis=-1, keepdims=True)
        weighted = jnp.dot(
            terms.reshape(heads * rows, span).astype(BF16), value_rows[...], preferred_element_type=F32
        ).reshape(heads, rows, HEAD_SIZE)
        result = (weighted / normalizer).astype(BF16)
        result = jnp.concatenate([result[h] for h in range(heads)], axis=1)
        target = lax.div(slab, per_shard)
        slot = lax.rem(lax.div(target, 2) - x + columns_x, columns_x) * per_shard + lax.rem(slab, per_shard)

        @pl.when(lax.rem(target, 2) == core)
        def _():
            keep[slot] = result

        @pl.when(lax.rem(target, 2) != core)
        def _():
            send[slot] = result

    for copy in copies:
        copy.wait()


def attend(key_doc, now, before, queries, weights, *, slabs, heads, share, stage, **rest):
    span = key_doc.shape[2]
    rows = share * len(stage)
    out = jax.ShapeDtypeStruct((slabs // 2, rows, heads * HEAD_SIZE), BF16)
    terms = slabs * rows * span * heads
    fetched = len(weights)
    return pl.pallas_call(
        partial(
            attend_kernel, slabs=slabs, heads=heads, share=share, stage=stage, fetched=fetched, **rest
        ),
        out_shape=[out, out] + [pltpu.VMEM(w.shape, w.dtype) for w in weights],
        in_specs=[VMEM] * (1 + 3 * slabs) + [HBM] * fetched,
        out_specs=[VMEM] * (2 + fetched),
        scratch_shapes=[pltpu.VMEM((span, HEAD_SIZE), BF16)] * 2
        + [pltpu.SemaphoreType.DMA((fetched,))] * (fetched > 0),
        compiler_params=LIMIT,
        cost_estimate=pl.CostEstimate(
            flops=4 * terms * HEAD_SIZE, bytes_accessed=sum(w.size * 2 for w in weights), transcendentals=terms
        ),
        name="attend",
    )(key_doc, *now, *before, *queries, *[in_hbm(w) for w in weights])


def first_half_kernel(rows_here, weight, total):
    for n in range(0, total.shape[1], TILE):
        total[:, n : n + TILE] = jnp.dot(rows_here[...], weight[:, n : n + TILE], preferred_element_type=F32)


def first_half(rows_here, weight):
    count, depth = rows_here.shape
    width = weight.shape[1]
    return pl.pallas_call(
        first_half_kernel,
        out_shape=pltpu.VMEM((count, width), F32),
        in_specs=[VMEM, VMEM],
        out_specs=VMEM,
        compiler_params=LIMIT,
        cost_estimate=pl.CostEstimate(flops=2 * count * depth * width, bytes_accessed=0, transcendentals=0),
        name="first_half",
    )(rows_here, in_vmem(weight))


def project_kernel(*refs, terms, begun, share, halves):
    lhs, rhs, start = refs[:terms], refs[terms : 2 * terms], refs[2 * terms : 2 * terms + begun]
    outs = refs[2 * terms + begun :]
    half = outs[0].shape[1]
    for n in range(0, half * halves, TILE):
        total = sum(
            jnp.dot(a[...], w[:, n : n + TILE], preferred_element_type=F32) for a, w in zip(lhs, rhs)
        )
        for s in start:
            total = total + s[:, n : n + TILE]
        for m in range(total.shape[0] // share):
            outs[m * halves + n // half][:, n % half : n % half + TILE] = total[m * share : (m + 1) * share].astype(BF16)


def project(lhs, rhs, start, share, halves):
    count, depth = lhs[0].shape
    width = rhs[0].shape[1]
    return pl.pallas_call(
        partial(project_kernel, terms=len(lhs), begun=len(start), share=share, halves=halves),
        out_shape=[jax.ShapeDtypeStruct((share, width // halves), BF16)] * (count // share * halves),
        in_specs=[VMEM] * (2 * len(lhs) + len(start)),
        out_specs=[VMEM] * (count // share * halves),
        compiler_params=LIMIT,
        cost_estimate=pl.CostEstimate(
            flops=2 * len(lhs) * count * depth * width, bytes_accessed=2 * count * width, transcendentals=0
        ),
        name="project",
    )(*lhs, *[in_vmem(w) for w in rhs], *[in_vmem(s) for s in start])


def on_device(queries, keys, values, doc_ids, block_mask, out_weight, *, order):
    groups, head_shards, slabs = (lax.axis_size(a) for a in ("srv", "head", "wsh"))
    z = lax.axis_index("wsh")
    columns_x = head_shards // 2
    block = queries.shape[0]
    heads = queries.shape[1] // HEAD_SIZE // slabs
    share = block // head_shards
    per_shard = slabs // head_shards
    staged = per_shard == 1
    stages = [[0], list(range(1, slabs))] if staged else [[0]]
    rows_at_once = share if staged else block
    halves = 2
    siblings = [(h, h ^ 1) for h in range(head_shards)]

    def around(array, k):
        return lax.ppermute(array, "wsh", [(i, (i + k) % slabs) for i in range(slabs)])

    packed = pack(
        queries,
        keys,
        values,
        slabs=slabs,
        heads=heads,
        kv_local=keys.shape[1] // HEAD_SIZE,
        order=order,
        share=rows_at_once,
        stages=stages,
    )
    loads = [packed[0]] + [around(packed[k], k) for k in range(1, slabs)]
    before = [
        lax.ppermute(a[: 2 * block], "srv", [(g, g + 1) for g in range(groups - 1)]) for a in loads
    ]
    weight_sibling = lax.ppermute(out_weight, "head", siblings)
    stage_queries = [loads]
    for n in range(1, len(stages)):
        rest = packed[n * slabs : (n + 1) * slabs]
        stage_queries.append([rest[0]] + [around(after(rest[k], *loads), k) for k in range(1, slabs)])

    reach = SLAB_REACH - 1
    padded = jnp.concatenate([jnp.full((reach, block), -1.0, F32), doc_ids.reshape(-1, block).astype(F32)])
    count = padded.shape[0] - reach
    key_doc = jnp.stack(
        [jnp.where(block_mask[:, reach - j, None] > 0, padded[j : j + count], -1.0) for j in range(SLAB_REACH)],
        axis=1,
    ).reshape(count, 1, SLAB_REACH * block)

    partials = []
    results = weight_near = None
    for n, (stage, arrived) in enumerate(zip(stages, stage_queries)):
        if n:
            arrived = after(arrived, *results)
        fetch = [] if n else [out_weight]
        keep, send, *fetched = attend(
            key_doc,
            loads,
            before,
            arrived,
            fetch,
            slabs=slabs,
            heads=heads,
            share=rows_at_once,
            stage=stage,
            order=order,
            offset=2 * block if n == 0 else 0,
            columns_x=columns_x,
            per_shard=per_shard,
        )
        pieces = stage
        if not staged:
            pieces = range(slabs)
            keep, send = (
                jnp.concatenate(
                    [
                        lax.dynamic_slice_in_dim(
                            a.reshape(columns_x, -1, a.shape[-1]), chosen(order, z, i) * share, share, 1
                        )
                        for i in pieces
                    ],
                    axis=1,
                )
                for a in (keep, send)
            )
        theirs = lax.ppermute(send, "head", siblings)
        keep, theirs = (a.reshape(-1, a.shape[-1]) for a in (keep, theirs))
        if n == 0 and staged:
            weight_near = fetched[0]
            begun = first_half(keep, weight_near)
            results = project([theirs], [weight_sibling], [begun], share, halves)
        else:
            if fetched:
                weight_near = fetched[0]
            results = project([keep, theirs], [weight_near, weight_sibling], [], share, halves)
        for m in range(len(pieces)):
            partials.append(
                [
                    [results[(k * len(pieces) + m) * halves + half] for half in range(halves)]
                    for k in range(columns_x)
                ]
            )

    position = np.argsort(order, axis=1)

    def senders(direction, t):
        found = {}
        for i in range(slabs):
            step = i if direction > 0 else slabs - 1 - i
            if step <= t:
                d = slabs - 1 - t + step
                found[i] = int(position[i, d if direction > 0 else slabs - 1 - d])
        return found

    def message(which, own, arrived):
        picked = None
        for i, piece in which.items():
            picked = own[piece] if picked is None else jnp.where(z == i, own[piece], picked)
        if arrived is None:
            return picked
        return (picked.astype(F32) + arrived.astype(F32)).astype(BF16)

    sums = [[] for _ in range(halves)]
    messages = [[] for _ in range(halves)]
    arrived = [{1: None, -1: None} for _ in range(halves)]
    for t in range(slabs):
        for half in range(halves):
            total = partials[t][0][half].astype(F32)
            for k in range(1, columns_x):
                route = [(h, (h + 2 * k) % head_shards) for h in range(head_shards)]
                piece = partials[t][k][half]
                if t >= 2:
                    piece = after(piece, *messages[half][t - 2])
                total = total + lax.ppermute(piece, "head", route).astype(F32)
            sums[half].append(total.astype(BF16))
            if t == slabs - 1:
                continue
            up, down = senders(1, t), senders(-1, t)
            if t + 1 < slabs - 2 - t:
                sent = message({**up, **down}, sums[half], arrived[half][1])
                both = lax.ppermute(sent, "wsh", [(i, i + 1) for i in up] + [(i, i - 1) for i in down])
                arrived[half] = {1: both, -1: both}
                messages[half].append([sent])
            else:
                sent = {
                    direction: message(found, sums[half], arrived[half][direction])
                    for direction, found in ((1, up), (-1, down))
                }
                for direction, found in ((1, up), (-1, down)):
                    arrived[half][direction] = lax.ppermute(
                        sent[direction], "wsh", [(i, i + direction) for i in found]
                    )
                messages[half].append(list(sent.values()))
    outs = []
    for half in range(halves):
        total = sums[half][-1].astype(F32)
        if slabs > 1:
            total = total + arrived[half][1].astype(F32) + arrived[half][-1].astype(F32)
        outs.append(total.astype(BF16))
    return jnp.concatenate(outs, axis=1)


def solution(mesh):
    in_specs = (
        P(("srv", "wsh"), "head"),
        P(("srv", "wsh"), "head"),
        P(("srv", "wsh"), "head"),
        P(),
        P(),
        P(("head", "wsh"), None),
    )
    out_specs = P(("srv", "head", "wsh"), None)
    return jax.shard_map(
        partial(on_device, order=destination_order(mesh.shape["wsh"])),
        mesh=mesh,
        in_specs=in_specs,
        out_specs=out_specs,
        check_vma=False,
    )
```

```python
from functools import partial
import math

import jax
import jax.numpy as jnp
import numpy as np
from jax import lax
from jax.experimental import pallas as pl
from jax.experimental.pallas import tpu as pltpu
from jax.sharding import PartitionSpec as P

QUERY_HEAD_COUNT = 64
KEY_VALUE_HEADS = 8
HEAD_SIZE = 128
SLAB_REACH = 4

MASKED = -1e30
F32 = jnp.float32
BF16 = jnp.bfloat16
VMEM = pl.BlockSpec(memory_space=pltpu.VMEM)
SMEM = pl.BlockSpec(memory_space=pltpu.SMEM)
HBM = pl.BlockSpec(memory_space=pltpu.HBM)
LIMIT = pltpu.CompilerParams(vmem_limit_bytes=20 << 20)
TILE = 1024
FREE = pl.CostEstimate(flops=0, bytes_accessed=0, transcendentals=0)


def destination_order(count):
    table = []
    for z in range(count):
        due = {d: (count - 1 - d + z if d > z else count - 1 - z + d) for d in range(count)}
        due[z] = count
        table.append(sorted(range(count), key=lambda d: (due[d], -d if z < count // 2 else d)))
    return np.array(table, np.int32)


def in_vmem(array):
    return pltpu.with_memory_space_constraint(array, pltpu.VMEM)


def in_hbm(array):
    return pltpu.with_memory_space_constraint(array, pltpu.HBM)


def after(value, *others):
    return lax.optimization_barrier((value, others))[0]


def chosen(table, z, i):
    picked = jnp.int32(int(table[0, i]))
    for n in range(1, table.shape[0]):
        picked = jnp.where(z == n, jnp.int32(int(table[n, i])), picked)
    return picked


def joined(parts):
    return parts[0] if len(parts) == 1 else jnp.concatenate(parts, axis=0)


def pack_kernel(queries, keys, values, *outs, slabs, heads, kv_local, order, share, stages):
    z = lax.axis_index("wsh")
    block = queries.shape[0]
    for k in range(slabs):
        target = lax.rem(z + k, slabs)
        first = pl.multiple_of(lax.div(target * kv_local, slabs) * HEAD_SIZE, HEAD_SIZE)
        load = outs[k]
        load[:block, :] = keys[:, pl.ds(first, HEAD_SIZE)]
        load[block : 2 * block, :] = values[:, pl.ds(first, HEAD_SIZE)]
        for n, stage in enumerate(stages):
            out, place = outs[n * slabs + k], 2 * block if n == 0 else 0
            for h in range(heads):
                column = pl.multiple_of((target * heads + h) * HEAD_SIZE, HEAD_SIZE)
                for i in stage:
                    if share == block:
                        rows, count = slice(None), block
                    else:
                        rows, count = pl.ds(pl.multiple_of(chosen(order, target, i) * share, 16), share), share
                    out[place : place + count, :] = queries[rows, pl.ds(column, HEAD_SIZE)]
                    place += count


def pack(queries, keys, values, *, slabs, heads, kv_local, order, share, stages):
    block = queries.shape[0]
    counts = [heads * share * len(stage) + (2 * block if n == 0 else 0) for n, stage in enumerate(stages)]
    return pl.pallas_call(
        partial(
            pack_kernel, slabs=slabs, heads=heads, kv_local=kv_local, order=order, share=share, stages=stages
        ),
        out_shape=[jax.ShapeDtypeStruct((count, HEAD_SIZE), BF16) for count in counts for _ in range(slabs)],
        in_specs=[VMEM] * 3,
        out_specs=[VMEM] * (slabs * len(stages)),
        compiler_params=LIMIT,
        cost_estimate=FREE,
        name="pack",
    )(queries, keys, values)


def attend_kernel(key_doc, *refs, slabs, heads, share, stage, order, offset, columns_x, per_shard, fetched):
    refs = list(refs)
    take = lambda n: [refs.pop(0) for _ in range(n)]
    now, before, queries, weights = take(slabs), take(slabs), take(slabs), take(fetched)
    (keep, send), copied = take(2), take(fetched)
    key_rows, value_rows = take(2)
    copies = [pltpu.make_async_copy(w, c, refs[0].at[n]) for n, (w, c) in enumerate(zip(weights, copied))]
    for copy in copies:
        copy.start()
    scale = math.log2(math.e) / math.sqrt(HEAD_SIZE)
    span = key_doc.shape[2]
    block = span // SLAB_REACH
    rows = share * len(stage)
    srv, head, z = (lax.axis_index(a) for a in ("srv", "head", "wsh"))
    core, x = lax.rem(head, 2), lax.div(head, 2)
    column = lax.broadcasted_iota(jnp.int32, (share, span), 1) - (SLAB_REACH - 1) * block
    row = lax.broadcasted_iota(jnp.int32, (share, span), 0)
    behind = [column - row - (0 if share == block else chosen(order, z, i) * share) for i in stage]
    causal = joined([b <= 0 for b in behind])
    for k in range(slabs):
        slab = lax.rem(z - k + slabs, slabs)
        for o in range(SLAB_REACH):
            place = slice((SLAB_REACH - 1 - o) * block, (SLAB_REACH - o) * block)
            held = (k + o) % slabs

            def fill(source):
                key_rows[place, :] = source[:block, :]
                value_rows[place, :] = source[block : 2 * block, :]

            if o == 0:
                fill(now[held])
            else:
                pl.when(slab >= o)(partial(fill, now[held]))
                pl.when(slab < o)(partial(fill, before[held]))
        docs = key_doc[srv * slabs + slab]
        query_doc = joined([jnp.max(jnp.where(b == 0, docs, -2.0), axis=1, keepdims=True) for b in behind])
        visible = causal & (query_doc == docs)
        scores = lax.dot_general(
            queries[k][offset : offset + heads * rows, :],
            key_rows[...],
            (((1,), (1,)), ((), ())),
            preferred_element_type=F32,
        ).reshape(heads, rows, span)
        scores = jnp.where(visible[None], scores, MASKED)
        largest = jnp.max(scores, axis=-1, keepdims=True)
        terms = jnp.exp2((scores - largest) * scale)
        normalizer = jnp.sum(terms, axis=-1, keepdims=True)
        weighted = jnp.dot(
            terms.reshape(heads * rows, span).astype(BF16), value_rows[...], preferred_element_type=F32
        ).reshape(heads, rows, HEAD_SIZE)
        result = (weighted / normalizer).astype(BF16)
        result = jnp.concatenate([result[h] for h in range(heads)], axis=1)
        target = lax.div(slab, per_shard)
        slot = lax.rem(lax.div(target, 2) - x + columns_x, columns_x) * per_shard + lax.rem(slab, per_shard)

        @pl.when(lax.rem(target, 2) == core)
        def _():
            keep[slot] = result

        @pl.when(lax.rem(target, 2) != core)
        def _():
            send[slot] = result

    for copy in copies:
        copy.wait()


def attend(key_doc, now, before, queries, weights, *, slabs, heads, share, stage, **rest):
    span = key_doc.shape[2]
    rows = share * len(stage)
    out = jax.ShapeDtypeStruct((slabs // 2, rows, heads * HEAD_SIZE), BF16)
    terms = slabs * rows * span * heads
    fetched = len(weights)
    return pl.pallas_call(
        partial(
            attend_kernel, slabs=slabs, heads=heads, share=share, stage=stage, fetched=fetched, **rest
        ),
        out_shape=[out, out] + [pltpu.VMEM(w.shape, w.dtype) for w in weights],
        in_specs=[VMEM] * (1 + 3 * slabs) + [HBM] * fetched,
        out_specs=[VMEM] * (2 + fetched),
        scratch_shapes=[pltpu.VMEM((span, HEAD_SIZE), BF16)] * 2
        + [pltpu.SemaphoreType.DMA((fetched,))] * (fetched > 0),
        compiler_params=LIMIT,
        cost_estimate=FREE,
        name="attend",
    )(key_doc, *now, *before, *queries, *[in_hbm(w) for w in weights])


def first_half_kernel(rows_here, weight, fetch, total, fetched, semaphore):
    copy = pltpu.make_async_copy(fetch, fetched, semaphore)
    copy.start()
    for n in range(0, total.shape[1], TILE):
        total[:, n : n + TILE] = jnp.dot(rows_here[...], weight[:, n : n + TILE], preferred_element_type=F32)
    copy.wait()


def first_half(rows_here, weight, fetch):
    return pl.pallas_call(
        first_half_kernel,
        out_shape=[pltpu.VMEM((rows_here.shape[0], weight.shape[1]), F32), pltpu.VMEM(fetch.shape, fetch.dtype)],
        in_specs=[VMEM, VMEM, HBM],
        out_specs=[VMEM, VMEM],
        scratch_shapes=[pltpu.SemaphoreType.DMA],
        compiler_params=LIMIT,
        cost_estimate=FREE,
        name="first_half",
    )(rows_here, in_vmem(weight), in_hbm(fetch))


def project_kernel(*refs, terms, begun, share, halves):
    lhs, rhs, start = refs[:terms], refs[terms : 2 * terms], refs[2 * terms : 2 * terms + begun]
    outs = refs[2 * terms + begun :]
    half = outs[0].shape[1]
    for n in range(0, half * halves, TILE):
        total = sum(
            jnp.dot(a[...], w[:, n : n + TILE], preferred_element_type=F32) for a, w in zip(lhs, rhs)
        )
        for s in start:
            total = total + s[:, n : n + TILE]
        for m in range(total.shape[0] // share):
            outs[m * halves + n // half][:, n % half : n % half + TILE] = total[m * share : (m + 1) * share].astype(BF16)


def project(lhs, rhs, start, share, halves):
    count, depth = lhs[0].shape
    width = rhs[0].shape[1]
    return pl.pallas_call(
        partial(project_kernel, terms=len(lhs), begun=len(start), share=share, halves=halves),
        out_shape=[jax.ShapeDtypeStruct((share, width // halves), BF16)] * (count // share * halves),
        in_specs=[VMEM] * (2 * len(lhs) + len(start)),
        out_specs=[VMEM] * (count // share * halves),
        compiler_params=LIMIT,
        cost_estimate=FREE,
        name="project",
    )(*lhs, *[in_vmem(w) for w in rhs], *[in_vmem(s) for s in start])


def on_device(queries, keys, values, doc_ids, block_mask, out_weight, *, order):
    groups, head_shards, slabs = (lax.axis_size(a) for a in ("srv", "head", "wsh"))
    z = lax.axis_index("wsh")
    columns_x = head_shards // 2
    block = queries.shape[0]
    heads = queries.shape[1] // HEAD_SIZE // slabs
    share = block // head_shards
    per_shard = slabs // head_shards
    staged = per_shard == 1
    stages = [[0], list(range(1, slabs))] if staged else [[0]]
    rows_at_once = share if staged else block
    halves = 2
    siblings = [(h, h ^ 1) for h in range(head_shards)]

    def around(array, k):
        return lax.ppermute(array, "wsh", [(i, (i + k) % slabs) for i in range(slabs)])

    packed = pack(
        queries,
        keys,
        values,
        slabs=slabs,
        heads=heads,
        kv_local=keys.shape[1] // HEAD_SIZE,
        order=order,
        share=rows_at_once,
        stages=stages,
    )
    loads = [packed[0]] + [around(packed[k], k) for k in range(1, slabs)]
    before = [
        lax.ppermute(a[: 2 * block], "srv", [(g, g + 1) for g in range(groups - 1)]) for a in loads
    ]
    weight_sibling = lax.ppermute(out_weight, "head", siblings)
    stage_queries = [loads]
    for n in range(1, len(stages)):
        rest = packed[n * slabs : (n + 1) * slabs]
        stage_queries.append([rest[0]] + [around(after(rest[k], *loads), k) for k in range(1, slabs)])

    reach = SLAB_REACH - 1
    padded = jnp.concatenate([jnp.full((reach, block), -1.0, F32), doc_ids.reshape(-1, block).astype(F32)])
    count = padded.shape[0] - reach
    key_doc = jnp.stack(
        [jnp.where(block_mask[:, reach - j, None] > 0, padded[j : j + count], -1.0) for j in range(SLAB_REACH)],
        axis=1,
    ).reshape(count, 1, SLAB_REACH * block)

    partials = []
    results = weight_near = None
    for n, (stage, arrived) in enumerate(zip(stages, stage_queries)):
        if n:
            arrived = after(arrived, *results)
        fetch = [] if n else [out_weight]
        keep, send, *fetched = attend(
            key_doc,
            loads,
            before,
            arrived,
            fetch,
            slabs=slabs,
            heads=heads,
            share=rows_at_once,
            stage=stage,
            order=order,
            offset=2 * block if n == 0 else 0,
            columns_x=columns_x,
            per_shard=per_shard,
        )
        pieces = stage
        if not staged:
            pieces = range(slabs)
            keep, send = (
                jnp.concatenate(
                    [
                        lax.dynamic_slice_in_dim(
                            a.reshape(columns_x, -1, a.shape[-1]), chosen(order, z, i) * share, share, 1
                        )
                        for i in pieces
                    ],
                    axis=1,
                )
                for a in (keep, send)
            )
        theirs = lax.ppermute(send, "head", siblings)
        keep, theirs = (a.reshape(-1, a.shape[-1]) for a in (keep, theirs))
        if n == 0 and staged:
            weight_near = fetched[0]
            begun, weight_sibling = first_half(keep, weight_near, weight_sibling)
            results = project([theirs], [weight_sibling], [begun], share, halves)
        else:
            if fetched:
                weight_near = fetched[0]
            results = project([keep, theirs], [weight_near, weight_sibling], [], share, halves)
        for m in range(len(pieces)):
            partials.append(
                [
                    [results[(k * len(pieces) + m) * halves + half] for half in range(halves)]
                    for k in range(columns_x)
                ]
            )

    position = np.argsort(order, axis=1)

    def senders(direction, t):
        found = {}
        for i in range(slabs):
            step = i if direction > 0 else slabs - 1 - i
            if step <= t:
                d = slabs - 1 - t + step
                found[i] = int(position[i, d if direction > 0 else slabs - 1 - d])
        return found

    def message(which, own, arrived):
        picked = None
        for i, piece in which.items():
            picked = own[piece] if picked is None else jnp.where(z == i, own[piece], picked)
        if arrived is None:
            return picked
        return (picked.astype(F32) + arrived.astype(F32)).astype(BF16)

    sums = [[] for _ in range(halves)]
    messages = [[] for _ in range(halves)]
    arrived = [{1: None, -1: None} for _ in range(halves)]
    for t in range(slabs):
        for half in range(halves):
            total = partials[t][0][half].astype(F32)
            for k in range(1, columns_x):
                route = [(h, (h + 2 * k) % head_shards) for h in range(head_shards)]
                piece = partials[t][k][half]
                if t >= 2:
                    piece = after(piece, *messages[half][t - 2])
                total = total + lax.ppermute(piece, "head", route).astype(F32)
            sums[half].append(total.astype(BF16))
            if t == slabs - 1:
                continue
            up, down = senders(1, t), senders(-1, t)
            if t + 1 < slabs - 2 - t:
                sent = message({**up, **down}, sums[half], arrived[half][1])
                both = lax.ppermute(sent, "wsh", [(i, i + 1) for i in up] + [(i, i - 1) for i in down])
                arrived[half] = {1: both, -1: both}
                messages[half].append([sent])
            else:
                sent = {
                    direction: message(found, sums[half], arrived[half][direction])
                    for direction, found in ((1, up), (-1, down))
                }
                for direction, found in ((1, up), (-1, down)):
                    arrived[half][direction] = lax.ppermute(
                        sent[direction], "wsh", [(i, i + direction) for i in found]
                    )
                messages[half].append(list(sent.values()))
    outs = []
    for half in range(halves):
        total = sums[half][-1].astype(F32)
        if slabs > 1:
            total = total + arrived[half][1].astype(F32) + arrived[half][-1].astype(F32)
        outs.append(total.astype(BF16))
    return jnp.concatenate(outs, axis=1)


def solution(mesh):
    in_specs = (
        P(("srv", "wsh"), "head"),
        P(("srv", "wsh"), "head"),
        P(("srv", "wsh"), "head"),
        P(),
        P(),
        P(("head", "wsh"), None),
    )
    out_specs = P(("srv", "head", "wsh"), None)
    return jax.shard_map(
        partial(on_device, order=destination_order(mesh.shape["wsh"])),
        mesh=mesh,
        in_specs=in_specs,
        out_specs=out_specs,
        check_vma=False,
    )
```

```python
from functools import partial
import math

import jax
import jax.numpy as jnp
import numpy as np
from jax import lax
from jax.experimental import pallas as pl
from jax.experimental.pallas import tpu as pltpu
from jax.sharding import PartitionSpec as P

QUERY_HEAD_COUNT = 64
KEY_VALUE_HEADS = 8
HEAD_SIZE = 128
SLAB_REACH = 4

MASKED = -1e30
F32 = jnp.float32
BF16 = jnp.bfloat16
VMEM = pl.BlockSpec(memory_space=pltpu.VMEM)
SMEM = pl.BlockSpec(memory_space=pltpu.SMEM)
HBM = pl.BlockSpec(memory_space=pltpu.HBM)
LIMIT = pltpu.CompilerParams(vmem_limit_bytes=20 << 20)
TILE = 1024
FREE = pl.CostEstimate(flops=0, bytes_accessed=0, transcendentals=0)


def destination_order(count):
    table = []
    for z in range(count):
        due = {d: (count - 1 - d + z if d > z else count - 1 - z + d) for d in range(count)}
        due[z] = count
        table.append(sorted(range(count), key=lambda d: (due[d], -d if z < count // 2 else d)))
    return np.array(table, np.int32)


def in_vmem(array):
    return pltpu.with_memory_space_constraint(array, pltpu.VMEM)


def in_hbm(array):
    return pltpu.with_memory_space_constraint(array, pltpu.HBM)


def after(value, *others):
    return lax.optimization_barrier((value, others))[0]


def chosen(table, z, i):
    picked = jnp.int32(int(table[0, i]))
    for n in range(1, table.shape[0]):
        picked = jnp.where(z == n, jnp.int32(int(table[n, i])), picked)
    return picked


def joined(parts):
    return parts[0] if len(parts) == 1 else jnp.concatenate(parts, axis=0)


def pack_kernel(queries, keys, values, *refs, slabs, heads, kv_local, order, share, stages):
    *outs, all_queries, all_keys, all_values, semaphores = refs
    z = lax.axis_index("wsh")
    pairs = ((keys, all_keys), (values, all_values), (queries, all_queries))
    copies = [pltpu.make_async_copy(a, b, semaphores.at[n]) for n, (a, b) in enumerate(pairs)]
    for copy in copies:
        copy.start()
    block = queries.shape[0]
    targets = [lax.rem(z + k, slabs) for k in range(slabs)]
    for n in range(2):
        copies[n].wait()
        for k, target in enumerate(targets):
            first = pl.multiple_of(lax.div(target * kv_local, slabs) * HEAD_SIZE, HEAD_SIZE)
            outs[k][n * block : (n + 1) * block, :] = pairs[n][1][:, pl.ds(first, HEAD_SIZE)]
    copies[2].wait()
    for n, stage in enumerate(stages, 1):
        for k, target in enumerate(targets):
            place = 0
            for h in range(heads):
                column = pl.multiple_of((target * heads + h) * HEAD_SIZE, HEAD_SIZE)
                for i in stage:
                    if share == block:
                        rows, count = slice(None), block
                    else:
                        rows, count = pl.ds(pl.multiple_of(chosen(order, target, i) * share, 16), share), share
                    outs[n * slabs + k][place : place + count, :] = all_queries[rows, pl.ds(column, HEAD_SIZE)]
                    place += count


def pack(queries, keys, values, *, slabs, heads, kv_local, order, share, stages):
    block = queries.shape[0]
    counts = [2 * block] + [heads * share * len(stage) for stage in stages]
    return pl.pallas_call(
        partial(
            pack_kernel, slabs=slabs, heads=heads, kv_local=kv_local, order=order, share=share, stages=stages
        ),
        out_shape=[jax.ShapeDtypeStruct((count, HEAD_SIZE), BF16) for count in counts for _ in range(slabs)],
        in_specs=[HBM] * 3,
        out_specs=[VMEM] * (slabs * len(counts)),
        scratch_shapes=[pltpu.VMEM(a.shape, BF16) for a in (queries, keys, values)]
        + [pltpu.SemaphoreType.DMA((3,))],
        compiler_params=LIMIT,
        cost_estimate=FREE,
        name="pack",
    )(in_hbm(queries), in_hbm(keys), in_hbm(values))


def attend_kernel(key_doc, *refs, slabs, heads, share, stage, order, columns_x, per_shard, fetched):
    refs = list(refs)
    take = lambda n: [refs.pop(0) for _ in range(n)]
    now, before, queries, weights = take(slabs), take(slabs), take(slabs), take(fetched)
    (keep, send), copied = take(2), take(fetched)
    key_rows, value_rows = take(2)
    copies = [pltpu.make_async_copy(w, c, refs[0].at[n]) for n, (w, c) in enumerate(zip(weights, copied))]
    for copy in copies:
        copy.start()
    scale = math.log2(math.e) / math.sqrt(HEAD_SIZE)
    span = key_doc.shape[2]
    block = span // SLAB_REACH
    rows = share * len(stage)
    srv, head, z = (lax.axis_index(a) for a in ("srv", "head", "wsh"))
    core, x = lax.rem(head, 2), lax.div(head, 2)
    column = lax.broadcasted_iota(jnp.int32, (share, span), 1) - (SLAB_REACH - 1) * block
    row = lax.broadcasted_iota(jnp.int32, (share, span), 0)
    behind = [column - row - (0 if share == block else chosen(order, z, i) * share) for i in stage]
    causal = joined([b <= 0 for b in behind])
    for k in range(slabs):
        slab = lax.rem(z - k + slabs, slabs)
        for o in range(SLAB_REACH):
            place = slice((SLAB_REACH - 1 - o) * block, (SLAB_REACH - o) * block)
            held = (k + o) % slabs

            def fill(source):
                key_rows[place, :] = source[:block, :]
                value_rows[place, :] = source[block : 2 * block, :]

            if o == 0:
                fill(now[held])
            else:
                pl.when(slab >= o)(partial(fill, now[held]))
                pl.when(slab < o)(partial(fill, before[held]))
        docs = key_doc[srv * slabs + slab]
        query_doc = joined([jnp.max(jnp.where(b == 0, docs, -2.0), axis=1, keepdims=True) for b in behind])
        visible = causal & (query_doc == docs)
        scores = lax.dot_general(
            queries[k][...],
            key_rows[...],
            (((1,), (1,)), ((), ())),
            preferred_element_type=F32,
        ).reshape(heads, rows, span)
        scores = jnp.where(visible[None], scores, MASKED)
        largest = jnp.max(scores, axis=-1, keepdims=True)
        terms = jnp.exp2((scores - largest) * scale)
        normalizer = jnp.sum(terms, axis=-1, keepdims=True)
        weighted = jnp.dot(
            terms.reshape(heads * rows, span).astype(BF16), value_rows[...], preferred_element_type=F32
        ).reshape(heads, rows, HEAD_SIZE)
        result = (weighted / normalizer).astype(BF16)
        result = jnp.concatenate([result[h] for h in range(heads)], axis=1)
        target = lax.div(slab, per_shard)
        slot = lax.rem(lax.div(target, 2) - x + columns_x, columns_x) * per_shard + lax.rem(slab, per_shard)

        @pl.when(lax.rem(target, 2) == core)
        def _():
            keep[slot] = result

        @pl.when(lax.rem(target, 2) != core)
        def _():
            send[slot] = result

    for copy in copies:
        copy.wait()


def attend(key_doc, now, before, queries, weights, *, slabs, heads, share, stage, **rest):
    span = key_doc.shape[2]
    rows = share * len(stage)
    out = jax.ShapeDtypeStruct((slabs // 2, rows, heads * HEAD_SIZE), BF16)
    terms = slabs * rows * span * heads
    fetched = len(weights)
    return pl.pallas_call(
        partial(
            attend_kernel, slabs=slabs, heads=heads, share=share, stage=stage, fetched=fetched, **rest
        ),
        out_shape=[out, out] + [pltpu.VMEM(w.shape, w.dtype) for w in weights],
        in_specs=[VMEM] * (1 + 3 * slabs) + [HBM] * fetched,
        out_specs=[VMEM] * (2 + fetched),
        scratch_shapes=[pltpu.VMEM((span, HEAD_SIZE), BF16)] * 2
        + [pltpu.SemaphoreType.DMA((fetched,))] * (fetched > 0),
        compiler_params=LIMIT,
        cost_estimate=pl.CostEstimate(flops=4 * terms * HEAD_SIZE, bytes_accessed=0, transcendentals=terms),
        name="attend",
    )(key_doc, *now, *before, *queries, *[in_hbm(w) for w in weights])


def first_half_kernel(rows_here, weight, fetch, total, fetched, semaphore):
    copy = pltpu.make_async_copy(fetch, fetched, semaphore)
    copy.start()
    for n in range(0, total.shape[1], TILE):
        total[:, n : n + TILE] = jnp.dot(rows_here[...], weight[:, n : n + TILE], preferred_element_type=F32)
    copy.wait()


def first_half(rows_here, weight, fetch):
    return pl.pallas_call(
        first_half_kernel,
        out_shape=[pltpu.VMEM((rows_here.shape[0], weight.shape[1]), F32), pltpu.VMEM(fetch.shape, fetch.dtype)],
        in_specs=[VMEM, VMEM, HBM],
        out_specs=[VMEM, VMEM],
        scratch_shapes=[pltpu.SemaphoreType.DMA],
        compiler_params=LIMIT,
        cost_estimate=FREE,
        name="first_half",
    )(rows_here, in_vmem(weight), in_hbm(fetch))


def project_kernel(*refs, terms, begun, share, halves):
    lhs, rhs, start = refs[:terms], refs[terms : 2 * terms], refs[2 * terms : 2 * terms + begun]
    outs = refs[2 * terms + begun :]
    half = outs[0].shape[1]
    for n in range(0, half * halves, TILE):
        total = sum(
            jnp.dot(a[...], w[:, n : n + TILE], preferred_element_type=F32) for a, w in zip(lhs, rhs)
        )
        for s in start:
            total = total + s[:, n : n + TILE]
        for m in range(total.shape[0] // share):
            outs[m * halves + n // half][:, n % half : n % half + TILE] = total[m * share : (m + 1) * share].astype(BF16)


def project(lhs, rhs, start, share, halves):
    count, depth = lhs[0].shape
    width = rhs[0].shape[1]
    return pl.pallas_call(
        partial(project_kernel, terms=len(lhs), begun=len(start), share=share, halves=halves),
        out_shape=[jax.ShapeDtypeStruct((share, width // halves), BF16)] * (count // share * halves),
        in_specs=[VMEM] * (2 * len(lhs) + len(start)),
        out_specs=[VMEM] * (count // share * halves),
        compiler_params=LIMIT,
        cost_estimate=FREE,
        name="project",
    )(*lhs, *[in_vmem(w) for w in rhs], *[in_vmem(s) for s in start])


def on_device(queries, keys, values, doc_ids, block_mask, out_weight, *, order):
    groups, head_shards, slabs = (lax.axis_size(a) for a in ("srv", "head", "wsh"))
    z = lax.axis_index("wsh")
    columns_x = head_shards // 2
    block = queries.shape[0]
    heads = queries.shape[1] // HEAD_SIZE // slabs
    share = block // head_shards
    per_shard = slabs // head_shards
    staged = per_shard == 1
    stages = [[0], list(range(1, slabs))] if staged else [[0]]
    rows_at_once = share if staged else block
    halves = 2
    siblings = [(h, h ^ 1) for h in range(head_shards)]

    def around(array, k):
        return lax.ppermute(array, "wsh", [(i, (i + k) % slabs) for i in range(slabs)])

    packed = pack(
        queries,
        keys,
        values,
        slabs=slabs,
        heads=heads,
        kv_local=keys.shape[1] // HEAD_SIZE,
        order=order,
        share=rows_at_once,
        stages=stages,
    )
    loads = [packed[0]] + [around(packed[k], k) for k in range(1, slabs)]
    before = [
        lax.ppermute(a, "srv", [(g, g + 1) for g in range(groups - 1)]) for a in loads
    ]
    weight_sibling = lax.ppermute(out_weight, "head", siblings)
    stage_queries = []
    for n in range(len(stages)):
        sent = packed[(n + 1) * slabs : (n + 2) * slabs]
        if n:
            sent = [after(a, *loads) for a in sent]
        stage_queries.append([sent[0]] + [around(sent[k], k) for k in range(1, slabs)])

    reach = SLAB_REACH - 1
    padded = jnp.concatenate([jnp.full((reach, block), -1.0, F32), doc_ids.reshape(-1, block).astype(F32)])
    count = padded.shape[0] - reach
    key_doc = jnp.stack(
        [jnp.where(block_mask[:, reach - j, None] > 0, padded[j : j + count], -1.0) for j in range(SLAB_REACH)],
        axis=1,
    ).reshape(count, 1, SLAB_REACH * block)

    partials = []
    results = None
    for n, (stage, arrived) in enumerate(zip(stages, stage_queries)):
        if n:
            arrived = after(arrived, *results)
        fetch = [out_weight] if n == 0 else [out_weight, weight_sibling]
        keep, send, *fetched = attend(
            key_doc,
            loads,
            before,
            arrived,
            fetch,
            slabs=slabs,
            heads=heads,
            share=rows_at_once,
            stage=stage,
            order=order,
            columns_x=columns_x,
            per_shard=per_shard,
        )
        pieces = stage
        if not staged:
            pieces = range(slabs)
            keep, send = (
                jnp.concatenate(
                    [
                        lax.dynamic_slice_in_dim(
                            a.reshape(columns_x, -1, a.shape[-1]), chosen(order, z, i) * share, share, 1
                        )
                        for i in pieces
                    ],
                    axis=1,
                )
                for a in (keep, send)
            )
        theirs = lax.ppermute(send, "head", siblings)
        keep, theirs = (a.reshape(-1, a.shape[-1]) for a in (keep, theirs))
        if n == 0 and staged:
            begun, far = first_half(keep, fetched[0], weight_sibling)
            results = project([theirs], [far], [begun], share, halves)
        else:
            weights = fetched if n else [fetched[0], weight_sibling]
            results = project([keep, theirs], weights, [], share, halves)
        for m in range(len(pieces)):
            partials.append(
                [
                    [results[(k * len(pieces) + m) * halves + half] for half in range(halves)]
                    for k in range(columns_x)
                ]
            )

    position = np.argsort(order, axis=1)

    def senders(direction, t):
        found = {}
        for i in range(slabs):
            step = i if direction > 0 else slabs - 1 - i
            if step <= t:
                d = slabs - 1 - t + step
                found[i] = int(position[i, d if direction > 0 else slabs - 1 - d])
        return found

    def message(which, own, arrived):
        picked = None
        for i, piece in which.items():
            picked = own[piece] if picked is None else jnp.where(z == i, own[piece], picked)
        if arrived is None:
            return picked
        return (picked.astype(F32) + arrived.astype(F32)).astype(BF16)

    sums = [[] for _ in range(halves)]
    messages = [[] for _ in range(halves)]
    arrived = [{1: None, -1: None} for _ in range(halves)]
    for t in range(slabs):
        for half in range(halves):
            total = partials[t][0][half].astype(F32)
            for k in range(1, columns_x):
                route = [(h, (h + 2 * k) % head_shards) for h in range(head_shards)]
                piece = partials[t][k][half]
                if t >= 2:
                    piece = after(piece, *messages[half][t - 2])
                total = total + lax.ppermute(piece, "head", route).astype(F32)
            sums[half].append(total.astype(BF16))
            if t == slabs - 1:
                continue
            up, down = senders(1, t), senders(-1, t)
            if t + 1 < slabs - 2 - t:
                sent = message({**up, **down}, sums[half], arrived[half][1])
                both = lax.ppermute(sent, "wsh", [(i, i + 1) for i in up] + [(i, i - 1) for i in down])
                arrived[half] = {1: both, -1: both}
                messages[half].append([sent])
            else:
                sent = {
                    direction: message(found, sums[half], arrived[half][direction])
                    for direction, found in ((1, up), (-1, down))
                }
                for direction, found in ((1, up), (-1, down)):
                    arrived[half][direction] = lax.ppermute(
                        sent[direction], "wsh", [(i, i + direction) for i in found]
                    )
                messages[half].append(list(sent.values()))
    outs = []
    for half in range(halves):
        total = sums[half][-1].astype(F32)
        if slabs > 1:
            total = total + arrived[half][1].astype(F32) + arrived[half][-1].astype(F32)
        outs.append(total.astype(BF16))
    return jnp.concatenate(outs, axis=1)


def solution(mesh):
    in_specs = (
        P(("srv", "wsh"), "head"),
        P(("srv", "wsh"), "head"),
        P(("srv", "wsh"), "head"),
        P(),
        P(),
        P(("head", "wsh"), None),
    )
    out_specs = P(("srv", "head", "wsh"), None)
    return jax.shard_map(
        partial(on_device, order=destination_order(mesh.shape["wsh"])),
        mesh=mesh,
        in_specs=in_specs,
        out_specs=out_specs,
        check_vma=False,
    )
```

```python
from functools import partial
import math

import jax
import jax.numpy as jnp
import numpy as np
from jax import lax
from jax.experimental import pallas as pl
from jax.experimental.pallas import tpu as pltpu
from jax.sharding import PartitionSpec as P

QUERY_HEAD_COUNT = 64
KEY_VALUE_HEADS = 8
HEAD_SIZE = 128
SLAB_REACH = 4

MASKED = -1e30
F32 = jnp.float32
BF16 = jnp.bfloat16
VMEM = pl.BlockSpec(memory_space=pltpu.VMEM)
SMEM = pl.BlockSpec(memory_space=pltpu.SMEM)
HBM = pl.BlockSpec(memory_space=pltpu.HBM)
LIMIT = pltpu.CompilerParams(vmem_limit_bytes=14 << 20)
TILE = 1024
FREE = pl.CostEstimate(flops=0, bytes_accessed=0, transcendentals=0)


def destination_order(count):
    table = []
    for z in range(count):
        due = {d: (count - 1 - d + z if d > z else count - 1 - z + d) for d in range(count)}
        due[z] = count
        table.append(sorted(range(count), key=lambda d: (due[d], -d if z < count // 2 else d)))
    return np.array(table, np.int32)


def in_vmem(array):
    return pltpu.with_memory_space_constraint(array, pltpu.VMEM)


def in_hbm(array):
    return pltpu.with_memory_space_constraint(array, pltpu.HBM)


def after(value, *others):
    return lax.optimization_barrier((value, others))[0]


def chosen(table, z, i):
    picked = jnp.int32(int(table[0, i]))
    for n in range(1, table.shape[0]):
        picked = jnp.where(z == n, jnp.int32(int(table[n, i])), picked)
    return picked


def joined(parts):
    return parts[0] if len(parts) == 1 else jnp.concatenate(parts, axis=0)


def pack_kernel(queries, keys, values, *refs, slabs, heads, kv_local, order, share, stages):
    *outs, all_queries, all_keys, all_values, semaphores = refs
    z = lax.axis_index("wsh")
    pairs = ((keys, all_keys), (values, all_values), (queries, all_queries))
    copies = [pltpu.make_async_copy(a, b, semaphores.at[n]) for n, (a, b) in enumerate(pairs)]
    for copy in copies:
        copy.start()
    block = queries.shape[0]
    targets = [lax.rem(z + k, slabs) for k in range(slabs)]
    for n in range(2):
        copies[n].wait()
        for k, target in enumerate(targets):
            first = pl.multiple_of(lax.div(target * kv_local, slabs) * HEAD_SIZE, HEAD_SIZE)
            outs[k][n * block : (n + 1) * block, :] = pairs[n][1][:, pl.ds(first, HEAD_SIZE)]
    copies[2].wait()
    for n, stage in enumerate(stages):
        for k, target in enumerate(targets):
            place = 2 * block if n == 0 else 0
            for h in range(heads):
                column = pl.multiple_of((target * heads + h) * HEAD_SIZE, HEAD_SIZE)
                for i in stage:
                    if share == block:
                        rows, count = slice(None), block
                    else:
                        rows, count = pl.ds(pl.multiple_of(chosen(order, target, i) * share, 16), share), share
                    outs[n * slabs + k][place : place + count, :] = all_queries[rows, pl.ds(column, HEAD_SIZE)]
                    place += count


def pack(queries, keys, values, *, slabs, heads, kv_local, order, share, stages):
    block = queries.shape[0]
    counts = [heads * share * len(stage) + (2 * block if n == 0 else 0) for n, stage in enumerate(stages)]
    return pl.pallas_call(
        partial(
            pack_kernel, slabs=slabs, heads=heads, kv_local=kv_local, order=order, share=share, stages=stages
        ),
        out_shape=[jax.ShapeDtypeStruct((count, HEAD_SIZE), BF16) for count in counts for _ in range(slabs)],
        in_specs=[HBM] * 3,
        out_specs=[VMEM] * (slabs * len(counts)),
        scratch_shapes=[pltpu.VMEM(a.shape, BF16) for a in (queries, keys, values)]
        + [pltpu.SemaphoreType.DMA((3,))],
        compiler_params=LIMIT,
        cost_estimate=FREE,
        name="pack",
    )(in_hbm(queries), in_hbm(keys), in_hbm(values))


def attend_kernel(key_doc, *refs, slabs, heads, share, stage, order, offset, columns_x, per_shard, fetched):
    refs = list(refs)
    take = lambda n: [refs.pop(0) for _ in range(n)]
    now, before, queries, weights = take(slabs), take(slabs), take(slabs), take(fetched)
    (keep, send), copied = take(2), take(fetched)
    key_rows, value_rows = take(2)
    copies = [pltpu.make_async_copy(w, c, refs[0].at[n]) for n, (w, c) in enumerate(zip(weights, copied))]
    for copy in copies:
        copy.start()
    scale = math.log2(math.e) / math.sqrt(HEAD_SIZE)
    span = key_doc.shape[2]
    block = span // SLAB_REACH
    rows = share * len(stage)
    srv, head, z = (lax.axis_index(a) for a in ("srv", "head", "wsh"))
    core, x = lax.rem(head, 2), lax.div(head, 2)
    column = lax.broadcasted_iota(jnp.int32, (share, span), 1) - (SLAB_REACH - 1) * block
    row = lax.broadcasted_iota(jnp.int32, (share, span), 0)
    behind = [column - row - (0 if share == block else chosen(order, z, i) * share) for i in stage]
    causal = joined([b <= 0 for b in behind])
    for k in range(slabs):
        slab = lax.rem(z - k + slabs, slabs)
        for o in range(SLAB_REACH):
            place = slice((SLAB_REACH - 1 - o) * block, (SLAB_REACH - o) * block)
            held = (k + o) % slabs

            def fill(source):
                key_rows[place, :] = source[:block, :]
                value_rows[place, :] = source[block : 2 * block, :]

            if o == 0:
                fill(now[held])
            else:
                pl.when(slab >= o)(partial(fill, now[held]))
                pl.when(slab < o)(partial(fill, before[held]))
        docs = key_doc[srv * slabs + slab]
        query_doc = joined([jnp.max(jnp.where(b == 0, docs, -2.0), axis=1, keepdims=True) for b in behind])
        visible = causal & (query_doc == docs)
        scores = lax.dot_general(
            queries[k][offset : offset + heads * rows, :],
            key_rows[...],
            (((1,), (1,)), ((), ())),
            preferred_element_type=F32,
        ).reshape(heads, rows, span)
        scores = jnp.where(visible[None], scores, MASKED)
        largest = jnp.max(scores, axis=-1, keepdims=True)
        terms = jnp.exp2((scores - largest) * scale)
        normalizer = jnp.sum(terms, axis=-1, keepdims=True)
        weighted = jnp.dot(
            terms.reshape(heads * rows, span).astype(BF16), value_rows[...], preferred_element_type=F32
        ).reshape(heads, rows, HEAD_SIZE)
        result = (weighted / normalizer).astype(BF16)
        result = jnp.concatenate([result[h] for h in range(heads)], axis=1)
        target = lax.div(slab, per_shard)
        slot = lax.rem(lax.div(target, 2) - x + columns_x, columns_x) * per_shard + lax.rem(slab, per_shard)

        @pl.when(lax.rem(target, 2) == core)
        def _():
            keep[slot] = result

        @pl.when(lax.rem(target, 2) != core)
        def _():
            send[slot] = result

    for copy in copies:
        copy.wait()


def attend(key_doc, now, before, queries, weights, *, slabs, heads, share, stage, **rest):
    span = key_doc.shape[2]
    rows = share * len(stage)
    out = jax.ShapeDtypeStruct((slabs // 2, rows, heads * HEAD_SIZE), BF16)
    terms = slabs * rows * span * heads
    fetched = len(weights)
    return pl.pallas_call(
        partial(
            attend_kernel, slabs=slabs, heads=heads, share=share, stage=stage, fetched=fetched, **rest
        ),
        out_shape=[out, out] + [pltpu.VMEM(w.shape, w.dtype) for w in weights],
        in_specs=[VMEM] * (1 + 3 * slabs) + [HBM] * fetched,
        out_specs=[VMEM] * (2 + fetched),
        scratch_shapes=[pltpu.VMEM((span, HEAD_SIZE), BF16)] * 2
        + [pltpu.SemaphoreType.DMA((fetched,))] * (fetched > 0),
        compiler_params=LIMIT,
        cost_estimate=pl.CostEstimate(flops=4 * terms * HEAD_SIZE, bytes_accessed=0, transcendentals=terms),
        name="attend",
    )(key_doc, *now, *before, *queries, *[in_hbm(w) for w in weights])


def first_half_kernel(rows_here, weight, fetch, total, fetched, semaphore):
    copy = pltpu.make_async_copy(fetch, fetched, semaphore)
    copy.start()
    for n in range(0, total.shape[1], TILE):
        total[:, n : n + TILE] = jnp.dot(rows_here[...], weight[:, n : n + TILE], preferred_element_type=F32)
    copy.wait()


def first_half(rows_here, weight, fetch):
    return pl.pallas_call(
        first_half_kernel,
        out_shape=[pltpu.VMEM((rows_here.shape[0], weight.shape[1]), F32), pltpu.VMEM(fetch.shape, fetch.dtype)],
        in_specs=[VMEM, VMEM, HBM],
        out_specs=[VMEM, VMEM],
        scratch_shapes=[pltpu.SemaphoreType.DMA],
        compiler_params=LIMIT,
        cost_estimate=FREE,
        name="first_half",
    )(rows_here, in_vmem(weight), in_hbm(fetch))


def project_kernel(*refs, terms, begun, share, halves):
    lhs, rhs, start = refs[:terms], refs[terms : 2 * terms], refs[2 * terms : 2 * terms + begun]
    outs = refs[2 * terms + begun :]
    half = outs[0].shape[1]
    for n in range(0, half * halves, TILE):
        total = sum(
            jnp.dot(a[...], w[:, n : n + TILE], preferred_element_type=F32) for a, w in zip(lhs, rhs)
        )
        for s in start:
            total = total + s[:, n : n + TILE]
        for m in range(total.shape[0] // share):
            outs[m * halves + n // half][:, n % half : n % half + TILE] = total[m * share : (m + 1) * share].astype(BF16)


def project(lhs, rhs, start, share, halves):
    count, depth = lhs[0].shape
    width = rhs[0].shape[1]
    return pl.pallas_call(
        partial(project_kernel, terms=len(lhs), begun=len(start), share=share, halves=halves),
        out_shape=[jax.ShapeDtypeStruct((share, width // halves), BF16)] * (count // share * halves),
        in_specs=[VMEM] * (2 * len(lhs) + len(start)),
        out_specs=[VMEM] * (count // share * halves),
        compiler_params=LIMIT,
        cost_estimate=FREE,
        name="project",
    )(*lhs, *[in_vmem(w) for w in rhs], *[in_vmem(s) for s in start])


def on_device(queries, keys, values, doc_ids, block_mask, out_weight, *, order):
    groups, head_shards, slabs = (lax.axis_size(a) for a in ("srv", "head", "wsh"))
    z = lax.axis_index("wsh")
    columns_x = head_shards // 2
    block = queries.shape[0]
    heads = queries.shape[1] // HEAD_SIZE // slabs
    share = block // head_shards
    per_shard = slabs // head_shards
    staged = per_shard == 1
    stages = [[0], list(range(1, slabs))] if staged else [[0]]
    rows_at_once = share if staged else block
    halves = 2
    siblings = [(h, h ^ 1) for h in range(head_shards)]

    def around(array, k):
        return lax.ppermute(array, "wsh", [(i, (i + k) % slabs) for i in range(slabs)])

    packed = pack(
        queries,
        keys,
        values,
        slabs=slabs,
        heads=heads,
        kv_local=keys.shape[1] // HEAD_SIZE,
        order=order,
        share=rows_at_once,
        stages=stages,
    )
    loads = [packed[0]] + [around(packed[k], k) for k in range(1, slabs)]
    behind = [loads[0]] + loads[:0:-1]
    cuts = [behind[: slabs // 2], behind[slabs // 2 :]] if slabs > 1 else [behind]
    cuts = [joined([a[: 2 * block] for a in cut]) for cut in cuts]
    cuts = [lax.ppermute(cut, "srv", [(g, g + 1) for g in range(groups - 1)]) for cut in cuts]
    before = [
        cut[n * 2 * block : (n + 1) * 2 * block] for cut in cuts for n in range(cut.shape[0] // (2 * block))
    ]
    before = [before[0]] + before[:0:-1]
    weight_sibling = lax.ppermute(out_weight, "head", siblings)
    stage_queries = [loads]
    for n in range(1, len(stages)):
        sent = [after(a, *loads) for a in packed[n * slabs : (n + 1) * slabs]]
        stage_queries.append([sent[0]] + [around(sent[k], k) for k in range(1, slabs)])

    reach = SLAB_REACH - 1
    padded = jnp.concatenate([jnp.full((reach, block), -1.0, F32), doc_ids.reshape(-1, block).astype(F32)])
    count = padded.shape[0] - reach
    key_doc = jnp.stack(
        [jnp.where(block_mask[:, reach - j, None] > 0, padded[j : j + count], -1.0) for j in range(SLAB_REACH)],
        axis=1,
    ).reshape(count, 1, SLAB_REACH * block)

    partials = []
    results = None
    for n, (stage, arrived) in enumerate(zip(stages, stage_queries)):
        if n:
            arrived = after(arrived, *results)
        keep, send, *fetched = attend(
            key_doc,
            loads,
            before,
            arrived,
            [out_weight],
            slabs=slabs,
            heads=heads,
            share=rows_at_once,
            stage=stage,
            order=order,
            offset=2 * block if n == 0 else 0,
            columns_x=columns_x,
            per_shard=per_shard,
        )
        pieces = stage
        if not staged:
            pieces = range(slabs)
            keep, send = (
                jnp.concatenate(
                    [
                        lax.dynamic_slice_in_dim(
                            a.reshape(columns_x, -1, a.shape[-1]), chosen(order, z, i) * share, share, 1
                        )
                        for i in pieces
                    ],
                    axis=1,
                )
                for a in (keep, send)
            )
        theirs = lax.ppermute(send, "head", siblings)
        keep, theirs = (a.reshape(-1, a.shape[-1]) for a in (keep, theirs))
        if staged:
            begun, far = first_half(keep, fetched[0], weight_sibling)
            results = project([theirs], [far], [begun], share, halves)
        else:
            results = project([keep, theirs], [fetched[0], weight_sibling], [], share, halves)
        for m in range(len(pieces)):
            partials.append(
                [
                    [results[(k * len(pieces) + m) * halves + half] for half in range(halves)]
                    for k in range(columns_x)
                ]
            )

    position = np.argsort(order, axis=1)

    def senders(direction, t):
        found = {}
        for i in range(slabs):
            step = i if direction > 0 else slabs - 1 - i
            if step <= t:
                d = slabs - 1 - t + step
                found[i] = int(position[i, d if direction > 0 else slabs - 1 - d])
        return found

    def message(which, own, arrived):
        picked = None
        for i, piece in which.items():
            picked = own[piece] if picked is None else jnp.where(z == i, own[piece], picked)
        if arrived is None:
            return picked
        return (picked.astype(F32) + arrived.astype(F32)).astype(BF16)

    sums = [[] for _ in range(halves)]
    crossed = [None] * halves
    arrived = [{1: None, -1: None} for _ in range(halves)]
    for t in range(slabs):
        for half in range(halves):
            total = partials[t][0][half].astype(F32)
            for k in range(1, columns_x):
                route = [(h, (h + 2 * k) % head_shards) for h in range(head_shards)]
                piece = partials[t][k][half]
                if t:
                    piece = after(piece, crossed[half])
                crossed[half] = lax.ppermute(piece, "head", route)
                total = total + crossed[half].astype(F32)
            sums[half].append(total.astype(BF16))
            if t == slabs - 1:
                continue
            up, down = senders(1, t), senders(-1, t)
            if t + 1 < slabs - 2 - t:
                sent = message({**up, **down}, sums[half], arrived[half][1])
                both = lax.ppermute(sent, "wsh", [(i, i + 1) for i in up] + [(i, i - 1) for i in down])
                arrived[half] = {1: both, -1: both}
            else:
                sent = {
                    direction: message(found, sums[half], arrived[half][direction])
                    for direction, found in ((1, up), (-1, down))
                }
                for direction, found in ((1, up), (-1, down)):
                    arrived[half][direction] = lax.ppermute(
                        sent[direction], "wsh", [(i, i + direction) for i in found]
                    )
    outs = []
    for half in range(halves):
        total = sums[half][-1].astype(F32)
        if slabs > 1:
            total = total + arrived[half][1].astype(F32) + arrived[half][-1].astype(F32)
        outs.append(total.astype(BF16))
    return jnp.concatenate(outs, axis=1)


def solution(mesh):
    in_specs = (
        P(("srv", "wsh"), "head"),
        P(("srv", "wsh"), "head"),
        P(("srv", "wsh"), "head"),
        P(),
        P(),
        P(("head", "wsh"), None),
    )
    out_specs = P(("srv", "head", "wsh"), None)
    return jax.shard_map(
        partial(on_device, order=destination_order(mesh.shape["wsh"])),
        mesh=mesh,
        in_specs=in_specs,
        out_specs=out_specs,
        check_vma=False,
    )
```

```python
from functools import partial
import math

import jax
import jax.numpy as jnp
import numpy as np
from jax import lax
from jax.experimental import pallas as pl
from jax.experimental.pallas import tpu as pltpu
from jax.sharding import PartitionSpec as P

QUERY_HEAD_COUNT = 64
KEY_VALUE_HEADS = 8
HEAD_SIZE = 128
SLAB_REACH = 4

MASKED = -1e30
F32 = jnp.float32
BF16 = jnp.bfloat16
VMEM = pl.BlockSpec(memory_space=pltpu.VMEM)
SMEM = pl.BlockSpec(memory_space=pltpu.SMEM)
HBM = pl.BlockSpec(memory_space=pltpu.HBM)
LIMIT = pltpu.CompilerParams(vmem_limit_bytes=18 << 20)
TILE = 1024
FREE = pl.CostEstimate(flops=0, bytes_accessed=0, transcendentals=0)


def destination_order(count):
    table = []
    for z in range(count):
        due = {d: (count - 1 - d + z if d > z else count - 1 - z + d) for d in range(count)}
        due[z] = count
        table.append(sorted(range(count), key=lambda d: (due[d], -d if z < count // 2 else d)))
    return np.array(table, np.int32)


def in_vmem(array):
    return pltpu.with_memory_space_constraint(array, pltpu.VMEM)


def in_hbm(array):
    return pltpu.with_memory_space_constraint(array, pltpu.HBM)


def after(value, *others):
    return lax.optimization_barrier((value, others))[0]


def chosen(table, z, i):
    picked = jnp.int32(int(table[0, i]))
    for n in range(1, table.shape[0]):
        picked = jnp.where(z == n, jnp.int32(int(table[n, i])), picked)
    return picked


def joined(parts):
    return parts[0] if len(parts) == 1 else jnp.concatenate(parts, axis=0)


def pack_kernel(queries, keys, values, *refs, slabs, heads, kv_local, order, share, stages):
    *outs, all_queries, all_keys, all_values, semaphores = refs
    z = lax.axis_index("wsh")
    pairs = ((keys, all_keys), (values, all_values), (queries, all_queries))
    copies = [pltpu.make_async_copy(a, b, semaphores.at[n]) for n, (a, b) in enumerate(pairs)]
    for copy in copies:
        copy.start()
    block = queries.shape[0]
    targets = [lax.rem(z + k, slabs) for k in range(slabs)]
    for n in range(2):
        copies[n].wait()
        for k, target in enumerate(targets):
            first = pl.multiple_of(lax.div(target * kv_local, slabs) * HEAD_SIZE, HEAD_SIZE)
            outs[k][n * block : (n + 1) * block, :] = pairs[n][1][:, pl.ds(first, HEAD_SIZE)]
    copies[2].wait()
    for n, stage in enumerate(stages):
        for k, target in enumerate(targets):
            place = 2 * block if n == 0 else 0
            for h in range(heads):
                column = pl.multiple_of((target * heads + h) * HEAD_SIZE, HEAD_SIZE)
                for i in stage:
                    if share == block:
                        rows, count = slice(None), block
                    else:
                        rows, count = pl.ds(pl.multiple_of(chosen(order, target, i) * share, 16), share), share
                    outs[n * slabs + k][place : place + count, :] = all_queries[rows, pl.ds(column, HEAD_SIZE)]
                    place += count


def pack(queries, keys, values, *, slabs, heads, kv_local, order, share, stages):
    block = queries.shape[0]
    counts = [heads * share * len(stage) + (2 * block if n == 0 else 0) for n, stage in enumerate(stages)]
    return pl.pallas_call(
        partial(
            pack_kernel, slabs=slabs, heads=heads, kv_local=kv_local, order=order, share=share, stages=stages
        ),
        out_shape=[jax.ShapeDtypeStruct((count, HEAD_SIZE), BF16) for count in counts for _ in range(slabs)],
        in_specs=[HBM] * 3,
        out_specs=[VMEM] * (slabs * len(counts)),
        scratch_shapes=[pltpu.VMEM(a.shape, BF16) for a in (queries, keys, values)]
        + [pltpu.SemaphoreType.DMA((3,))],
        compiler_params=LIMIT,
        cost_estimate=FREE,
        name="pack",
    )(in_hbm(queries), in_hbm(keys), in_hbm(values))


def attend_kernel(key_doc, *refs, slabs, heads, share, stage, order, offset, columns_x, per_shard, fetched):
    refs = list(refs)
    take = lambda n: [refs.pop(0) for _ in range(n)]
    now, before, queries, weights = take(slabs), take(slabs), take(slabs), take(fetched)
    (keep, send), copied = take(2), take(fetched)
    key_rows, value_rows = take(2)
    copies = [pltpu.make_async_copy(w, c, refs[0].at[n]) for n, (w, c) in enumerate(zip(weights, copied))]
    for copy in copies:
        copy.start()
    scale = math.log2(math.e) / math.sqrt(HEAD_SIZE)
    span = key_doc.shape[2]
    block = span // SLAB_REACH
    rows = share * len(stage)
    srv, head, z = (lax.axis_index(a) for a in ("srv", "head", "wsh"))
    core, x = lax.rem(head, 2), lax.div(head, 2)
    column = lax.broadcasted_iota(jnp.int32, (share, span), 1) - (SLAB_REACH - 1) * block
    row = lax.broadcasted_iota(jnp.int32, (share, span), 0)
    behind = [column - row - (0 if share == block else chosen(order, z, i) * share) for i in stage]
    causal = joined([b <= 0 for b in behind])
    for k in range(slabs):
        slab = lax.rem(z - k + slabs, slabs)
        for o in range(SLAB_REACH):
            place = slice((SLAB_REACH - 1 - o) * block, (SLAB_REACH - o) * block)
            held = (k + o) % slabs

            def fill(source):
                key_rows[place, :] = source[:block, :]
                value_rows[place, :] = source[block : 2 * block, :]

            if o == 0:
                fill(now[held])
            else:
                pl.when(slab >= o)(partial(fill, now[held]))
                pl.when(slab < o)(partial(fill, before[held]))
        docs = key_doc[srv * slabs + slab]
        query_doc = joined([jnp.max(jnp.where(b == 0, docs, -2.0), axis=1, keepdims=True) for b in behind])
        visible = causal & (query_doc == docs)
        scores = lax.dot_general(
            queries[k][offset : offset + heads * rows, :],
            key_rows[...],
            (((1,), (1,)), ((), ())),
            preferred_element_type=F32,
        ).reshape(heads, rows, span)
        scores = jnp.where(visible[None], scores, MASKED)
        largest = jnp.max(scores, axis=-1, keepdims=True)
        terms = jnp.exp2((scores - largest) * scale)
        normalizer = jnp.sum(terms, axis=-1, keepdims=True)
        weighted = jnp.dot(
            terms.reshape(heads * rows, span).astype(BF16), value_rows[...], preferred_element_type=F32
        ).reshape(heads, rows, HEAD_SIZE)
        result = (weighted / normalizer).astype(BF16)
        result = jnp.concatenate([result[h] for h in range(heads)], axis=1)
        target = lax.div(slab, per_shard)
        slot = lax.rem(lax.div(target, 2) - x + columns_x, columns_x) * per_shard + lax.rem(slab, per_shard)

        @pl.when(lax.rem(target, 2) == core)
        def _():
            keep[slot] = result

        @pl.when(lax.rem(target, 2) != core)
        def _():
            send[slot] = result

    for copy in copies:
        copy.wait()


def attend(key_doc, now, before, queries, weights, *, slabs, heads, share, stage, **rest):
    span = key_doc.shape[2]
    rows = share * len(stage)
    out = jax.ShapeDtypeStruct((slabs // 2, rows, heads * HEAD_SIZE), BF16)
    terms = slabs * rows * span * heads
    fetched = len(weights)
    return pl.pallas_call(
        partial(
            attend_kernel, slabs=slabs, heads=heads, share=share, stage=stage, fetched=fetched, **rest
        ),
        out_shape=[out, out] + [pltpu.VMEM(w.shape, w.dtype) for w in weights],
        in_specs=[VMEM] * (1 + 3 * slabs) + [HBM] * fetched,
        out_specs=[VMEM] * (2 + fetched),
        scratch_shapes=[pltpu.VMEM((span, HEAD_SIZE), BF16)] * 2
        + [pltpu.SemaphoreType.DMA((fetched,))] * (fetched > 0),
        compiler_params=LIMIT,
        cost_estimate=pl.CostEstimate(flops=4 * terms * HEAD_SIZE, bytes_accessed=0, transcendentals=terms),
        name="attend",
    )(key_doc, *now, *before, *queries, *[in_hbm(w) for w in weights])


def first_half_kernel(rows_here, near, far, total, far_held, semaphores, *held):
    copies = [pltpu.make_async_copy(far, far_held, semaphores.at[0])]
    for near_held in held:
        copies.insert(0, pltpu.make_async_copy(near, near_held, semaphores.at[1]))
    for copy in copies:
        copy.start()
    for copy in copies[:-1]:
        copy.wait()
    weight = held[0] if held else near
    for n in range(0, total.shape[1], TILE):
        total[:, n : n + TILE] = jnp.dot(rows_here[...], weight[:, n : n + TILE], preferred_element_type=F32)
    copies[-1].wait()


def first_half(rows_here, near, far, near_held):
    return pl.pallas_call(
        first_half_kernel,
        out_shape=[pltpu.VMEM((rows_here.shape[0], near.shape[1]), F32), pltpu.VMEM(far.shape, far.dtype)],
        in_specs=[VMEM, VMEM if near_held else HBM, HBM],
        out_specs=[VMEM, VMEM],
        scratch_shapes=[pltpu.SemaphoreType.DMA((2,))] + [pltpu.VMEM(near.shape, near.dtype)] * (not near_held),
        compiler_params=LIMIT,
        cost_estimate=FREE,
        name="first_half",
    )(rows_here, in_vmem(near) if near_held else in_hbm(near), in_hbm(far))


def project_kernel(*refs, terms, begun, share, halves):
    lhs, rhs, start = refs[:terms], refs[terms : 2 * terms], refs[2 * terms : 2 * terms + begun]
    outs = refs[2 * terms + begun :]
    half = outs[0].shape[1]
    for n in range(0, half * halves, TILE):
        total = sum(
            jnp.dot(a[...], w[:, n : n + TILE], preferred_element_type=F32) for a, w in zip(lhs, rhs)
        )
        for s in start:
            total = total + s[:, n : n + TILE]
        for m in range(total.shape[0] // share):
            outs[m * halves + n // half][:, n % half : n % half + TILE] = total[m * share : (m + 1) * share].astype(BF16)


def project(lhs, rhs, start, share, halves):
    count, depth = lhs[0].shape
    width = rhs[0].shape[1]
    return pl.pallas_call(
        partial(project_kernel, terms=len(lhs), begun=len(start), share=share, halves=halves),
        out_shape=[jax.ShapeDtypeStruct((share, width // halves), BF16)] * (count // share * halves),
        in_specs=[VMEM] * (2 * len(lhs) + len(start)),
        out_specs=[VMEM] * (count // share * halves),
        compiler_params=LIMIT,
        cost_estimate=FREE,
        name="project",
    )(*lhs, *[in_vmem(w) for w in rhs], *[in_vmem(s) for s in start])


def on_device(queries, keys, values, doc_ids, block_mask, out_weight, *, order):
    groups, head_shards, slabs = (lax.axis_size(a) for a in ("srv", "head", "wsh"))
    z = lax.axis_index("wsh")
    columns_x = head_shards // 2
    block = queries.shape[0]
    heads = queries.shape[1] // HEAD_SIZE // slabs
    share = block // head_shards
    per_shard = slabs // head_shards
    staged = per_shard == 1
    stages = [[0], list(range(1, slabs))] if staged else [[0]]
    rows_at_once = share if staged else block
    halves = 2
    siblings = [(h, h ^ 1) for h in range(head_shards)]

    def around(array, k):
        return lax.ppermute(array, "wsh", [(i, (i + k) % slabs) for i in range(slabs)])

    packed = pack(
        queries,
        keys,
        values,
        slabs=slabs,
        heads=heads,
        kv_local=keys.shape[1] // HEAD_SIZE,
        order=order,
        share=rows_at_once,
        stages=stages,
    )
    loads = [packed[0]] + [around(packed[k], k) for k in range(1, slabs)]
    before = [
        lax.ppermute(a[: 2 * block], "srv", [(g, g + 1) for g in range(groups - 1)]) for a in loads
    ]
    weight_sibling = lax.ppermute(out_weight, "head", siblings)
    stage_queries = [loads]
    for n in range(1, len(stages)):
        sent = [after(a, *loads) for a in packed[n * slabs : (n + 1) * slabs]]
        stage_queries.append([sent[0]] + [around(sent[k], k) for k in range(1, slabs)])

    reach = SLAB_REACH - 1
    padded = jnp.concatenate([jnp.full((reach, block), -1.0, F32), doc_ids.reshape(-1, block).astype(F32)])
    count = padded.shape[0] - reach
    key_doc = jnp.stack(
        [jnp.where(block_mask[:, reach - j, None] > 0, padded[j : j + count], -1.0) for j in range(SLAB_REACH)],
        axis=1,
    ).reshape(count, 1, SLAB_REACH * block)

    partials = []
    results = None
    for n, (stage, arrived) in enumerate(zip(stages, stage_queries)):
        if n:
            arrived = after(arrived, *results)
        keep, send, *fetched = attend(
            key_doc,
            loads,
            before,
            arrived,
            [out_weight] if n == 0 else [],
            slabs=slabs,
            heads=heads,
            share=rows_at_once,
            stage=stage,
            order=order,
            offset=2 * block if n == 0 else 0,
            columns_x=columns_x,
            per_shard=per_shard,
        )
        pieces = stage
        if not staged:
            pieces = range(slabs)
            keep, send = (
                jnp.concatenate(
                    [
                        lax.dynamic_slice_in_dim(
                            a.reshape(columns_x, -1, a.shape[-1]), chosen(order, z, i) * share, share, 1
                        )
                        for i in pieces
                    ],
                    axis=1,
                )
                for a in (keep, send)
            )
        theirs = lax.ppermute(send, "head", siblings)
        keep, theirs = (a.reshape(-1, a.shape[-1]) for a in (keep, theirs))
        if staged:
            near = fetched[0] if fetched else out_weight
            begun, far = first_half(keep, near, weight_sibling, bool(fetched))
            results = project([theirs], [far], [begun], share, 1 if n == 0 else halves)
        else:
            results = project([keep, theirs], [fetched[0], weight_sibling], [], share, halves)
        cuts = len(results) // (len(pieces) * columns_x)
        for m in range(len(pieces)):
            partials.append(
                [
                    [results[(k * len(pieces) + m) * cuts + cut] for cut in range(cuts)]
                    for k in range(columns_x)
                ]
            )

    position = np.argsort(order, axis=1)

    def senders(direction, t):
        found = {}
        for i in range(slabs):
            step = i if direction > 0 else slabs - 1 - i
            if step <= t:
                d = slabs - 1 - t + step
                found[i] = int(position[i, d if direction > 0 else slabs - 1 - d])
        return found

    def message(which, own, arrived):
        picked = None
        for i, piece in which.items():
            picked = own[piece] if picked is None else jnp.where(z == i, own[piece], picked)
        if arrived is None:
            return picked
        return (picked.astype(F32) + arrived.astype(F32)).astype(BF16)

    sums = [[] for _ in range(halves)]
    crossed = [None] * halves
    routes = [[(h, (h + 2 * k) % head_shards) for h in range(head_shards)] for k in range(columns_x)]
    arrived = [{1: None, -1: None} for _ in range(halves)]
    for t in range(slabs):
        for half in range(halves):
            whole = len(partials[t][0]) < halves
            if whole and half == 0:
                crossed = [[lax.ppermute(partials[t][k][0], "head", routes[k]) for k in range(1, columns_x)]] * halves
            elif not whole:
                pieces = [partials[t][k][half] for k in range(1, columns_x)]
                if t:
                    pieces = [after(piece, *crossed[half]) for piece in pieces]
                crossed[half] = [lax.ppermute(a, "head", r) for a, r in zip(pieces, routes[1:])]
            total = 0.0
            for piece in [partials[t][0][0 if whole else half]] + crossed[half]:
                if whole:
                    piece = piece[:, half * (piece.shape[1] // halves) : (half + 1) * (piece.shape[1] // halves)]
                total = total + piece.astype(F32)
            sums[half].append(total.astype(BF16))
            if t == slabs - 1:
                continue
            up, down = senders(1, t), senders(-1, t)
            if t + 1 < slabs - 2 - t:
                sent = message({**up, **down}, sums[half], arrived[half][1])
                both = lax.ppermute(sent, "wsh", [(i, i + 1) for i in up] + [(i, i - 1) for i in down])
                arrived[half] = {1: both, -1: both}
            else:
                sent = {
                    direction: message(found, sums[half], arrived[half][direction])
                    for direction, found in ((1, up), (-1, down))
                }
                for direction, found in ((1, up), (-1, down)):
                    arrived[half][direction] = lax.ppermute(
                        sent[direction], "wsh", [(i, i + direction) for i in found]
                    )
    outs = []
    for half in range(halves):
        total = sums[half][-1].astype(F32)
        if slabs > 1:
            total = total + arrived[half][1].astype(F32) + arrived[half][-1].astype(F32)
        outs.append(total.astype(BF16))
    return jnp.concatenate(outs, axis=1)


def solution(mesh):
    in_specs = (
        P(("srv", "wsh"), "head"),
        P(("srv", "wsh"), "head"),
        P(("srv", "wsh"), "head"),
        P(),
        P(),
        P(("head", "wsh"), None),
    )
    out_specs = P(("srv", "head", "wsh"), None)
    return jax.shard_map(
        partial(on_device, order=destination_order(mesh.shape["wsh"])),
        mesh=mesh,
        in_specs=in_specs,
        out_specs=out_specs,
        check_vma=False,
    )
```

```python
from functools import partial
import math

import jax
import jax.numpy as jnp
import numpy as np
from jax import lax
from jax.experimental import pallas as pl
from jax.experimental.pallas import tpu as pltpu
from jax.sharding import PartitionSpec as P

QUERY_HEAD_COUNT = 64
KEY_VALUE_HEADS = 8
HEAD_SIZE = 128
SLAB_REACH = 4

MASKED = -1e30
F32 = jnp.float32
BF16 = jnp.bfloat16
VMEM = pl.BlockSpec(memory_space=pltpu.VMEM)
SMEM = pl.BlockSpec(memory_space=pltpu.SMEM)
HBM = pl.BlockSpec(memory_space=pltpu.HBM)
LIMIT = pltpu.CompilerParams(vmem_limit_bytes=18 << 20)
TILE = 1024
FREE = pl.CostEstimate(flops=0, bytes_accessed=0, transcendentals=0)


def destination_order(count):
    table = []
    for z in range(count):
        due = {d: (count - 1 - d + z if d > z else count - 1 - z + d) for d in range(count)}
        due[z] = count
        table.append(sorted(range(count), key=lambda d: (due[d], -d if z < count // 2 else d)))
    return np.array(table, np.int32)


def in_vmem(array):
    return pltpu.with_memory_space_constraint(array, pltpu.VMEM)


def in_hbm(array):
    return pltpu.with_memory_space_constraint(array, pltpu.HBM)


def after(value, *others):
    return lax.optimization_barrier((value, others))[0]


def chosen(table, z, i):
    picked = jnp.int32(int(table[0, i]))
    for n in range(1, table.shape[0]):
        picked = jnp.where(z == n, jnp.int32(int(table[n, i])), picked)
    return picked


def joined(parts):
    return parts[0] if len(parts) == 1 else jnp.concatenate(parts, axis=0)


def pack_kernel(queries, keys, values, *refs, slabs, heads, kv_local, order, share, stages):
    *outs, all_queries, all_keys, all_values, semaphores = refs
    z = lax.axis_index("wsh")
    pairs = ((keys, all_keys), (values, all_values), (queries, all_queries))
    copies = [pltpu.make_async_copy(a, b, semaphores.at[n]) for n, (a, b) in enumerate(pairs)]
    for copy in copies:
        copy.start()
    block = queries.shape[0]
    targets = [lax.rem(z + k, slabs) for k in range(slabs)]
    for n in range(2):
        copies[n].wait()
        for k, target in enumerate(targets):
            first = pl.multiple_of(lax.div(target * kv_local, slabs) * HEAD_SIZE, HEAD_SIZE)
            outs[k][n * block : (n + 1) * block, :] = pairs[n][1][:, pl.ds(first, HEAD_SIZE)]
    copies[2].wait()
    for n, stage in enumerate(stages):
        for k, target in enumerate(targets):
            place = 2 * block if n == 0 else 0
            for h in range(heads):
                column = pl.multiple_of((target * heads + h) * HEAD_SIZE, HEAD_SIZE)
                for i in stage:
                    if share == block:
                        rows, count = slice(None), block
                    else:
                        rows, count = pl.ds(pl.multiple_of(chosen(order, target, i) * share, 16), share), share
                    outs[n * slabs + k][place : place + count, :] = all_queries[rows, pl.ds(column, HEAD_SIZE)]
                    place += count


def pack(queries, keys, values, *, slabs, heads, kv_local, order, share, stages):
    block = queries.shape[0]
    counts = [heads * share * len(stage) + (2 * block if n == 0 else 0) for n, stage in enumerate(stages)]
    return pl.pallas_call(
        partial(
            pack_kernel, slabs=slabs, heads=heads, kv_local=kv_local, order=order, share=share, stages=stages
        ),
        out_shape=[jax.ShapeDtypeStruct((count, HEAD_SIZE), BF16) for count in counts for _ in range(slabs)],
        in_specs=[HBM] * 3,
        out_specs=[VMEM] * (slabs * len(counts)),
        scratch_shapes=[pltpu.VMEM(a.shape, BF16) for a in (queries, keys, values)]
        + [pltpu.SemaphoreType.DMA((3,))],
        compiler_params=LIMIT,
        cost_estimate=FREE,
        name="pack",
    )(in_hbm(queries), in_hbm(keys), in_hbm(values))


def attend_kernel(key_doc, *refs, slabs, heads, share, stage, order, offset, columns_x, per_shard, fetched):
    refs = list(refs)
    take = lambda n: [refs.pop(0) for _ in range(n)]
    now, before, queries, weights = take(slabs), take(slabs), take(slabs), take(fetched)
    (keep, send), copied = take(2), take(fetched)
    key_rows, value_rows = take(2)
    copies = [pltpu.make_async_copy(w, c, refs[0].at[n]) for n, (w, c) in enumerate(zip(weights, copied))]
    for copy in copies:
        copy.start()
    scale = math.log2(math.e) / math.sqrt(HEAD_SIZE)
    span = key_doc.shape[2]
    block = span // SLAB_REACH
    rows = share * len(stage)
    srv, head, z = (lax.axis_index(a) for a in ("srv", "head", "wsh"))
    core, x = lax.rem(head, 2), lax.div(head, 2)
    column = lax.broadcasted_iota(jnp.int32, (share, span), 1) - (SLAB_REACH - 1) * block
    row = lax.broadcasted_iota(jnp.int32, (share, span), 0)
    behind = [column - row - (0 if share == block else chosen(order, z, i) * share) for i in stage]
    causal = joined([b <= 0 for b in behind])
    for k in range(slabs):
        slab = lax.rem(z - k + slabs, slabs)
        for o in range(SLAB_REACH):
            place = slice((SLAB_REACH - 1 - o) * block, (SLAB_REACH - o) * block)
            held = (k + o) % slabs

            def fill(source):
                key_rows[place, :] = source[:block, :]
                value_rows[place, :] = source[block : 2 * block, :]

            if o == 0:
                fill(now[held])
            else:
                pl.when(slab >= o)(partial(fill, now[held]))
                pl.when(slab < o)(partial(fill, before[held]))
        docs = key_doc[srv * slabs + slab]
        query_doc = joined([jnp.max(jnp.where(b == 0, docs, -2.0), axis=1, keepdims=True) for b in behind])
        visible = causal & (query_doc == docs)
        scores = lax.dot_general(
            queries[k][offset : offset + heads * rows, :],
            key_rows[...],
            (((1,), (1,)), ((), ())),
            preferred_element_type=F32,
        ).reshape(heads, rows, span)
        scores = jnp.where(visible[None], scores, MASKED)
        largest = jnp.max(scores, axis=-1, keepdims=True)
        terms = jnp.exp2((scores - largest) * scale)
        normalizer = jnp.sum(terms, axis=-1, keepdims=True)
        weighted = jnp.dot(
            terms.reshape(heads * rows, span).astype(BF16), value_rows[...], preferred_element_type=F32
        ).reshape(heads, rows, HEAD_SIZE)
        result = (weighted / normalizer).astype(BF16)
        result = jnp.concatenate([result[h] for h in range(heads)], axis=1)
        target = lax.div(slab, per_shard)
        slot = lax.rem(lax.div(target, 2) - x + columns_x, columns_x) * per_shard + lax.rem(slab, per_shard)

        @pl.when(lax.rem(target, 2) == core)
        def _():
            keep[slot] = result

        @pl.when(lax.rem(target, 2) != core)
        def _():
            send[slot] = result

    for copy in copies:
        copy.wait()


def attend(key_doc, now, before, queries, weights, *, slabs, heads, share, stage, **rest):
    span = key_doc.shape[2]
    rows = share * len(stage)
    out = jax.ShapeDtypeStruct((slabs // 2, rows, heads * HEAD_SIZE), BF16)
    terms = slabs * rows * span * heads
    fetched = len(weights)
    return pl.pallas_call(
        partial(
            attend_kernel, slabs=slabs, heads=heads, share=share, stage=stage, fetched=fetched, **rest
        ),
        out_shape=[out, out] + [pltpu.VMEM(w.shape, w.dtype) for w in weights],
        in_specs=[VMEM] * (1 + 3 * slabs) + [HBM] * fetched,
        out_specs=[VMEM] * (2 + fetched),
        scratch_shapes=[pltpu.VMEM((span, HEAD_SIZE), BF16)] * 2
        + [pltpu.SemaphoreType.DMA((fetched,))] * (fetched > 0),
        compiler_params=LIMIT,
        cost_estimate=pl.CostEstimate(flops=4 * terms * HEAD_SIZE, bytes_accessed=0, transcendentals=terms),
        name="attend",
    )(key_doc, *now, *before, *queries, *[in_hbm(w) for w in weights])


def first_half_kernel(rows_here, near, far, total, far_held, semaphores, *held):
    copies = [pltpu.make_async_copy(far, far_held, semaphores.at[0])]
    for near_held in held:
        copies.insert(0, pltpu.make_async_copy(near, near_held, semaphores.at[1]))
    for copy in copies:
        copy.start()
    for copy in copies[:-1]:
        copy.wait()
    weight = held[0] if held else near
    for n in range(0, total.shape[1], TILE):
        total[:, n : n + TILE] = jnp.dot(rows_here[...], weight[:, n : n + TILE], preferred_element_type=F32)
    copies[-1].wait()


def first_half(rows_here, near, far, near_held):
    return pl.pallas_call(
        first_half_kernel,
        out_shape=[pltpu.VMEM((rows_here.shape[0], near.shape[1]), F32), pltpu.VMEM(far.shape, far.dtype)],
        in_specs=[VMEM, VMEM if near_held else HBM, HBM],
        out_specs=[VMEM, VMEM],
        scratch_shapes=[pltpu.SemaphoreType.DMA((2,))] + [pltpu.VMEM(near.shape, near.dtype)] * (not near_held),
        compiler_params=LIMIT,
        cost_estimate=FREE,
        name="first_half",
    )(rows_here, in_vmem(near) if near_held else in_hbm(near), in_hbm(far))


def project_kernel(*refs, terms, begun, share, halves):
    lhs, rhs, start = refs[:terms], refs[terms : 2 * terms], refs[2 * terms : 2 * terms + begun]
    outs = refs[2 * terms + begun :]
    half = outs[0].shape[1]
    for n in range(0, half * halves, TILE):
        total = sum(
            jnp.dot(a[...], w[:, n : n + TILE], preferred_element_type=F32) for a, w in zip(lhs, rhs)
        )
        for s in start:
            total = total + s[:, n : n + TILE]
        for m in range(total.shape[0] // share):
            outs[m * halves + n // half][:, n % half : n % half + TILE] = total[m * share : (m + 1) * share].astype(BF16)


def project(lhs, rhs, start, share, halves):
    count, depth = lhs[0].shape
    width = rhs[0].shape[1]
    return pl.pallas_call(
        partial(project_kernel, terms=len(lhs), begun=len(start), share=share, halves=halves),
        out_shape=[jax.ShapeDtypeStruct((share, width // halves), BF16)] * (count // share * halves),
        in_specs=[VMEM] * (2 * len(lhs) + len(start)),
        out_specs=[VMEM] * (count // share * halves),
        compiler_params=LIMIT,
        cost_estimate=FREE,
        name="project",
    )(*lhs, *[in_vmem(w) for w in rhs], *[in_vmem(s) for s in start])


def on_device(queries, keys, values, doc_ids, block_mask, out_weight, *, order):
    groups, head_shards, slabs = (lax.axis_size(a) for a in ("srv", "head", "wsh"))
    z = lax.axis_index("wsh")
    columns_x = head_shards // 2
    block = queries.shape[0]
    heads = queries.shape[1] // HEAD_SIZE // slabs
    share = block // head_shards
    per_shard = slabs // head_shards
    staged = per_shard == 1
    stages = [[0], list(range(1, slabs))] if staged else [[0]]
    rows_at_once = share if staged else block
    halves = 2
    siblings = [(h, h ^ 1) for h in range(head_shards)]

    def around(array, k):
        return lax.ppermute(array, "wsh", [(i, (i + k) % slabs) for i in range(slabs)])

    packed = pack(
        queries,
        keys,
        values,
        slabs=slabs,
        heads=heads,
        kv_local=keys.shape[1] // HEAD_SIZE,
        order=order,
        share=rows_at_once,
        stages=stages,
    )
    loads = [packed[0]] + [around(packed[k], k) for k in range(1, slabs)]
    cuts = [loads[:1], loads[1:2], loads[2:]]
    before = []
    for cut in cuts:
        if cut:
            kv = joined([a[: 2 * block] for a in cut])
            kv = lax.ppermute(kv, "srv", [(g, g + 1) for g in range(groups - 1)])
            before += [kv[n * 2 * block : (n + 1) * 2 * block] for n in range(len(cut))]
    weight_sibling = lax.ppermute(out_weight, "head", siblings)
    stage_queries = [loads]
    for n in range(1, len(stages)):
        sent = [after(a, *loads) for a in packed[n * slabs : (n + 1) * slabs]]
        stage_queries.append([sent[0]] + [around(sent[k], k) for k in range(1, slabs)])

    reach = SLAB_REACH - 1
    padded = jnp.concatenate([jnp.full((reach, block), -1.0, F32), doc_ids.reshape(-1, block).astype(F32)])
    count = padded.shape[0] - reach
    key_doc = jnp.stack(
        [jnp.where(block_mask[:, reach - j, None] > 0, padded[j : j + count], -1.0) for j in range(SLAB_REACH)],
        axis=1,
    ).reshape(count, 1, SLAB_REACH * block)

    partials = []
    results = None
    for n, (stage, arrived) in enumerate(zip(stages, stage_queries)):
        if n:
            arrived = after(arrived, *results)
        keep, send, *fetched = attend(
            key_doc,
            loads,
            before,
            arrived,
            [out_weight] if n == 0 else [],
            slabs=slabs,
            heads=heads,
            share=rows_at_once,
            stage=stage,
            order=order,
            offset=2 * block if n == 0 else 0,
            columns_x=columns_x,
            per_shard=per_shard,
        )
        pieces = stage
        if not staged:
            pieces = range(slabs)
            keep, send = (
                jnp.concatenate(
                    [
                        lax.dynamic_slice_in_dim(
                            a.reshape(columns_x, -1, a.shape[-1]), chosen(order, z, i) * share, share, 1
                        )
                        for i in pieces
                    ],
                    axis=1,
                )
                for a in (keep, send)
            )
        theirs = lax.ppermute(send, "head", siblings)
        keep, theirs = (a.reshape(-1, a.shape[-1]) for a in (keep, theirs))
        if staged:
            near = fetched[0] if fetched else out_weight
            begun, far = first_half(keep, near, weight_sibling, bool(fetched))
            results = project([theirs], [far], [begun], share, halves)
        else:
            results = project([keep, theirs], [fetched[0], weight_sibling], [], share, halves)
        for m in range(len(pieces)):
            partials.append(
                [
                    [results[(k * len(pieces) + m) * halves + half] for half in range(halves)]
                    for k in range(columns_x)
                ]
            )

    position = np.argsort(order, axis=1)

    def senders(direction, t):
        found = {}
        for i in range(slabs):
            step = i if direction > 0 else slabs - 1 - i
            if step <= t:
                d = slabs - 1 - t + step
                found[i] = int(position[i, d if direction > 0 else slabs - 1 - d])
        return found

    def message(which, own, arrived):
        picked = None
        for i, piece in which.items():
            picked = own[piece] if picked is None else jnp.where(z == i, own[piece], picked)
        if arrived is None:
            return picked
        return (picked.astype(F32) + arrived.astype(F32)).astype(BF16)

    sums = [[] for _ in range(halves)]
    crossed = [None] * halves
    routes = [[(h, (h + 2 * k) % head_shards) for h in range(head_shards)] for k in range(columns_x)]
    arrived = [{1: None, -1: None} for _ in range(halves)]
    for t in range(slabs):
        for half in range(halves):
            pieces = [partials[t][k][half] for k in range(1, columns_x)]
            if t:
                pieces = [after(piece, *crossed[half]) for piece in pieces]
            crossed[half] = [lax.ppermute(a, "head", r) for a, r in zip(pieces, routes[1:])]
            total = sum(a.astype(F32) for a in [partials[t][0][half]] + crossed[half])
            sums[half].append(total.astype(BF16))
            if t == slabs - 1:
                continue
            up, down = senders(1, t), senders(-1, t)
            if t + 1 < slabs - 2 - t:
                sent = message({**up, **down}, sums[half], arrived[half][1])
                both = lax.ppermute(sent, "wsh", [(i, i + 1) for i in up] + [(i, i - 1) for i in down])
                arrived[half] = {1: both, -1: both}
            else:
                sent = {
                    direction: message(found, sums[half], arrived[half][direction])
                    for direction, found in ((1, up), (-1, down))
                }
                for direction, found in ((1, up), (-1, down)):
                    arrived[half][direction] = lax.ppermute(
                        sent[direction], "wsh", [(i, i + direction) for i in found]
                    )
    outs = []
    for half in range(halves):
        total = sums[half][-1].astype(F32)
        if slabs > 1:
            total = total + arrived[half][1].astype(F32) + arrived[half][-1].astype(F32)
        outs.append(total.astype(BF16))
    return jnp.concatenate(outs, axis=1)


def solution(mesh):
    in_specs = (
        P(("srv", "wsh"), "head"),
        P(("srv", "wsh"), "head"),
        P(("srv", "wsh"), "head"),
        P(),
        P(),
        P(("head", "wsh"), None),
    )
    out_specs = P(("srv", "head", "wsh"), None)
    return jax.shard_map(
        partial(on_device, order=destination_order(mesh.shape["wsh"])),
        mesh=mesh,
        in_specs=in_specs,
        out_specs=out_specs,
        check_vma=False,
    )
```

```python
from functools import partial
import math

import jax
import jax.numpy as jnp
import numpy as np
from jax import lax
from jax.experimental import pallas as pl
from jax.experimental.pallas import tpu as pltpu
from jax.sharding import PartitionSpec as P

QUERY_HEAD_COUNT = 64
KEY_VALUE_HEADS = 8
HEAD_SIZE = 128
SLAB_REACH = 4

MASKED = -1e30
F32 = jnp.float32
BF16 = jnp.bfloat16
VMEM = pl.BlockSpec(memory_space=pltpu.VMEM)
SMEM = pl.BlockSpec(memory_space=pltpu.SMEM)
HBM = pl.BlockSpec(memory_space=pltpu.HBM)
LIMIT = pltpu.CompilerParams(vmem_limit_bytes=18 << 20)
TILE = 1024
FREE = pl.CostEstimate(flops=0, bytes_accessed=0, transcendentals=0)


def destination_order(count):
    table = []
    for z in range(count):
        due = {d: (count - 1 - d + z if d > z else count - 1 - z + d) for d in range(count)}
        due[z] = count
        table.append(sorted(range(count), key=lambda d: (due[d], -d if z < count // 2 else d)))
    return np.array(table, np.int32)


def in_vmem(array):
    return pltpu.with_memory_space_constraint(array, pltpu.VMEM)


def in_hbm(array):
    return pltpu.with_memory_space_constraint(array, pltpu.HBM)


def after(value, *others):
    return lax.optimization_barrier((value, others))[0]


def chosen(table, z, i):
    picked = jnp.int32(int(table[0, i]))
    for n in range(1, table.shape[0]):
        picked = jnp.where(z == n, jnp.int32(int(table[n, i])), picked)
    return picked


def joined(parts):
    return parts[0] if len(parts) == 1 else jnp.concatenate(parts, axis=0)


def pack_kernel(queries, keys, values, *refs, slabs, heads, kv_local, order, share, stages):
    *outs, all_queries, all_keys, all_values, semaphores = refs
    z = lax.axis_index("wsh")
    pairs = ((keys, all_keys), (values, all_values), (queries, all_queries))
    copies = [pltpu.make_async_copy(a, b, semaphores.at[n]) for n, (a, b) in enumerate(pairs)]
    for copy in copies:
        copy.start()
    block = queries.shape[0]
    targets = [lax.rem(z + k, slabs) for k in range(slabs)]
    for n in range(2):
        copies[n].wait()
        for k, target in enumerate(targets):
            first = pl.multiple_of(lax.div(target * kv_local, slabs) * HEAD_SIZE, HEAD_SIZE)
            outs[k][n * block : (n + 1) * block, :] = pairs[n][1][:, pl.ds(first, HEAD_SIZE)]
    copies[2].wait()
    for n, stage in enumerate(stages):
        for k, target in enumerate(targets):
            place = 2 * block if n == 0 else 0
            for h in range(heads):
                column = pl.multiple_of((target * heads + h) * HEAD_SIZE, HEAD_SIZE)
                for i in stage:
                    if share == block:
                        rows, count = slice(None), block
                    else:
                        rows, count = pl.ds(pl.multiple_of(chosen(order, target, i) * share, 16), share), share
                    outs[n * slabs + k][place : place + count, :] = all_queries[rows, pl.ds(column, HEAD_SIZE)]
                    place += count


def pack(queries, keys, values, *, slabs, heads, kv_local, order, share, stages):
    block = queries.shape[0]
    counts = [heads * share * len(stage) + (2 * block if n == 0 else 0) for n, stage in enumerate(stages)]
    return pl.pallas_call(
        partial(
            pack_kernel, slabs=slabs, heads=heads, kv_local=kv_local, order=order, share=share, stages=stages
        ),
        out_shape=[jax.ShapeDtypeStruct((count, HEAD_SIZE), BF16) for count in counts for _ in range(slabs)],
        in_specs=[HBM] * 3,
        out_specs=[VMEM] * (slabs * len(counts)),
        scratch_shapes=[pltpu.VMEM(a.shape, BF16) for a in (queries, keys, values)]
        + [pltpu.SemaphoreType.DMA((3,))],
        compiler_params=LIMIT,
        cost_estimate=FREE,
        name="pack",
    )(in_hbm(queries), in_hbm(keys), in_hbm(values))


def attend_kernel(key_doc, *refs, slabs, heads, share, stage, order, offset, columns_x, per_shard, fetched):
    refs = list(refs)
    take = lambda n: [refs.pop(0) for _ in range(n)]
    now, before, queries, weights = take(slabs), take(slabs), take(slabs), take(fetched)
    (keep, send), copied = take(2), take(fetched)
    key_rows, value_rows = take(2)
    copies = [pltpu.make_async_copy(w, c, refs[0].at[n]) for n, (w, c) in enumerate(zip(weights, copied))]
    for copy in copies:
        copy.start()
    scale = math.log2(math.e) / math.sqrt(HEAD_SIZE)
    span = key_doc.shape[2]
    block = span // SLAB_REACH
    rows = share * len(stage)
    srv, head, z = (lax.axis_index(a) for a in ("srv", "head", "wsh"))
    core, x = lax.rem(head, 2), lax.div(head, 2)
    column = lax.broadcasted_iota(jnp.int32, (share, span), 1) - (SLAB_REACH - 1) * block
    row = lax.broadcasted_iota(jnp.int32, (share, span), 0)
    behind = [column - row - (0 if share == block else chosen(order, z, i) * share) for i in stage]
    causal = joined([b <= 0 for b in behind])
    for k in range(slabs):
        slab = lax.rem(z - k + slabs, slabs)
        for o in range(SLAB_REACH):
            place = slice((SLAB_REACH - 1 - o) * block, (SLAB_REACH - o) * block)
            held = (k + o) % slabs

            def fill(source):
                key_rows[place, :] = source[:block, :]
                value_rows[place, :] = source[block : 2 * block, :]

            if o == 0:
                fill(now[held])
            else:
                pl.when(slab >= o)(partial(fill, now[held]))
                pl.when(slab < o)(partial(fill, before[held]))
        docs = key_doc[srv * slabs + slab]
        query_doc = joined([jnp.max(jnp.where(b == 0, docs, -2.0), axis=1, keepdims=True) for b in behind])
        visible = causal & (query_doc == docs)
        scores = lax.dot_general(
            queries[k][offset : offset + heads * rows, :],
            key_rows[...],
            (((1,), (1,)), ((), ())),
            preferred_element_type=F32,
        ).reshape(heads, rows, span)
        scores = jnp.where(visible[None], scores, MASKED)
        largest = jnp.max(scores, axis=-1, keepdims=True)
        terms = jnp.exp2((scores - largest) * scale)
        normalizer = jnp.sum(terms, axis=-1, keepdims=True)
        weighted = jnp.dot(
            terms.reshape(heads * rows, span).astype(BF16), value_rows[...], preferred_element_type=F32
        ).reshape(heads, rows, HEAD_SIZE)
        result = (weighted / normalizer).astype(BF16)
        result = jnp.concatenate([result[h] for h in range(heads)], axis=1)
        target = lax.div(slab, per_shard)
        slot = lax.rem(lax.div(target, 2) - x + columns_x, columns_x) * per_shard + lax.rem(slab, per_shard)

        @pl.when(lax.rem(target, 2) == core)
        def _():
            keep[slot] = result

        @pl.when(lax.rem(target, 2) != core)
        def _():
            send[slot] = result

    for copy in copies:
        copy.wait()


def attend(key_doc, now, before, queries, weights, *, slabs, heads, share, stage, **rest):
    span = key_doc.shape[2]
    rows = share * len(stage)
    out = jax.ShapeDtypeStruct((slabs // 2, rows, heads * HEAD_SIZE), BF16)
    terms = slabs * rows * span * heads
    fetched = len(weights)
    return pl.pallas_call(
        partial(
            attend_kernel, slabs=slabs, heads=heads, share=share, stage=stage, fetched=fetched, **rest
        ),
        out_shape=[out, out] + [pltpu.VMEM(w.shape, w.dtype) for w in weights],
        in_specs=[VMEM] * (1 + 3 * slabs) + [HBM] * fetched,
        out_specs=[VMEM] * (2 + fetched),
        scratch_shapes=[pltpu.VMEM((span, HEAD_SIZE), BF16)] * 2
        + [pltpu.SemaphoreType.DMA((fetched,))] * (fetched > 0),
        compiler_params=LIMIT,
        cost_estimate=pl.CostEstimate(flops=4 * terms * HEAD_SIZE, bytes_accessed=0, transcendentals=terms),
        name="attend",
    )(key_doc, *now, *before, *queries, *[in_hbm(w) for w in weights])


def first_half_kernel(rows_here, near, far, total, far_held, semaphores, *held):
    copies = [pltpu.make_async_copy(far, far_held, semaphores.at[0])]
    for near_held in held:
        copies.insert(0, pltpu.make_async_copy(near, near_held, semaphores.at[1]))
    for copy in copies:
        copy.start()
    for copy in copies[:-1]:
        copy.wait()
    weight = held[0] if held else near
    for n in range(0, total.shape[1], TILE):
        total[:, n : n + TILE] = jnp.dot(rows_here[...], weight[:, n : n + TILE], preferred_element_type=F32)
    copies[-1].wait()


def first_half(rows_here, near, far, near_held):
    return pl.pallas_call(
        first_half_kernel,
        out_shape=[pltpu.VMEM((rows_here.shape[0], near.shape[1]), F32), pltpu.VMEM(far.shape, far.dtype)],
        in_specs=[VMEM, VMEM if near_held else HBM, HBM],
        out_specs=[VMEM, VMEM],
        scratch_shapes=[pltpu.SemaphoreType.DMA((2,))] + [pltpu.VMEM(near.shape, near.dtype)] * (not near_held),
        compiler_params=LIMIT,
        cost_estimate=FREE,
        name="first_half",
    )(rows_here, in_vmem(near) if near_held else in_hbm(near), in_hbm(far))


def project_kernel(*refs, terms, begun, share, halves):
    lhs, rhs, start = refs[:terms], refs[terms : 2 * terms], refs[2 * terms : 2 * terms + begun]
    outs = refs[2 * terms + begun :]
    half = outs[0].shape[1]
    for n in range(0, half * halves, TILE):
        total = sum(
            jnp.dot(a[...], w[:, n : n + TILE], preferred_element_type=F32) for a, w in zip(lhs, rhs)
        )
        for s in start:
            total = total + s[:, n : n + TILE]
        for m in range(total.shape[0] // share):
            outs[m * halves + n // half][:, n % half : n % half + TILE] = total[m * share : (m + 1) * share].astype(BF16)


def project(lhs, rhs, start, share, halves):
    count, depth = lhs[0].shape
    width = rhs[0].shape[1]
    return pl.pallas_call(
        partial(project_kernel, terms=len(lhs), begun=len(start), share=share, halves=halves),
        out_shape=[jax.ShapeDtypeStruct((share, width // halves), BF16)] * (count // share * halves),
        in_specs=[VMEM] * (2 * len(lhs) + len(start)),
        out_specs=[VMEM] * (count // share * halves),
        compiler_params=LIMIT,
        cost_estimate=FREE,
        name="project",
    )(*lhs, *[in_vmem(w) for w in rhs], *[in_vmem(s) for s in start])


def on_device(queries, keys, values, doc_ids, block_mask, out_weight, *, order):
    groups, head_shards, slabs = (lax.axis_size(a) for a in ("srv", "head", "wsh"))
    z = lax.axis_index("wsh")
    columns_x = head_shards // 2
    block = queries.shape[0]
    heads = queries.shape[1] // HEAD_SIZE // slabs
    share = block // head_shards
    per_shard = slabs // head_shards
    staged = per_shard == 1
    stages = [[0], list(range(1, slabs))] if staged else [[0]]
    rows_at_once = share if staged else block
    halves = 2
    siblings = [(h, h ^ 1) for h in range(head_shards)]

    def around(array, k):
        return lax.ppermute(array, "wsh", [(i, (i + k) % slabs) for i in range(slabs)])

    packed = pack(
        queries,
        keys,
        values,
        slabs=slabs,
        heads=heads,
        kv_local=keys.shape[1] // HEAD_SIZE,
        order=order,
        share=rows_at_once,
        stages=stages,
    )
    loads = [packed[0]] + [around(packed[k], k) for k in range(1, slabs)]
    before = [
        lax.ppermute(a[: 2 * block], "srv", [(g, g + 1) for g in range(groups - 1)]) for a in loads
    ]
    weight_sibling = lax.ppermute(out_weight, "head", siblings)
    stage_queries = [loads]
    for n in range(1, len(stages)):
        sent = packed[n * slabs : (n + 1) * slabs]
        stage_queries.append(
            [sent[0]] + [around(after(sent[k], *loads, before[k - 1]), k) for k in range(1, slabs)]
        )

    reach = SLAB_REACH - 1
    padded = jnp.concatenate([jnp.full((reach, block), -1.0, F32), doc_ids.reshape(-1, block).astype(F32)])
    count = padded.shape[0] - reach
    key_doc = jnp.stack(
        [jnp.where(block_mask[:, reach - j, None] > 0, padded[j : j + count], -1.0) for j in range(SLAB_REACH)],
        axis=1,
    ).reshape(count, 1, SLAB_REACH * block)

    partials = []
    results = None
    for n, (stage, arrived) in enumerate(zip(stages, stage_queries)):
        if n:
            arrived = after(arrived, *results)
        keep, send, *fetched = attend(
            key_doc,
            loads,
            before,
            arrived,
            [out_weight] if n == 0 else [],
            slabs=slabs,
            heads=heads,
            share=rows_at_once,
            stage=stage,
            order=order,
            offset=2 * block if n == 0 else 0,
            columns_x=columns_x,
            per_shard=per_shard,
        )
        pieces = stage
        if not staged:
            pieces = range(slabs)
            keep, send = (
                jnp.concatenate(
                    [
                        lax.dynamic_slice_in_dim(
                            a.reshape(columns_x, -1, a.shape[-1]), chosen(order, z, i) * share, share, 1
                        )
                        for i in pieces
                    ],
                    axis=1,
                )
                for a in (keep, send)
            )
        theirs = lax.ppermute(send, "head", siblings)
        keep, theirs = (a.reshape(-1, a.shape[-1]) for a in (keep, theirs))
        if staged:
            near = fetched[0] if fetched else out_weight
            begun, far = first_half(keep, near, weight_sibling, bool(fetched))
            results = project([theirs], [far], [begun], share, halves)
        else:
            results = project([keep, theirs], [fetched[0], weight_sibling], [], share, halves)
        for m in range(len(pieces)):
            partials.append(
                [
                    [results[(k * len(pieces) + m) * halves + half] for half in range(halves)]
                    for k in range(columns_x)
                ]
            )

    position = np.argsort(order, axis=1)
    middle = slabs // 2 - 1

    def inward(c):
        return [(c, c + 1), (slabs - 1 - c, slabs - 2 - c)]

    def outward(c):
        return [(b, a) for a, b in inward(c)]

    sums = [[] for _ in range(halves)]
    crossed = [None] * halves
    routes = [[(h, (h + 2 * k) % head_shards) for h in range(head_shards)] for k in range(columns_x)]
    passed = [{} for _ in range(halves)]
    for t in range(slabs):
        for half in range(halves):
            pieces = [partials[t][k][half] for k in range(1, columns_x)]
            if t:
                pieces = [after(piece, *crossed[half]) for piece in pieces]
            crossed[half] = [lax.ppermute(a, "head", r) for a, r in zip(pieces, routes[1:])]
            total = sum(a.astype(F32) for a in [partials[t][0][half]] + crossed[half])
            sums[half].append(total.astype(BF16))
            if t == slabs - 1:
                continue
            now = {}
            for c in range(min(t, middle) + 1):
                message = sums[half][position[c, slabs - 1 - t + c]]
                if c:
                    message = (message.astype(F32) + passed[half][c - 1].astype(F32)).astype(BF16)
                route = inward(c)
                if c < middle and t >= slabs - 2 - c:
                    z_out = slabs - 2 - c
                    back = sums[half][position[z_out, slabs - 1 - t + z_out]]
                    back = (back.astype(F32) + passed[half][c + 1].astype(F32)).astype(BF16)
                    message = jnp.where((z == c) | (z == slabs - 1 - c), message, back)
                    route = route + outward(c)
                now[c] = lax.ppermute(message, "wsh", route)
            passed[half] = now
    outs = []
    for half in range(halves):
        total = sums[half][-1].astype(F32)
        for a in passed[half].values():
            total = total + a.astype(F32)
        outs.append(total.astype(BF16))
    return jnp.concatenate(outs, axis=1)


def solution(mesh):
    in_specs = (
        P(("srv", "wsh"), "head"),
        P(("srv", "wsh"), "head"),
        P(("srv", "wsh"), "head"),
        P(),
        P(),
        P(("head", "wsh"), None),
    )
    out_specs = P(("srv", "head", "wsh"), None)
    return jax.shard_map(
        partial(on_device, order=destination_order(mesh.shape["wsh"])),
        mesh=mesh,
        in_specs=in_specs,
        out_specs=out_specs,
        check_vma=False,
    )
```

```python
from functools import partial
import math

import jax
import jax.numpy as jnp
import numpy as np
from jax import lax
from jax.experimental import pallas as pl
from jax.experimental.pallas import tpu as pltpu
from jax.sharding import PartitionSpec as P

QUERY_HEAD_COUNT = 64
KEY_VALUE_HEADS = 8
HEAD_SIZE = 128
SLAB_REACH = 4

MASKED = -1e30
F32 = jnp.float32
BF16 = jnp.bfloat16
VMEM = pl.BlockSpec(memory_space=pltpu.VMEM)
SMEM = pl.BlockSpec(memory_space=pltpu.SMEM)
HBM = pl.BlockSpec(memory_space=pltpu.HBM)
LIMIT = pltpu.CompilerParams(vmem_limit_bytes=18 << 20)
TILE = 1024
HALVES = 2
UNDER_WAY = 2
ATTEND_US = {0: 1.0, 1: 0.84, 2: 1.05}
FIRST_HALF_US = {True: 1.02, False: 1.74}
PROJECT_US = {1: 0.45, 2: 0.45}
FREE = pl.CostEstimate(flops=0, bytes_accessed=0, transcendentals=0)


def worth(us):
    return pl.CostEstimate(flops=int(us * 1.15e9), bytes_accessed=0, transcendentals=0)


def destination_order(count):
    table = []
    for z in range(count):
        due = {d: (count - 1 - d + z if d > z else count - 1 - z + d) for d in range(count)}
        due[z] = count
        table.append(sorted(range(count), key=lambda d: (due[d], -d if z < count // 2 else d)))
    return np.array(table, np.int32)


def in_vmem(array):
    return pltpu.with_memory_space_constraint(array, pltpu.VMEM)


def in_hbm(array):
    return pltpu.with_memory_space_constraint(array, pltpu.HBM)


def after(value, *others):
    return lax.optimization_barrier((value, others))[0]


def chosen(table, z, i):
    picked = jnp.int32(int(table[0, i]))
    for n in range(1, table.shape[0]):
        picked = jnp.where(z == n, jnp.int32(int(table[n, i])), picked)
    return picked


def joined(parts):
    return parts[0] if len(parts) == 1 else jnp.concatenate(parts, axis=0)


def pack_kernel(queries, keys, values, *refs, slabs, heads, kv_local, order, share, stages):
    *outs, all_queries, all_keys, all_values, semaphores = refs
    z = lax.axis_index("wsh")
    pairs = ((keys, all_keys), (values, all_values), (queries, all_queries))
    copies = [pltpu.make_async_copy(a, b, semaphores.at[n]) for n, (a, b) in enumerate(pairs)]
    for copy in copies:
        copy.start()
    block = queries.shape[0]
    targets = [lax.rem(z + k, slabs) for k in range(slabs)]
    for n in range(2):
        copies[n].wait()
        for k, target in enumerate(targets):
            first = pl.multiple_of(lax.div(target * kv_local, slabs) * HEAD_SIZE, HEAD_SIZE)
            outs[k][n * block : (n + 1) * block, :] = pairs[n][1][:, pl.ds(first, HEAD_SIZE)]
    copies[2].wait()
    for n, stage in enumerate(stages):
        for k, target in enumerate(targets):
            place = 2 * block if n == 0 else 0
            for h in range(heads):
                column = pl.multiple_of((target * heads + h) * HEAD_SIZE, HEAD_SIZE)
                for i in stage:
                    if share == block:
                        rows, count = slice(None), block
                    else:
                        rows, count = pl.ds(pl.multiple_of(chosen(order, target, i) * share, 16), share), share
                    outs[n * slabs + k][place : place + count, :] = all_queries[rows, pl.ds(column, HEAD_SIZE)]
                    place += count


def pack(queries, keys, values, *, slabs, heads, kv_local, order, share, stages):
    block = queries.shape[0]
    counts = [heads * share * len(stage) + (2 * block if n == 0 else 0) for n, stage in enumerate(stages)]
    return pl.pallas_call(
        partial(
            pack_kernel, slabs=slabs, heads=heads, kv_local=kv_local, order=order, share=share, stages=stages
        ),
        out_shape=[jax.ShapeDtypeStruct((count, HEAD_SIZE), BF16) for count in counts for _ in range(slabs)],
        in_specs=[HBM] * 3,
        out_specs=[VMEM] * (slabs * len(counts)),
        scratch_shapes=[pltpu.VMEM(a.shape, BF16) for a in (queries, keys, values)]
        + [pltpu.SemaphoreType.DMA((3,))],
        compiler_params=LIMIT,
        cost_estimate=FREE,
        name="pack",
    )(in_hbm(queries), in_hbm(keys), in_hbm(values))


def attend_kernel(key_doc, *refs, slabs, heads, share, stage, stages, order, offset, columns_x, per_shard, fetched):
    refs = list(refs)
    take = lambda n: [refs.pop(0) for _ in range(n)]
    now, before, queries, weights = take(slabs), take(slabs), take(slabs), take(fetched)
    (keep, send), copied = take(2), take(fetched)
    key_rows, value_rows = take(2)
    copies = [pltpu.make_async_copy(w, c, refs[0].at[n]) for n, (w, c) in enumerate(zip(weights, copied))]
    for copy in copies:
        copy.start()
    scale = math.log2(math.e) / math.sqrt(HEAD_SIZE)
    span = key_doc.shape[2]
    block = span // SLAB_REACH
    rows = share * len(stage)
    srv, head, z = (lax.axis_index(a) for a in ("srv", "head", "wsh"))
    core, x = lax.rem(head, 2), lax.div(head, 2)
    column = lax.broadcasted_iota(jnp.int32, (share, span), 1) - (SLAB_REACH - 1) * block
    row = lax.broadcasted_iota(jnp.int32, (share, span), 0)
    behind = [column - row - (0 if share == block else chosen(order, z, i) * share) for i in stage]
    causal = joined([b <= 0 for b in behind])
    places = [offset + (h * len(stages) + stages.index(stage[0])) * share for h in range(heads)]
    for k in range(slabs):
        slab = lax.rem(z - k + slabs, slabs)
        for o in range(SLAB_REACH):
            place = slice((SLAB_REACH - 1 - o) * block, (SLAB_REACH - o) * block)
            held = (k + o) % slabs

            def fill(source):
                key_rows[place, :] = source[:block, :]
                value_rows[place, :] = source[block : 2 * block, :]

            if o == 0:
                fill(now[held])
            else:
                pl.when(slab >= o)(partial(fill, now[held]))
                pl.when(slab < o)(partial(fill, before[held]))
        docs = key_doc[srv * slabs + slab]
        query_doc = joined([jnp.max(jnp.where(b == 0, docs, -2.0), axis=1, keepdims=True) for b in behind])
        visible = causal & (query_doc == docs)
        scores = lax.dot_general(
            joined([queries[k][start : start + rows, :] for start in places]),
            key_rows[...],
            (((1,), (1,)), ((), ())),
            preferred_element_type=F32,
        ).reshape(heads, rows, span)
        scores = jnp.where(visible[None], scores, MASKED)
        largest = jnp.max(scores, axis=-1, keepdims=True)
        terms = jnp.exp2((scores - largest) * scale)
        normalizer = jnp.sum(terms, axis=-1, keepdims=True)
        weighted = jnp.dot(
            terms.reshape(heads * rows, span).astype(BF16), value_rows[...], preferred_element_type=F32
        ).reshape(heads, rows, HEAD_SIZE)
        result = (weighted / normalizer).astype(BF16)
        result = jnp.concatenate([result[h] for h in range(heads)], axis=1)
        target = lax.div(slab, per_shard)
        slot = lax.rem(lax.div(target, 2) - x + columns_x, columns_x) * per_shard + lax.rem(slab, per_shard)

        @pl.when(lax.rem(target, 2) == core)
        def _():
            keep[slot] = result

        @pl.when(lax.rem(target, 2) != core)
        def _():
            send[slot] = result

    for copy in copies:
        copy.wait()


def attend(key_doc, now, before, queries, weights, *, slabs, heads, share, stage, **rest):
    span = key_doc.shape[2]
    rows = share * len(stage)
    out = jax.ShapeDtypeStruct((slabs // 2, rows, heads * HEAD_SIZE), BF16)
    terms = slabs * rows * span * heads
    fetched = len(weights)
    return pl.pallas_call(
        partial(
            attend_kernel, slabs=slabs, heads=heads, share=share, stage=stage, fetched=fetched, **rest
        ),
        out_shape=[out, out] + [pltpu.VMEM(w.shape, w.dtype) for w in weights],
        in_specs=[VMEM] * (1 + 3 * slabs) + [HBM] * fetched,
        out_specs=[VMEM] * (2 + fetched),
        scratch_shapes=[pltpu.VMEM((span, HEAD_SIZE), BF16)] * 2
        + [pltpu.SemaphoreType.DMA((fetched,))] * (fetched > 0),
        compiler_params=LIMIT,
        cost_estimate=worth(ATTEND_US[0 if stage[0] == 0 else min(len(stage), 2)]),
        name="attend",
    )(key_doc, *now, *before, *queries, *[in_hbm(w) for w in weights])


def first_half_kernel(rows_here, near, far, total, far_held, semaphores, *held):
    copies = [pltpu.make_async_copy(far, far_held, semaphores.at[0])]
    for near_held in held:
        copies.insert(0, pltpu.make_async_copy(near, near_held, semaphores.at[1]))
    for copy in copies:
        copy.start()
    for copy in copies[:-1]:
        copy.wait()
    weight = held[0] if held else near
    for n in range(0, total.shape[1], TILE):
        total[:, n : n + TILE] = jnp.dot(rows_here[...], weight[:, n : n + TILE], preferred_element_type=F32)
    copies[-1].wait()


def first_half(rows_here, near, far, near_held):
    return pl.pallas_call(
        first_half_kernel,
        out_shape=[pltpu.VMEM((rows_here.shape[0], near.shape[1]), F32), pltpu.VMEM(far.shape, far.dtype)],
        in_specs=[VMEM, VMEM if near_held else HBM, HBM],
        out_specs=[VMEM, VMEM],
        scratch_shapes=[pltpu.SemaphoreType.DMA((2,))] + [pltpu.VMEM(near.shape, near.dtype)] * (not near_held),
        compiler_params=LIMIT,
        cost_estimate=worth(FIRST_HALF_US[near_held]),
        name="first_half",
    )(rows_here, in_vmem(near) if near_held else in_hbm(near), in_hbm(far))


def project_kernel(*refs, terms, begun, share, splits, columns_x):
    lhs, rhs, start = refs[:terms], refs[terms : 2 * terms], refs[2 * terms : 2 * terms + begun]
    outs = refs[2 * terms + begun :]
    width = rhs[0].shape[1]
    for n in range(0, width, TILE):
        total = sum(
            jnp.dot(a[...], w[:, n : n + TILE], preferred_element_type=F32) for a, w in zip(lhs, rhs)
        )
        for s in start:
            total = total + s[:, n : n + TILE]
        place = 0
        for i, split in enumerate(splits):
            part = width // split
            for k in range(columns_x):
                row = (k * len(splits) + i) * share
                out = outs[place + k * split + n // part]
                out[:, n % part : n % part + TILE] = total[row : row + share].astype(BF16)
            place += columns_x * split


def project(lhs, rhs, start, share, splits):
    width = rhs[0].shape[1]
    columns_x = lhs[0].shape[0] // (share * len(splits))
    shapes = [
        jax.ShapeDtypeStruct((share, width // split), BF16) for split in splits for _ in range(columns_x * split)
    ]
    results = pl.pallas_call(
        partial(
            project_kernel, terms=len(lhs), begun=len(start), share=share, splits=splits, columns_x=columns_x
        ),
        out_shape=shapes,
        in_specs=[VMEM] * (2 * len(lhs) + len(start)),
        out_specs=[VMEM] * len(shapes),
        compiler_params=LIMIT,
        cost_estimate=worth(PROJECT_US[min(len(splits), 2)]),
        name="project",
    )(*lhs, *[in_vmem(w) for w in rhs], *[in_vmem(s) for s in start])
    pieces = []
    for split in splits:
        pieces.append([results[k * split : (k + 1) * split] for k in range(columns_x)])
        results = results[columns_x * split :]
    return pieces


def on_device(queries, keys, values, doc_ids, block_mask, out_weight, *, order):
    groups, head_shards, slabs = (lax.axis_size(a) for a in ("srv", "head", "wsh"))
    z = lax.axis_index("wsh")
    columns_x = head_shards // 2
    block = queries.shape[0]
    heads = queries.shape[1] // HEAD_SIZE // slabs
    share = block // head_shards
    per_shard = slabs // head_shards
    staged = per_shard == 1
    stages = [[0], list(range(1, slabs))] if staged else [[0]]
    rounds = [[0], list(range(1, slabs - 1)), [slabs - 1]] if staged and slabs > 2 else stages
    rows_at_once = share if staged else block
    siblings = [(h, h ^ 1) for h in range(head_shards)]

    def around(array, k):
        return lax.ppermute(array, "wsh", [(i, (i + k) % slabs) for i in range(slabs)])

    packed = pack(
        queries,
        keys,
        values,
        slabs=slabs,
        heads=heads,
        kv_local=keys.shape[1] // HEAD_SIZE,
        order=order,
        share=rows_at_once,
        stages=stages,
    )
    loads = [packed[0]] + [around(packed[k], k) for k in range(1, slabs)]
    before = [
        lax.ppermute(a[: 2 * block], "srv", [(g, g + 1) for g in range(groups - 1)]) for a in loads
    ]
    weight_sibling = lax.ppermute(out_weight, "head", siblings)
    stage_queries = [loads]
    for n in range(1, len(stages)):
        sent = packed[n * slabs : (n + 1) * slabs]
        stage_queries.append(
            [sent[0]] + [around(after(sent[k], *loads, before[k - 1]), k) for k in range(1, slabs)]
        )

    reach = SLAB_REACH - 1
    padded = jnp.concatenate([jnp.full((reach, block), -1.0, F32), doc_ids.reshape(-1, block).astype(F32)])
    count = padded.shape[0] - reach
    key_doc = jnp.stack(
        [jnp.where(block_mask[:, reach - j, None] > 0, padded[j : j + count], -1.0) for j in range(SLAB_REACH)],
        axis=1,
    ).reshape(count, 1, SLAB_REACH * block)

    position = np.argsort(order, axis=1)
    middle = slabs // 2 - 1

    def inward(c):
        return [(c, c + 1), (slabs - 1 - c, slabs - 2 - c)]

    def outward(c):
        return [(b, a) for a, b in inward(c)]

    def add(*terms):
        return sum(a.astype(F32) for a in terms).astype(BF16)

    routes = [[(h, (h + 2 * k) % head_shards) for h in range(head_shards)] for k in range(columns_x)]
    sums, crossed, sent = [], [], []

    def cross(t):
        own, *others = partials[t]
        total = [None] * HALVES
        for n in range(HALVES):
            pieces = [other[n] for other in others]
            if len(crossed) >= UNDER_WAY:
                pieces = [after(piece, *crossed[-UNDER_WAY]) for piece in pieces]
            crossed.append([lax.ppermute(a, "head", r) for a, r in zip(pieces, routes[1:])])
            total[n] = add(own[n], *crossed[-1])
        sums.append(total)

    def step(t):
        passed = sent[-1] if sent else {}
        now = {}
        for n in range(HALVES):
            for c in range(min(t, middle) + 1):
                message = sums[position[c, slabs - 1 - t + c]][n]
                if c:
                    message = add(message, passed[c - 1][n])
                route = inward(c)
                if c < middle and t >= slabs - 2 - c:
                    z_out = slabs - 2 - c
                    back = add(sums[position[z_out, slabs - 1 - t + z_out]][n], passed[c + 1][n])
                    message = jnp.where((z == c) | (z == slabs - 1 - c), message, back)
                    route = route + outward(c)
                now.setdefault(c, {})[n] = lax.ppermute(message, "wsh", route)
        sent.append(now)

    partials = []
    results = None
    for n, stage in enumerate(rounds):
        payload = 0 if n == 0 else 1
        arrived = stage_queries[payload]
        if n:
            arrived = after(arrived, *results[0][0])
        if n > 1:
            arrived = after(arrived, *crossed[HALVES - 1])
        keep, send, *fetched = attend(
            key_doc,
            loads,
            before,
            arrived,
            [out_weight] if n == 0 else [],
            slabs=slabs,
            heads=heads,
            share=rows_at_once,
            stage=stage,
            order=order,
            offset=2 * block if n == 0 else 0,
            stages=stages[payload],
            columns_x=columns_x,
            per_shard=per_shard,
        )
        pieces = stage
        if not staged:
            pieces = range(slabs)
            keep, send = (
                jnp.concatenate(
                    [
                        lax.dynamic_slice_in_dim(
                            a.reshape(columns_x, -1, a.shape[-1]), chosen(order, z, i) * share, share, 1
                        )
                        for i in pieces
                    ],
                    axis=1,
                )
                for a in (keep, send)
            )
        theirs = lax.ppermute(send, "head", siblings)
        keep, theirs = (a.reshape(-1, a.shape[-1]) for a in (keep, theirs))
        splits = [HALVES] * len(pieces)
        if staged:
            near = fetched[0] if fetched else out_weight
            begun, far = first_half(keep, near, weight_sibling, bool(fetched))
            results = project([theirs], [far], [begun], share, splits)
        else:
            results = project([keep, theirs], [fetched[0], weight_sibling], [], share, splits)
        partials += results
        for t in range(len(sums), len(partials)):
            cross(t)
            if t < slabs - 1:
                step(t)

    outs = []
    for n in range(HALVES):
        outs.append(add(sums[-1][n], *[a[n] for a in (sent[-1] if sent else {}).values()]))
    return jnp.concatenate(outs, axis=1)


def solution(mesh):
    in_specs = (
        P(("srv", "wsh"), "head"),
        P(("srv", "wsh"), "head"),
        P(("srv", "wsh"), "head"),
        P(),
        P(),
        P(("head", "wsh"), None),
    )
    out_specs = P(("srv", "head", "wsh"), None)
    return jax.shard_map(
        partial(on_device, order=destination_order(mesh.shape["wsh"])),
        mesh=mesh,
        in_specs=in_specs,
        out_specs=out_specs,
        check_vma=False,
    )
```

```python
from functools import partial
import math

import jax
import jax.numpy as jnp
import numpy as np
from jax import lax
from jax.experimental import pallas as pl
from jax.experimental.pallas import tpu as pltpu
from jax.sharding import PartitionSpec as P

QUERY_HEAD_COUNT = 64
KEY_VALUE_HEADS = 8
HEAD_SIZE = 128
SLAB_REACH = 4

MASKED = -1e30
F32 = jnp.float32
BF16 = jnp.bfloat16
VMEM = pl.BlockSpec(memory_space=pltpu.VMEM)
SMEM = pl.BlockSpec(memory_space=pltpu.SMEM)
HBM = pl.BlockSpec(memory_space=pltpu.HBM)
LIMIT = pltpu.CompilerParams(vmem_limit_bytes=18 << 20)
TILE = 1024
HALVES = 2
UNDER_WAY = 2
ATTEND_US = {0: 1.0, 1: 0.84, 2: 1.05}
FIRST_HALF_US = {True: 1.02, False: 1.74}
PROJECT_US = {1: 0.45, 2: 0.45}
FREE = pl.CostEstimate(flops=0, bytes_accessed=0, transcendentals=0)


def worth(us):
    return pl.CostEstimate(flops=int(us * 1.15e9), bytes_accessed=0, transcendentals=0)


def destination_order(count):
    table = []
    for z in range(count):
        due = {d: (count - 1 - d + z if d > z else count - 1 - z + d) for d in range(count)}
        due[z] = count
        table.append(sorted(range(count), key=lambda d: (due[d], -d if z < count // 2 else d)))
    return np.array(table, np.int32)


def in_vmem(array):
    return pltpu.with_memory_space_constraint(array, pltpu.VMEM)


def in_hbm(array):
    return pltpu.with_memory_space_constraint(array, pltpu.HBM)


def after(value, *others):
    return lax.optimization_barrier((value, others))[0]


def chosen(table, z, i):
    picked = jnp.int32(int(table[0, i]))
    for n in range(1, table.shape[0]):
        picked = jnp.where(z == n, jnp.int32(int(table[n, i])), picked)
    return picked


def joined(parts):
    return parts[0] if len(parts) == 1 else jnp.concatenate(parts, axis=0)


def pack_kernel(queries, keys, values, *refs, slabs, heads, kv_local, order, share, stages):
    *outs, all_queries, all_keys, all_values, semaphores = refs
    z = lax.axis_index("wsh")
    pairs = ((keys, all_keys), (values, all_values), (queries, all_queries))
    copies = [pltpu.make_async_copy(a, b, semaphores.at[n]) for n, (a, b) in enumerate(pairs)]
    for copy in copies:
        copy.start()
    block = queries.shape[0]
    targets = [lax.rem(z + k, slabs) for k in range(slabs)]
    for n in range(2):
        copies[n].wait()
        for k, target in enumerate(targets):
            first = pl.multiple_of(lax.div(target * kv_local, slabs) * HEAD_SIZE, HEAD_SIZE)
            outs[k][n * block : (n + 1) * block, :] = pairs[n][1][:, pl.ds(first, HEAD_SIZE)]
    copies[2].wait()
    for n, stage in enumerate(stages):
        for k, target in enumerate(targets):
            place = 2 * block if n == 0 else 0
            for h in range(heads):
                column = pl.multiple_of((target * heads + h) * HEAD_SIZE, HEAD_SIZE)
                for i in stage:
                    if share == block:
                        rows, count = slice(None), block
                    else:
                        rows, count = pl.ds(pl.multiple_of(chosen(order, target, i) * share, 16), share), share
                    outs[n * slabs + k][place : place + count, :] = all_queries[rows, pl.ds(column, HEAD_SIZE)]
                    place += count


def pack(queries, keys, values, *, slabs, heads, kv_local, order, share, stages):
    block = queries.shape[0]
    counts = [heads * share * len(stage) + (2 * block if n == 0 else 0) for n, stage in enumerate(stages)]
    return pl.pallas_call(
        partial(
            pack_kernel, slabs=slabs, heads=heads, kv_local=kv_local, order=order, share=share, stages=stages
        ),
        out_shape=[jax.ShapeDtypeStruct((count, HEAD_SIZE), BF16) for count in counts for _ in range(slabs)],
        in_specs=[HBM] * 3,
        out_specs=[VMEM] * (slabs * len(counts)),
        scratch_shapes=[pltpu.VMEM(a.shape, BF16) for a in (queries, keys, values)]
        + [pltpu.SemaphoreType.DMA((3,))],
        compiler_params=LIMIT,
        cost_estimate=FREE,
        name="pack",
    )(in_hbm(queries), in_hbm(keys), in_hbm(values))


def attend_kernel(key_doc, *refs, slabs, heads, share, stage, stages, order, offset, columns_x, per_shard, fetched):
    refs = list(refs)
    take = lambda n: [refs.pop(0) for _ in range(n)]
    now, before, queries, weights = take(slabs), take(slabs), take(slabs), take(fetched)
    (keep, send), copied = take(2), take(fetched)
    key_rows, value_rows = take(2)
    copies = [pltpu.make_async_copy(w, c, refs[0].at[n]) for n, (w, c) in enumerate(zip(weights, copied))]
    for copy in copies:
        copy.start()
    scale = math.log2(math.e) / math.sqrt(HEAD_SIZE)
    span = key_doc.shape[2]
    block = span // SLAB_REACH
    rows = share * len(stage)
    srv, head, z = (lax.axis_index(a) for a in ("srv", "head", "wsh"))
    core, x = lax.rem(head, 2), lax.div(head, 2)
    column = lax.broadcasted_iota(jnp.int32, (share, span), 1) - (SLAB_REACH - 1) * block
    row = lax.broadcasted_iota(jnp.int32, (share, span), 0)
    behind = [column - row - (0 if share == block else chosen(order, z, i) * share) for i in stage]
    causal = joined([b <= 0 for b in behind])
    places = [offset + (h * len(stages) + stages.index(stage[0])) * share for h in range(heads)]
    for k in range(slabs):
        slab = lax.rem(z - k + slabs, slabs)
        for o in range(SLAB_REACH):
            place = slice((SLAB_REACH - 1 - o) * block, (SLAB_REACH - o) * block)
            held = (k + o) % slabs

            def fill(source):
                key_rows[place, :] = source[:block, :]
                value_rows[place, :] = source[block : 2 * block, :]

            if o == 0:
                fill(now[held])
            else:
                pl.when(slab >= o)(partial(fill, now[held]))
                pl.when(slab < o)(partial(fill, before[held]))
        docs = key_doc[srv * slabs + slab]
        query_doc = joined([jnp.max(jnp.where(b == 0, docs, -2.0), axis=1, keepdims=True) for b in behind])
        visible = causal & (query_doc == docs)
        scores = lax.dot_general(
            joined([queries[k][start : start + rows, :] for start in places]),
            key_rows[...],
            (((1,), (1,)), ((), ())),
            preferred_element_type=F32,
        ).reshape(heads, rows, span)
        scores = jnp.where(visible[None], scores, MASKED)
        largest = jnp.max(scores, axis=-1, keepdims=True)
        terms = jnp.exp2((scores - largest) * scale)
        normalizer = jnp.sum(terms, axis=-1, keepdims=True)
        weighted = jnp.dot(
            terms.reshape(heads * rows, span).astype(BF16), value_rows[...], preferred_element_type=F32
        ).reshape(heads, rows, HEAD_SIZE)
        result = (weighted / normalizer).astype(BF16)
        result = jnp.concatenate([result[h] for h in range(heads)], axis=1)
        target = lax.div(slab, per_shard)
        slot = lax.rem(lax.div(target, 2) - x + columns_x, columns_x) * per_shard + lax.rem(slab, per_shard)

        @pl.when(lax.rem(target, 2) == core)
        def _():
            keep[slot] = result

        @pl.when(lax.rem(target, 2) != core)
        def _():
            send[slot] = result

    for copy in copies:
        copy.wait()


def attend(key_doc, now, before, queries, weights, *, slabs, heads, share, stage, **rest):
    span = key_doc.shape[2]
    rows = share * len(stage)
    out = jax.ShapeDtypeStruct((slabs // 2, rows, heads * HEAD_SIZE), BF16)
    terms = slabs * rows * span * heads
    fetched = len(weights)
    return pl.pallas_call(
        partial(
            attend_kernel, slabs=slabs, heads=heads, share=share, stage=stage, fetched=fetched, **rest
        ),
        out_shape=[out, out] + [pltpu.VMEM(w.shape, w.dtype) for w in weights],
        in_specs=[VMEM] * (1 + 3 * slabs) + [HBM] * fetched,
        out_specs=[VMEM] * (2 + fetched),
        scratch_shapes=[pltpu.VMEM((span, HEAD_SIZE), BF16)] * 2
        + [pltpu.SemaphoreType.DMA((fetched,))] * (fetched > 0),
        compiler_params=LIMIT,
        cost_estimate=worth(ATTEND_US[0 if stage[0] == 0 else min(len(stage), 2)]),
        name="attend",
    )(key_doc, *now, *before, *queries, *[in_hbm(w) for w in weights])


def first_half_kernel(rows_here, near, far, total, far_held, semaphores, *held):
    copies = [pltpu.make_async_copy(far, far_held, semaphores.at[0])]
    for near_held in held:
        copies.insert(0, pltpu.make_async_copy(near, near_held, semaphores.at[1]))
    for copy in copies:
        copy.start()
    for copy in copies[:-1]:
        copy.wait()
    weight = held[0] if held else near
    for n in range(0, total.shape[1], TILE):
        total[:, n : n + TILE] = jnp.dot(rows_here[...], weight[:, n : n + TILE], preferred_element_type=F32)
    copies[-1].wait()


def first_half(rows_here, near, far, near_held):
    return pl.pallas_call(
        first_half_kernel,
        out_shape=[pltpu.VMEM((rows_here.shape[0], near.shape[1]), F32), pltpu.VMEM(far.shape, far.dtype)],
        in_specs=[VMEM, VMEM if near_held else HBM, HBM],
        out_specs=[VMEM, VMEM],
        scratch_shapes=[pltpu.SemaphoreType.DMA((2,))] + [pltpu.VMEM(near.shape, near.dtype)] * (not near_held),
        compiler_params=LIMIT,
        cost_estimate=worth(FIRST_HALF_US[near_held]),
        name="first_half",
    )(rows_here, in_vmem(near) if near_held else in_hbm(near), in_hbm(far))


def project_kernel(*refs, terms, begun, share, splits, columns_x):
    lhs, rhs, start = refs[:terms], refs[terms : 2 * terms], refs[2 * terms : 2 * terms + begun]
    outs = refs[2 * terms + begun :]
    width = rhs[0].shape[1]
    for n in range(0, width, TILE):
        total = sum(
            jnp.dot(a[...], w[:, n : n + TILE], preferred_element_type=F32) for a, w in zip(lhs, rhs)
        )
        for s in start:
            total = total + s[:, n : n + TILE]
        place = 0
        for i, split in enumerate(splits):
            part = width // split
            for k in range(columns_x):
                row = (k * len(splits) + i) * share
                out = outs[place + k * split + n // part]
                out[:, n % part : n % part + TILE] = total[row : row + share].astype(BF16)
            place += columns_x * split


def project(lhs, rhs, start, share, splits):
    width = rhs[0].shape[1]
    columns_x = lhs[0].shape[0] // (share * len(splits))
    shapes = [
        jax.ShapeDtypeStruct((share, width // split), BF16) for split in splits for _ in range(columns_x * split)
    ]
    results = pl.pallas_call(
        partial(
            project_kernel, terms=len(lhs), begun=len(start), share=share, splits=splits, columns_x=columns_x
        ),
        out_shape=shapes,
        in_specs=[VMEM] * (2 * len(lhs) + len(start)),
        out_specs=[VMEM] * len(shapes),
        compiler_params=LIMIT,
        cost_estimate=worth(PROJECT_US[min(len(splits), 2)]),
        name="project",
    )(*lhs, *[in_vmem(w) for w in rhs], *[in_vmem(s) for s in start])
    pieces = []
    for split in splits:
        pieces.append([results[k * split : (k + 1) * split] for k in range(columns_x)])
        results = results[columns_x * split :]
    return pieces


def on_device(queries, keys, values, doc_ids, block_mask, out_weight, *, order):
    groups, head_shards, slabs = (lax.axis_size(a) for a in ("srv", "head", "wsh"))
    z = lax.axis_index("wsh")
    columns_x = head_shards // 2
    block = queries.shape[0]
    heads = queries.shape[1] // HEAD_SIZE // slabs
    share = block // head_shards
    per_shard = slabs // head_shards
    staged = per_shard == 1
    stages = [[0], list(range(1, slabs))] if staged else [[0]]
    rounds = [[0], list(range(1, slabs - 1)), [slabs - 1]] if staged and slabs > 2 else stages
    rows_at_once = share if staged else block
    siblings = [(h, h ^ 1) for h in range(head_shards)]

    def within_reach(k):
        return [
            (g * slabs + i, (g + 1) * slabs + i)
            for g in range(groups - 1)
            for i in range(slabs)
            if (i - k) % slabs > slabs - SLAB_REACH
        ]

    def around(array, k):
        return lax.ppermute(array, "wsh", [(i, (i + k) % slabs) for i in range(slabs)])

    packed = pack(
        queries,
        keys,
        values,
        slabs=slabs,
        heads=heads,
        kv_local=keys.shape[1] // HEAD_SIZE,
        order=order,
        share=rows_at_once,
        stages=stages,
    )
    loads = [packed[0]] + [around(packed[k], k) for k in range(1, slabs)]
    before = [
        lax.ppermute(a[: 2 * block], ("srv", "wsh"), within_reach(k)) for k, a in enumerate(loads)
    ]
    weight_sibling = lax.ppermute(out_weight, "head", siblings)
    stage_queries = [loads]
    for n in range(1, len(stages)):
        sent = packed[n * slabs : (n + 1) * slabs]
        stage_queries.append(
            [sent[0]] + [around(after(sent[k], *loads, before[k - 1]), k) for k in range(1, slabs)]
        )

    reach = SLAB_REACH - 1
    padded = jnp.concatenate([jnp.full((reach, block), -1.0, F32), doc_ids.reshape(-1, block).astype(F32)])
    count = padded.shape[0] - reach
    key_doc = jnp.stack(
        [jnp.where(block_mask[:, reach - j, None] > 0, padded[j : j + count], -1.0) for j in range(SLAB_REACH)],
        axis=1,
    ).reshape(count, 1, SLAB_REACH * block)

    position = np.argsort(order, axis=1)
    middle = slabs // 2 - 1

    def inward(c):
        return [(c, c + 1), (slabs - 1 - c, slabs - 2 - c)]

    def outward(c):
        return [(b, a) for a, b in inward(c)]

    def add(*terms):
        return sum(a.astype(F32) for a in terms).astype(BF16)

    routes = [[(h, (h + 2 * k) % head_shards) for h in range(head_shards)] for k in range(columns_x)]
    sums, crossed, sent = [], [], []

    def cross(t):
        own, *others = partials[t]
        total = [None] * HALVES
        for n in range(HALVES):
            pieces = [other[n] for other in others]
            if len(crossed) >= UNDER_WAY:
                pieces = [after(piece, *crossed[-UNDER_WAY]) for piece in pieces]
            crossed.append([lax.ppermute(a, "head", r) for a, r in zip(pieces, routes[1:])])
            total[n] = add(own[n], *crossed[-1])
        sums.append(total)

    def step(t):
        passed = sent[-1] if sent else {}
        now = {}
        for n in range(HALVES):
            for c in range(min(t, middle) + 1):
                message = sums[position[c, slabs - 1 - t + c]][n]
                if c:
                    message = add(message, passed[c - 1][n])
                route = inward(c)
                if c < middle and t >= slabs - 2 - c:
                    z_out = slabs - 2 - c
                    back = add(sums[position[z_out, slabs - 1 - t + z_out]][n], passed[c + 1][n])
                    message = jnp.where((z == c) | (z == slabs - 1 - c), message, back)
                    route = route + outward(c)
                now.setdefault(c, {})[n] = lax.ppermute(message, "wsh", route)
        sent.append(now)

    partials = []
    results = None
    for n, stage in enumerate(rounds):
        payload = 0 if n == 0 else 1
        arrived = stage_queries[payload]
        if n:
            arrived = after(arrived, *results[0][0])
        if n > 1:
            arrived = after(arrived, *crossed[HALVES - 1])
        keep, send, *fetched = attend(
            key_doc,
            loads,
            before,
            arrived,
            [out_weight] if n == 0 else [],
            slabs=slabs,
            heads=heads,
            share=rows_at_once,
            stage=stage,
            order=order,
            offset=2 * block if n == 0 else 0,
            stages=stages[payload],
            columns_x=columns_x,
            per_shard=per_shard,
        )
        pieces = stage
        if not staged:
            pieces = range(slabs)
            keep, send = (
                jnp.concatenate(
                    [
                        lax.dynamic_slice_in_dim(
                            a.reshape(columns_x, -1, a.shape[-1]), chosen(order, z, i) * share, share, 1
                        )
                        for i in pieces
                    ],
                    axis=1,
                )
                for a in (keep, send)
            )
        theirs = lax.ppermute(send, "head", siblings)
        keep, theirs = (a.reshape(-1, a.shape[-1]) for a in (keep, theirs))
        splits = [HALVES] * len(pieces)
        if staged:
            near = fetched[0] if fetched else out_weight
            begun, far = first_half(keep, near, weight_sibling, bool(fetched))
            results = project([theirs], [far], [begun], share, splits)
        else:
            results = project([keep, theirs], [fetched[0], weight_sibling], [], share, splits)
        partials += results
        for t in range(len(sums), len(partials)):
            cross(t)
            if t < slabs - 1:
                step(t)

    outs = []
    for n in range(HALVES):
        outs.append(add(sums[-1][n], *[a[n] for a in (sent[-1] if sent else {}).values()]))
    return jnp.concatenate(outs, axis=1)


def solution(mesh):
    in_specs = (
        P(("srv", "wsh"), "head"),
        P(("srv", "wsh"), "head"),
        P(("srv", "wsh"), "head"),
        P(),
        P(),
        P(("head", "wsh"), None),
    )
    out_specs = P(("srv", "head", "wsh"), None)
    return jax.shard_map(
        partial(on_device, order=destination_order(mesh.shape["wsh"])),
        mesh=mesh,
        in_specs=in_specs,
        out_specs=out_specs,
        check_vma=False,
    )
```

```python
from functools import partial
import math

import jax
import jax.numpy as jnp
import numpy as np
from jax import lax
from jax.experimental import pallas as pl
from jax.experimental.pallas import tpu as pltpu
from jax.sharding import PartitionSpec as P

QUERY_HEAD_COUNT = 64
KEY_VALUE_HEADS = 8
HEAD_SIZE = 128
SLAB_REACH = 4

MASKED = -1e30
F32 = jnp.float32
BF16 = jnp.bfloat16
VMEM = pl.BlockSpec(memory_space=pltpu.VMEM)
SMEM = pl.BlockSpec(memory_space=pltpu.SMEM)
HBM = pl.BlockSpec(memory_space=pltpu.HBM)
LIMIT = pltpu.CompilerParams(vmem_limit_bytes=12 << 20)
TILE = 1024
HALVES = 2
UNDER_WAY = 2
ATTEND_US = {0: 1.0, 1: 0.84, 2: 1.05}
FIRST_HALF_US = {True: 1.02, False: 1.74}
PROJECT_US = {1: 0.45, 2: 0.45}
FREE = pl.CostEstimate(flops=0, bytes_accessed=0, transcendentals=0)


def worth(us):
    return pl.CostEstimate(flops=int(us * 1.15e9), bytes_accessed=0, transcendentals=0)


def destination_order(count):
    table = []
    for z in range(count):
        due = {d: (count - 1 - d + z if d > z else count - 1 - z + d) for d in range(count)}
        due[z] = count
        table.append(sorted(range(count), key=lambda d: (due[d], -d if z < count // 2 else d)))
    return np.array(table, np.int32)


def in_vmem(array):
    return pltpu.with_memory_space_constraint(array, pltpu.VMEM)


def in_hbm(array):
    return pltpu.with_memory_space_constraint(array, pltpu.HBM)


def after(value, *others):
    return lax.optimization_barrier((value, others))[0]


def chosen(table, z, i):
    picked = jnp.int32(int(table[0, i]))
    for n in range(1, table.shape[0]):
        picked = jnp.where(z == n, jnp.int32(int(table[n, i])), picked)
    return picked


def joined(parts):
    return parts[0] if len(parts) == 1 else jnp.concatenate(parts, axis=0)


def pack_kernel(queries, keys, values, *refs, slabs, heads, kv_local, order, share, stages):
    *outs, all_queries, all_keys, all_values, semaphores = refs
    z = lax.axis_index("wsh")
    pairs = ((keys, all_keys), (values, all_values), (queries, all_queries))
    copies = [pltpu.make_async_copy(a, b, semaphores.at[n]) for n, (a, b) in enumerate(pairs)]
    for copy in copies:
        copy.start()
    block = queries.shape[0]
    targets = [lax.rem(z + k, slabs) for k in range(slabs)]
    for n in range(2):
        copies[n].wait()
        for k, target in enumerate(targets):
            first = pl.multiple_of(lax.div(target * kv_local, slabs) * HEAD_SIZE, HEAD_SIZE)
            outs[k][n * block : (n + 1) * block, :] = pairs[n][1][:, pl.ds(first, HEAD_SIZE)]
    copies[2].wait()
    for n, stage in enumerate(stages):
        for k, target in enumerate(targets):
            place = 2 * block if n == 0 else 0
            for h in range(heads):
                column = pl.multiple_of((target * heads + h) * HEAD_SIZE, HEAD_SIZE)
                for i in stage:
                    if share == block:
                        rows, count = slice(None), block
                    else:
                        rows, count = pl.ds(pl.multiple_of(chosen(order, target, i) * share, 16), share), share
                    outs[n * slabs + k][place : place + count, :] = all_queries[rows, pl.ds(column, HEAD_SIZE)]
                    place += count


def pack(queries, keys, values, *, slabs, heads, kv_local, order, share, stages):
    block = queries.shape[0]
    counts = [heads * share * len(stage) + (2 * block if n == 0 else 0) for n, stage in enumerate(stages)]
    return pl.pallas_call(
        partial(
            pack_kernel, slabs=slabs, heads=heads, kv_local=kv_local, order=order, share=share, stages=stages
        ),
        out_shape=[jax.ShapeDtypeStruct((count, HEAD_SIZE), BF16) for count in counts for _ in range(slabs)],
        in_specs=[HBM] * 3,
        out_specs=[VMEM] * (slabs * len(counts)),
        scratch_shapes=[pltpu.VMEM(a.shape, BF16) for a in (queries, keys, values)]
        + [pltpu.SemaphoreType.DMA((3,))],
        compiler_params=LIMIT,
        cost_estimate=FREE,
        name="pack",
    )(in_hbm(queries), in_hbm(keys), in_hbm(values))


def attend_kernel(key_doc, *refs, slabs, heads, share, stage, stages, order, offset, columns_x, per_shard, fetched):
    refs = list(refs)
    take = lambda n: [refs.pop(0) for _ in range(n)]
    now, before, queries, weights = take(slabs), take(slabs), take(slabs), take(fetched)
    (keep, send), copied = take(2), take(fetched)
    key_rows, value_rows = take(2)
    copies = [pltpu.make_async_copy(w, c, refs[0].at[n]) for n, (w, c) in enumerate(zip(weights, copied))]
    for copy in copies:
        copy.start()
    scale = math.log2(math.e) / math.sqrt(HEAD_SIZE)
    span = key_doc.shape[2]
    block = span // SLAB_REACH
    rows = share * len(stage)
    srv, head, z = (lax.axis_index(a) for a in ("srv", "head", "wsh"))
    core, x = lax.rem(head, 2), lax.div(head, 2)
    column = lax.broadcasted_iota(jnp.int32, (share, span), 1) - (SLAB_REACH - 1) * block
    row = lax.broadcasted_iota(jnp.int32, (share, span), 0)
    behind = [column - row - (0 if share == block else chosen(order, z, i) * share) for i in stage]
    causal = joined([b <= 0 for b in behind])
    places = [offset + (h * len(stages) + stages.index(stage[0])) * share for h in range(heads)]
    for k in range(slabs):
        slab = lax.rem(z - k + slabs, slabs)
        for o in range(SLAB_REACH):
            place = slice((SLAB_REACH - 1 - o) * block, (SLAB_REACH - o) * block)
            held = (k + o) % slabs

            def fill(source):
                key_rows[place, :] = source[:block, :]
                value_rows[place, :] = source[block : 2 * block, :]

            if o == 0:
                fill(now[held])
            else:
                pl.when(slab >= o)(partial(fill, now[held]))
                pl.when(slab < o)(partial(fill, before[held]))
        docs = key_doc[srv * slabs + slab]
        query_doc = joined([jnp.max(jnp.where(b == 0, docs, -2.0), axis=1, keepdims=True) for b in behind])
        visible = causal & (query_doc == docs)
        scores = lax.dot_general(
            joined([queries[k][start : start + rows, :] for start in places]),
            key_rows[...],
            (((1,), (1,)), ((), ())),
            preferred_element_type=F32,
        ).reshape(heads, rows, span)
        scores = jnp.where(visible[None], scores, MASKED)
        largest = jnp.max(scores, axis=-1, keepdims=True)
        terms = jnp.exp2((scores - largest) * scale)
        normalizer = jnp.sum(terms, axis=-1, keepdims=True)
        weighted = jnp.dot(
            terms.reshape(heads * rows, span).astype(BF16), value_rows[...], preferred_element_type=F32
        ).reshape(heads, rows, HEAD_SIZE)
        result = (weighted / normalizer).astype(BF16)
        result = jnp.concatenate([result[h] for h in range(heads)], axis=1)
        target = lax.div(slab, per_shard)
        slot = lax.rem(lax.div(target, 2) - x + columns_x, columns_x) * per_shard + lax.rem(slab, per_shard)

        @pl.when(lax.rem(target, 2) == core)
        def _():
            keep[slot] = result

        @pl.when(lax.rem(target, 2) != core)
        def _():
            send[slot] = result

    for copy in copies:
        copy.wait()


def attend(key_doc, now, before, queries, weights, *, slabs, heads, share, stage, **rest):
    span = key_doc.shape[2]
    rows = share * len(stage)
    out = jax.ShapeDtypeStruct((slabs // 2, rows, heads * HEAD_SIZE), BF16)
    terms = slabs * rows * span * heads
    fetched = len(weights)
    return pl.pallas_call(
        partial(
            attend_kernel, slabs=slabs, heads=heads, share=share, stage=stage, fetched=fetched, **rest
        ),
        out_shape=[out, out] + [pltpu.VMEM(w.shape, w.dtype) for w in weights],
        in_specs=[VMEM] * (1 + 3 * slabs) + [HBM] * fetched,
        out_specs=[VMEM] * (2 + fetched),
        scratch_shapes=[pltpu.VMEM((span, HEAD_SIZE), BF16)] * 2
        + [pltpu.SemaphoreType.DMA((fetched,))] * (fetched > 0),
        compiler_params=LIMIT,
        cost_estimate=worth(ATTEND_US[0 if stage[0] == 0 else min(len(stage), 2)]),
        name="attend",
    )(key_doc, *now, *before, *queries, *[in_hbm(w) for w in weights])


def first_half_kernel(rows_here, near, far, total, far_held, semaphores, *held):
    copies = [pltpu.make_async_copy(far, far_held, semaphores.at[0])]
    for near_held in held:
        copies.insert(0, pltpu.make_async_copy(near, near_held, semaphores.at[1]))
    for copy in copies:
        copy.start()
    for copy in copies[:-1]:
        copy.wait()
    weight = held[0] if held else near
    for n in range(0, total.shape[1], TILE):
        total[:, n : n + TILE] = jnp.dot(rows_here[...], weight[:, n : n + TILE], preferred_element_type=F32)
    copies[-1].wait()


def first_half(rows_here, near, far, near_held):
    return pl.pallas_call(
        first_half_kernel,
        out_shape=[pltpu.VMEM((rows_here.shape[0], near.shape[1]), F32), pltpu.VMEM(far.shape, far.dtype)],
        in_specs=[VMEM, VMEM if near_held else HBM, HBM],
        out_specs=[VMEM, VMEM],
        scratch_shapes=[pltpu.SemaphoreType.DMA((2,))] + [pltpu.VMEM(near.shape, near.dtype)] * (not near_held),
        compiler_params=LIMIT,
        cost_estimate=worth(FIRST_HALF_US[near_held]),
        name="first_half",
    )(rows_here, in_vmem(near) if near_held else in_hbm(near), in_hbm(far))


def project_kernel(*refs, terms, begun, share, splits, columns_x):
    lhs, rhs, start = refs[:terms], refs[terms : 2 * terms], refs[2 * terms : 2 * terms + begun]
    outs = refs[2 * terms + begun :]
    width = rhs[0].shape[1]
    for n in range(0, width, TILE):
        total = sum(
            jnp.dot(a[...], w[:, n : n + TILE], preferred_element_type=F32) for a, w in zip(lhs, rhs)
        )
        for s in start:
            total = total + s[:, n : n + TILE]
        place = 0
        for i, split in enumerate(splits):
            part = width // split
            for k in range(columns_x):
                row = (k * len(splits) + i) * share
                out = outs[place + k * split + n // part]
                out[:, n % part : n % part + TILE] = total[row : row + share].astype(BF16)
            place += columns_x * split


def project(lhs, rhs, start, share, splits):
    width = rhs[0].shape[1]
    columns_x = lhs[0].shape[0] // (share * len(splits))
    shapes = [
        jax.ShapeDtypeStruct((share, width // split), BF16) for split in splits for _ in range(columns_x * split)
    ]
    results = pl.pallas_call(
        partial(
            project_kernel, terms=len(lhs), begun=len(start), share=share, splits=splits, columns_x=columns_x
        ),
        out_shape=shapes,
        in_specs=[VMEM] * (2 * len(lhs) + len(start)),
        out_specs=[VMEM] * len(shapes),
        compiler_params=LIMIT,
        cost_estimate=worth(PROJECT_US[min(len(splits), 2)]),
        name="project",
    )(*lhs, *[in_vmem(w) for w in rhs], *[in_vmem(s) for s in start])
    pieces = []
    for split in splits:
        pieces.append([results[k * split : (k + 1) * split] for k in range(columns_x)])
        results = results[columns_x * split :]
    return pieces


def on_device(queries, keys, values, doc_ids, block_mask, out_weight, *, order):
    groups, head_shards, slabs = (lax.axis_size(a) for a in ("srv", "head", "wsh"))
    z = lax.axis_index("wsh")
    columns_x = head_shards // 2
    block = queries.shape[0]
    heads = queries.shape[1] // HEAD_SIZE // slabs
    share = block // head_shards
    per_shard = slabs // head_shards
    staged = per_shard == 1
    stages = [[0], list(range(1, slabs))] if staged else [[0]]
    rounds = [[0], list(range(1, slabs - 1)), [slabs - 1]] if staged and slabs > 2 else stages
    rows_at_once = share if staged else block
    siblings = [(h, h ^ 1) for h in range(head_shards)]

    def within_reach(k):
        return [
            (g * slabs + i, (g + 1) * slabs + i)
            for g in range(groups - 1)
            for i in range(slabs)
            if (i - k) % slabs > slabs - SLAB_REACH
        ]

    def around(array, k):
        return lax.ppermute(array, "wsh", [(i, (i + k) % slabs) for i in range(slabs)])

    packed = pack(
        queries,
        keys,
        values,
        slabs=slabs,
        heads=heads,
        kv_local=keys.shape[1] // HEAD_SIZE,
        order=order,
        share=rows_at_once,
        stages=stages,
    )
    loads = [packed[0]] + [around(packed[k], k) for k in range(1, slabs)]
    before = [
        lax.ppermute(a[: 2 * block], ("srv", "wsh"), within_reach(k)) for k, a in enumerate(loads)
    ]
    weight_sibling = lax.ppermute(out_weight, "head", siblings)
    stage_queries = [loads]
    for n in range(1, len(stages)):
        sent = packed[n * slabs : (n + 1) * slabs]
        stage_queries.append(
            [sent[0]] + [around(after(sent[k], *loads, before[k - 1]), k) for k in range(1, slabs)]
        )

    reach = SLAB_REACH - 1
    padded = jnp.concatenate([jnp.full((reach, block), -1.0, F32), doc_ids.reshape(-1, block).astype(F32)])
    count = padded.shape[0] - reach
    key_doc = jnp.stack(
        [jnp.where(block_mask[:, reach - j, None] > 0, padded[j : j + count], -1.0) for j in range(SLAB_REACH)],
        axis=1,
    ).reshape(count, 1, SLAB_REACH * block)

    position = np.argsort(order, axis=1)
    middle = slabs // 2 - 1

    def inward(c):
        return [(c, c + 1), (slabs - 1 - c, slabs - 2 - c)]

    def outward(c):
        return [(b, a) for a, b in inward(c)]

    def add(*terms):
        return sum(a.astype(F32) for a in terms).astype(BF16)

    routes = [[(h, (h + 2 * k) % head_shards) for h in range(head_shards)] for k in range(columns_x)]
    sums, crossed, sent = [], [], []

    def cross(t):
        own, *others = partials[t]
        total = [None] * HALVES
        for n in range(HALVES):
            pieces = [other[n] for other in others]
            if len(crossed) >= UNDER_WAY:
                pieces = [after(piece, *crossed[-UNDER_WAY]) for piece in pieces]
            crossed.append([lax.ppermute(a, "head", r) for a, r in zip(pieces, routes[1:])])
            total[n] = add(own[n], *crossed[-1])
        sums.append(total)

    def step(t):
        passed = sent[-1] if sent else {}
        now = {}
        for n in range(HALVES):
            for c in range(min(t, middle) + 1):
                message = sums[position[c, slabs - 1 - t + c]][n]
                if c:
                    message = add(message, passed[c - 1][n])
                route = inward(c)
                if c < middle and t >= slabs - 2 - c:
                    z_out = slabs - 2 - c
                    back = add(sums[position[z_out, slabs - 1 - t + z_out]][n], passed[c + 1][n])
                    message = jnp.where((z == c) | (z == slabs - 1 - c), message, back)
                    route = route + outward(c)
                now.setdefault(c, {})[n] = lax.ppermute(message, "wsh", route)
        sent.append(now)

    partials = []
    results = None
    for n, stage in enumerate(rounds):
        payload = 0 if n == 0 else 1
        arrived = stage_queries[payload]
        if n:
            arrived = after(arrived, *results[0][0])
        if n > 1:
            arrived = after(arrived, *crossed[HALVES - 1])
        keep, send, *fetched = attend(
            key_doc,
            loads,
            before,
            arrived,
            [out_weight] if n == 0 else [],
            slabs=slabs,
            heads=heads,
            share=rows_at_once,
            stage=stage,
            order=order,
            offset=2 * block if n == 0 else 0,
            stages=stages[payload],
            columns_x=columns_x,
            per_shard=per_shard,
        )
        pieces = stage
        if not staged:
            pieces = range(slabs)
            keep, send = (
                jnp.concatenate(
                    [
                        lax.dynamic_slice_in_dim(
                            a.reshape(columns_x, -1, a.shape[-1]), chosen(order, z, i) * share, share, 1
                        )
                        for i in pieces
                    ],
                    axis=1,
                )
                for a in (keep, send)
            )
        theirs = lax.ppermute(send, "head", siblings)
        keep, theirs = (a.reshape(-1, a.shape[-1]) for a in (keep, theirs))
        splits = [HALVES] * len(pieces)
        if staged:
            near = fetched[0] if fetched else out_weight
            begun, far = first_half(keep, near, weight_sibling, bool(fetched))
            results = project([theirs], [far], [begun], share, splits)
        else:
            results = project([keep, theirs], [fetched[0], weight_sibling], [], share, splits)
        partials += results
        for t in range(len(sums), len(partials)):
            cross(t)
            if t < slabs - 1:
                step(t)

    outs = []
    for n in range(HALVES):
        outs.append(add(sums[-1][n], *[a[n] for a in (sent[-1] if sent else {}).values()]))
    return jnp.concatenate(outs, axis=1)


def solution(mesh):
    in_specs = (
        P(("srv", "wsh"), "head"),
        P(("srv", "wsh"), "head"),
        P(("srv", "wsh"), "head"),
        P(),
        P(),
        P(("head", "wsh"), None),
    )
    out_specs = P(("srv", "head", "wsh"), None)
    return jax.shard_map(
        partial(on_device, order=destination_order(mesh.shape["wsh"])),
        mesh=mesh,
        in_specs=in_specs,
        out_specs=out_specs,
        check_vma=False,
    )
```
